32 devices in a mesh: seq: 16 (over z, y, core), batch: 2 (over x).
Axes of the slice: x: 2, y: 2, z: 4, core: 2. Of those that a mesh axis runs over, the one named last changes fastest.
Arguments:
- frames: bfloat16 [4, 1024, 1024], P('batch', 'seq'), may hold values from -6 to 6
- skip_frames: bfloat16 [4, 1024, 1024], P('batch', 'seq'), may hold values from -6 to 6
- time_embed: bfloat16 [4, 1024, 1024], P('batch', 'seq'), may hold values from -6 to 6
- cotangent: bfloat16 [4, 1024, 1024], P('batch', 'seq'), may hold values from -6 to 6
- segments: int32 [4, 1024], P('batch', 'seq'), may hold values from 0 to 8, as said below
- owners: int32 [120], replicated, may hold values from 0 to 1, as said below
- master: float32 [180, 128, 1024], P('batch', None, 'seq'), may hold values from -5 to 5
- moment_one: float32 [180, 128, 1024], P('batch', None, 'seq'), may hold values from -3.5 to 3.5
- moment_two: float32 [180, 128, 1024], P('batch', None, 'seq'), may hold values from 0.004 to 0.016
- norm_gains: float32 [1024], replicated, may hold values from 0.5 to 1.5
- ff_biases: float32 [5120], replicated, may hold values from -2 to 2
- small_first: float32 [6144], replicated, may hold values from -40 to 40
- small_second: float32 [6144], replicated, may hold values from 4.096 to 16.384
Outputs:
- output: bfloat16 [4, 1024, 1024], P('batch', 'seq')
- grad_frames: float32 [4, 1024, 1024], P('batch', 'seq')
- grad_skip: float32 [4, 1024, 1024], P('batch', 'seq')
- grad_time: float32 [4, 1024, 1024], P('batch', 'seq')
- new_moment_one: float32 [180, 128, 1024], P('batch', None, 'seq')
- new_moment_two: float32 [180, 128, 1024], P('batch', None, 'seq')
- new_master: float32 [180, 128, 1024], P('batch', None, 'seq')
- new_low: bfloat16 [180, 128, 1024], P('batch', None, 'seq')
- small_moment_one: float32 [6144], replicated
- small_moment_two: float32 [6144], replicated
- small_params: float32 [6144], replicated
The draws below stay inside these ranges and needn't reach their ends.
Inputs may be any that keep to these rules, and one draw needn't show every extreme that they name: `segments`: along a row the ids never fall; id 8 marks padding, which lies only in the last 64 frames of a row. `owners`: each batch index owns at most 90 blocks, and one owns exactly 90.
All inputs are finite; a program needn't handle non-finite values.
Results may differ from the reference program's by a relative error of at most 0.015.
The reference program's roundings to bfloat16 on the way count: a program that leaves them out, or rounds other values in their place, can miss the bound.
Values may be sent and summed in bfloat16 or wider, within the bound.
No kernel may reach another device: no remote copies, remote signals or barrier semaphores. Data moves between devices by JAX's collectives and lax.ppermute only.
A program may use at most 320 MiB of HBM per device.

```python
import math
import jax
import jax.numpy as jnp
from jax import lax

D = 1024
FF = 4096
HEADS = 16
HEAD_DIM = 64
ROW_SEG = 64
ROWS = 2
UTTS = 8
BR = 128
STEP = 10
ROW_LEN = 1024
NR = 4
TOKENS = 4096
NBLK = 120
CAP = 90
N_SEQ = 16
N_BATCH = 2


def draw_segments(key, part):
    key = jax.random.fold_in(key, 11)
    pick_key, row_key = jax.random.split(key, 2)
    chosen = jax.random.randint(pick_key, (N_BATCH,), 0, ROWS)
    row_ids = jnp.arange(N_BATCH * ROWS)
    spanning = row_ids % ROWS == jnp.repeat(chosen, ROWS)
    row_length = ROW_SEG * N_SEQ
    position = jnp.arange(row_length)
    row_keys = jax.random.split(row_key, N_BATCH * ROWS)

    def one_row(single_key, span_flag):
        cut_key, pad_key, head_key, tail_key = jax.random.split(single_key, 4)
        cuts = jax.random.randint(cut_key, (UTTS - 1,), 1, row_length)
        ragged = jnp.sum((position[:, None] >= cuts[None, :]).astype(jnp.int32), axis=1)
        pad_start = jax.random.randint(pad_key, (), row_length - ROW_SEG + 1, row_length + 1)
        ragged = jnp.where(position >= pad_start, UTTS, ragged)
        head_len = jax.random.randint(head_key, (), 1, ROW_SEG)
        tail_len = jax.random.randint(tail_key, (), 1, ROW_SEG)
        whole = jnp.where(position < head_len, 0, jnp.where(position < row_length - tail_len, 1, UTTS))
        return jnp.where(span_flag, whole, ragged).astype(jnp.int32)
    return jax.vmap(one_row)(row_keys, spanning)


def draw_owners(key, part):
    key = jax.random.fold_in(key, 23)
    order_key, heavy_key = jax.random.split(key, 2)
    order = jax.random.permutation(order_key, NBLK)
    heavy = jax.random.randint(heavy_key, (), 0, N_BATCH)
    ranking = jnp.arange(NBLK)
    others = (heavy + 1 + (ranking - CAP) % (N_BATCH - 1)) % N_BATCH
    by_rank = jnp.where(ranking < CAP, heavy, others).astype(jnp.int32)
    return jnp.zeros((NBLK,), jnp.int32).at[order].set(by_rank)


def level_of(rng, shape, cuts, least, top_value):
    factor_of, own = 1.0, jax.random.fold_in(rng, 6)
    for dim, shards_of in cuts:
        steps = jnp.exp(jax.random.uniform(jax.random.fold_in(own, dim), (shards_of,), jnp.float32, least / len(cuts), top_value / len(cuts)))
        factor_of = factor_of * jnp.repeat(steps, shape[dim] // shards_of).reshape([-1 if axis == dim else 1 for axis in range(len(shape))])
    return factor_of


def normal_values(rng, extent, deviation, limit, cuts=(), held_as=jnp.bfloat16):
    loudness = level_of(rng, extent, cuts, -0.22, 0.18) if cuts else 1.0
    entries = jax.random.normal(rng, extent, jnp.float32) * deviation * loudness
    return jnp.minimum(jnp.maximum(entries, -limit), limit).astype(held_as)


def setup_inputs(seed: int = 0) -> dict:
    arg_keys = jax.random.split(jax.random.key(seed), 14)
    return {
        "frames": normal_values(arg_keys[0], (NR, ROW_LEN, D), 1.0, 6.0, ((0, 2), (1, 16))),
        "skip_frames": normal_values(arg_keys[1], (NR, ROW_LEN, D), 1.0, 6.0, ((0, 2), (1, 16))),
        "time_embed": normal_values(arg_keys[2], (NR, ROW_LEN, D), 1.0, 6.0, ((0, 2), (1, 16))),
        "cotangent": normal_values(arg_keys[3], (NR, ROW_LEN, D), 1.0, 6.0, ((0, 2), (1, 16))),
        "segments": draw_segments(jax.random.fold_in(arg_keys[13], 71), 0),
        "owners": draw_owners(jax.random.fold_in(arg_keys[13], 71), 0),
        "master": normal_values(arg_keys[6], (N_BATCH * CAP, BR, D), 1.0, 5.0, ((0, 2), (2, 16)), jnp.float32),
        "moment_one": normal_values(arg_keys[7], (N_BATCH * CAP, BR, D), (0.12 * (TOKENS / D) ** 0.5), 3.5, ((0, 2), (2, 16)), jnp.float32),
        "moment_two": jnp.clip(jnp.exp(math.log(0.016) - 1.3862944 * jax.random.uniform(arg_keys[8], (N_BATCH * CAP, BR, D), jnp.float32) ** level_of(arg_keys[8], (N_BATCH * CAP, BR, D), ((0, 2), (2, 16)), -0.2, 0.2)), 0.004, 0.016),
        "norm_gains": jnp.clip(1.0 + 0.1 * jax.random.normal(arg_keys[9], (D,), jnp.float32), 0.5, 1.5),
        "ff_biases": normal_values(arg_keys[10], (FF + D,), 0.3, 2.0, (), jnp.float32),
        "small_first": normal_values(arg_keys[11], (2 * D + FF,), (0.1 * TOKENS ** 0.5), 40.0, (), jnp.float32),
        "small_second": jnp.clip(jnp.exp(jax.random.uniform(arg_keys[12], (2 * D + FF,), jnp.float32, math.log(4.096), math.log(16.384))), 4.096, 16.384),
    }


@jax.custom_vjp
def low(v):
    return lax.optimization_barrier(v.astype(jnp.bfloat16)).astype(jnp.float32)

@jax.custom_vjp
def low_back(v):
    return v

def low_keep(v):
    return (low(v), None)

def low_pass(kept, grad):
    return (grad,)

def back_keep(v):
    return (v, None)

def back_low(kept, grad):
    return (low(grad),)
low.defvjp(low_keep, low_pass)
low_back.defvjp(back_keep, back_low)
NORM_EPS = 1e-06
MASKED_SCORE = -1e+30
BETA_ONE = 0.9
BETA_TWO = 0.999
ADAM_EPS = 1e-08
WEIGHT_DECAY = 0.01
LEARN_RATE = 1.0
SMALL_RATE = 0.1

def slot_places(owners, group_count, capacity):
    one_hot = (owners[:, None] == jnp.arange(group_count, dtype=jnp.int32)[None, :]).astype(jnp.int32)
    before = jnp.cumsum(one_hot, axis=0) - one_hot
    slot_index = lax.optimization_barrier(jnp.sum(before * one_hot, axis=1))
    return (owners * capacity + slot_index).astype(jnp.int32)

def rotate(tensor, offset):
    half_size = tensor.shape[-1] // 2
    position = (offset + jnp.arange(tensor.shape[1], dtype=jnp.int32)).astype(jnp.float32)
    inverse = 10000.0 ** (-jnp.arange(half_size, dtype=jnp.int32).astype(jnp.float32) / half_size)
    phases = position[:, None] * inverse[None, :]
    cosine = jnp.cos(phases)[None, :, None, :]
    sine_part = jnp.sin(phases)[None, :, None, :]
    front_half = tensor[..., :half_size]
    back_half = tensor[..., half_size:]
    return jnp.concatenate([front_half * cosine - back_half * sine_part, front_half * sine_part + back_half * cosine], axis=-1)

def adaptive_norm(trunk, gamma_map):
    return trunk * lax.rsqrt(lax.optimization_barrier(jnp.mean(trunk * trunk, axis=-1, keepdims=True)) + NORM_EPS) * (1.0 + gamma_map)

def root_norm(residual, norm_gains):
    return residual * lax.rsqrt(lax.optimization_barrier(jnp.mean(residual * residual, axis=-1, keepdims=True)) + NORM_EPS) * norm_gains

def gelu_exact(tensor):
    return jax.nn.gelu(tensor, approximate=False)

def adam_update(weight, gradient, first_moment, second_moment, step_rate):
    first_moment = BETA_ONE * first_moment + (1.0 - BETA_ONE) * gradient
    second_moment = BETA_TWO * second_moment + (1.0 - BETA_TWO) * gradient * gradient
    fix_one = 1.0 - BETA_ONE ** STEP
    fix_two = 1.0 - BETA_TWO ** STEP
    update = first_moment / fix_one / (jnp.sqrt(second_moment / fix_two) + ADAM_EPS)
    return (weight - step_rate * (update + WEIGHT_DECAY * weight), first_moment, second_moment)

def block_forward(master, norm_gains, ff_biases, frame_row, skip_row, time_row, segment_row, places):
    model_width = frame_row.shape[1]
    width_ff = ff_biases.shape[0] - model_width
    row_length = frame_row.shape[0]
    scale_in = model_width ** (-0.5)
    scale_time = 0.5 * model_width ** (-0.5)
    scale_out = 4.0 * model_width ** (-0.5)
    scale_ff = width_ff ** (-0.5)
    score_scale = HEAD_DIM ** (-0.5)
    highest = lax.Precision.HIGHEST
    tile_stack = low(master)[places].reshape(15, model_width, model_width)

    def product(former, latter):
        return jnp.dot(former, latter, precision=highest)

    def split_heads(tensor):
        return tensor.reshape(1, row_length, HEADS, HEAD_DIM)
    trunk = low_back((product(frame_row, tile_stack[0]) + product(skip_row, tile_stack[1])) * scale_in)
    gamma_map = low_back(product(time_row, tile_stack[2]) * scale_time)
    normed = low(adaptive_norm(trunk, gamma_map))
    queries = low(rotate(split_heads(low_back(product(normed, tile_stack[3]) * scale_in)), 0))[0]
    key_rows = low(rotate(split_heads(low_back(product(normed, tile_stack[4]) * scale_in)), 0))[0]
    values = low(split_heads(low_back(product(normed, tile_stack[5]) * scale_in)))[0]
    scores = low_back(jnp.einsum('qhd,khd->hqk', queries, key_rows, precision=highest) * score_scale)
    same_utt = (segment_row[:, None] == segment_row[None, :])[None]
    scores = jnp.where(same_utt, scores, MASKED_SCORE)
    row_max = lax.optimization_barrier(jnp.max(scores, axis=-1, keepdims=True))
    exponent = jnp.exp(scores - row_max)
    attn_probs = exponent / lax.optimization_barrier(jnp.sum(exponent, axis=-1, keepdims=True))
    mixed_rows = low_back(low(jnp.einsum('hqk,khd->qhd', low(attn_probs), values, precision=highest)))
    mixed_rows = mixed_rows.reshape(row_length, model_width)
    attention = low_back(product(mixed_rows, tile_stack[6]) * scale_out)
    residual = trunk + attention
    normed_two = low(root_norm(residual, norm_gains))
    up_weight = jnp.concatenate([tile_stack[7], tile_stack[8], tile_stack[9], tile_stack[10]], axis=1)
    down_weight = tile_stack[11:15].reshape(width_ff, model_width)
    pre_act = low_back(product(normed_two, up_weight) * scale_in + ff_biases[:width_ff])
    hidden = low(gelu_exact(pre_act))
    branch = low_back(product(hidden, down_weight) * scale_ff + ff_biases[width_ff:])
    valid_row = (segment_row < UTTS).astype(jnp.float32)
    return (residual + branch) * valid_row[:, None]

def reference(frames, skip_frames, time_embed, cotangent, segments, owners, master, moment_one, moment_two, norm_gains, ff_biases, small_first, small_second):
    places = slot_places(owners, N_BATCH, CAP)

    def row_step(totals, row_data):
        frame_row, skip_row, time_row, cot_row, segment_row = row_data

        def row_forward(master_in, gains_in, biases_in, frame_in, skip_in, time_in):
            return block_forward(master_in, gains_in, biases_in, frame_in, skip_in, time_in, segment_row, places)
        output_row, pullback = jax.vjp(row_forward, master, norm_gains, ff_biases, frame_row.astype(jnp.float32), skip_row.astype(jnp.float32), time_row.astype(jnp.float32))
        grad_master, grad_gains, grad_biases, grad_frame, grad_skip_row, grad_time_row = pullback(cot_row.astype(jnp.float32))
        totals = (totals[0] + grad_master, totals[1] + grad_gains, totals[2] + grad_biases)
        return (totals, (output_row.astype(jnp.bfloat16), grad_frame, grad_skip_row, grad_time_row))
    start_totals = (jnp.zeros_like(master), jnp.zeros_like(norm_gains), jnp.zeros_like(ff_biases))
    totals, outputs = lax.scan(row_step, start_totals, (frames, skip_frames, time_embed, cotangent, segments))
    output, grad_frames, grad_skip, grad_time = outputs
    live_slot = jnp.any(places[None, :] == jnp.arange(N_BATCH * CAP, dtype=jnp.int32)[:, None], axis=1)
    live_slot = live_slot.astype(jnp.float32)[:, None, None]
    new_master, new_first, new_second = adam_update(master, totals[0], moment_one, moment_two, LEARN_RATE)
    new_master = new_master * live_slot
    new_first = new_first * live_slot
    new_second = new_second * live_slot
    small_values = jnp.concatenate([norm_gains, ff_biases])
    small_grad = jnp.concatenate([totals[1], totals[2]])
    small_new, small_first_new, small_second_new = adam_update(small_values, small_grad, small_first, small_second, SMALL_RATE)
    return (output, grad_frames, grad_skip, grad_time, new_first, new_second, new_master, new_master.astype(jnp.bfloat16), small_first_new, small_second_new, small_new)
```

```python
import functools
import math

import jax
import jax.numpy as jnp
from jax import lax
from jax.experimental import pallas as pl
from jax.experimental.pallas import tpu as pltpu
from jax.sharding import PartitionSpec as P

HEADS = 16
HEAD_DIM = 64
UTTS = 8
STEP = 10
NORM_EPS = 1e-06
MASKED_SCORE = -1e30
BETA_ONE = 0.9
BETA_TWO = 0.999
ADAM_EPS = 1e-08
WEIGHT_DECAY = 0.01
LEARN_RATE = 1.0
SMALL_RATE = 0.1

F32 = jnp.float32
BF16 = jnp.bfloat16
MIB = 1 << 20


def kernel_call(body, outs, *args, scalars=(), scratch=(), vmem=48, flops=0, moved=None):
    specs = [pl.BlockSpec(memory_space=pltpu.SMEM) for _ in scalars]
    specs += [pl.BlockSpec(memory_space=pltpu.VMEM) for _ in args]
    out_shape = [jax.ShapeDtypeStruct(shape, dtype) for shape, dtype in outs]
    if moved is None:
        moved = sum(a.size * a.dtype.itemsize for a in args)
        moved += sum(math.prod(s) * jnp.dtype(d).itemsize for s, d in outs)
    return pl.pallas_call(
        body,
        out_shape=out_shape,
        in_specs=specs,
        out_specs=[pl.BlockSpec(memory_space=pltpu.VMEM) for _ in outs],
        scratch_shapes=list(scratch),
        compiler_params=pltpu.CompilerParams(vmem_limit_bytes=vmem * MIB),
        cost_estimate=pl.CostEstimate(flops=int(flops), bytes_accessed=int(moved), transcendentals=0),
    )(*scalars, *args)


def dot_nn(a, b):
    return jnp.dot(a, b, preferred_element_type=F32)


def dot_nt(a, b):
    return lax.dot_general(a, b, (((1,), (1,)), ((), ())), preferred_element_type=F32)


def dot_tn(a, b):
    return lax.dot_general(a, b, (((0,), (0,)), ((), ())), preferred_element_type=F32)


def lanes(blocks):
    return jnp.concatenate(blocks, axis=-1)


def at128(index):
    return pl.multiple_of(index * 128, 128)


def normal_cdf(x):
    return 0.5 * (1.0 + lax.erf(x * (2.0**-0.5)))


def pick_kernel(slots, group, master, out_a, out_b, out_c, keep, send):
    low = lambda k: master[slots[k]].astype(BF16)
    for k in range(24):
        out_a[k] = low(k)
    for k in range(24):
        out_b[k] = low(24 + k)
    for k in range(8):
        out_c[k] = low(48 + k)
    mine = group[0]
    for out, first in ((keep, 2 * mine), (send, 2 - 2 * mine)):
        for pair in range(2):
            for j in range(8):
                out[pair, j] = low((7 + first + pair) * 8 + j)
                out[pair, 8 + j] = low((11 + first + pair) * 8 + j)


def chip_pieces(refs):
    readers = [lambda s, k, r=r: r[s, k] for r in refs[:7]]
    readers.append(lambda s, k: refs[7 + s][0, k])
    return readers


def trunk_kernel(places, own_x, mate_x, *refs):
    pieces, (own_out, mate_out) = chip_pieces(refs[:9]), refs[9:]
    scale = own_x.shape[-1] * 2
    scale_in = scale**-0.5
    x = [jnp.concatenate([own_x[t], mate_x[t]], axis=0) for t in range(3)]
    for p, piece in enumerate(pieces):
        spot = pl.ds(at128(places[p]), 128)
        done = []
        for t in range(3):
            w = jnp.concatenate(
                [lanes([piece(s, 4 * t + j) for j in range(4)]) for s in range(2)], axis=0
            )
            done.append(dot_nt(x[t], w))
        trunk = (done[0] + done[1]) * scale_in
        gamma = done[2] * (0.5 * scale_in)
        own_out[0, :, spot] = trunk[:128]
        mate_out[0, :, spot] = trunk[128:]
        own_out[1, :, spot] = gamma[:128]
        mate_out[1, :, spot] = gamma[128:]


def norm_kernel(own, mate, trunk_out, gamma_out, normed_out):
    trunk = own[0] + mate[0]
    gamma = own[1] + mate[1]
    trunk_out[...] = trunk
    gamma_out[...] = gamma
    scale = lax.rsqrt(jnp.mean(trunk * trunk, axis=-1, keepdims=True) + NORM_EPS)
    normed_out[...] = (trunk * scale * (1.0 + gamma)).astype(BF16)


def swap_halves(x):
    half = HEAD_DIM // 2
    return jnp.concatenate([x[:, half:], x[:, :half]], axis=1)


def frame_rows(refs, p, m):
    base = 9 * m
    if p < 7:
        return refs[base + p][...]
    return jnp.concatenate([refs[base + 7][...], refs[base + 8][...]], axis=0)


def attend_kernel(sources, weight, cosine, sine, seg_col, seg_row, *refs):
    normed = refs[:18]
    q_ref, k_ref, v_ref, out_ref, mixed = refs[18:]
    width = normed[0].shape[1]
    scale_in = width**-0.5
    w = jnp.concatenate(
        [lanes([weight[8 * t + j] for j in range(8)]) for t in range(3)], axis=0
    )
    row_len = q_ref.shape[1]
    for p in range(8):
        for m in range(2):
            u = 2 * p + m
            spot = pl.ds(u * 64, 64)
            qkv = dot_nt(frame_rows(normed, p, m), w) * scale_in
            c, s = cosine[spot], sine[spot]
            for r in range(2):
                part = qkv[64 * r : 64 * r + 64]
                for ref, lo in ((q_ref, 0), (k_ref, 64)):
                    x = part[:, lo : lo + 64]
                    ref[r, spot] = (x * c + swap_halves(x) * s).astype(BF16)
                v_ref[r, spot] = part[:, 128:192].astype(BF16)
    block = 256
    for r in range(2):
        key, value = k_ref[r], v_ref[r]
        seg_keys = seg_row[r]
        for q in range(row_len // block):
            spot = pl.ds(q * block, block)
            scores = dot_nt(q_ref[r, spot], key) * HEAD_DIM**-0.5
            scores = jnp.where(seg_col[r, spot] == seg_keys, scores, MASKED_SCORE)
            top = jnp.max(scores, axis=-1, keepdims=True)
            exponent = jnp.exp(scores - top)
            total = jnp.sum(exponent, axis=-1, keepdims=True)
            probs = (exponent * (1.0 / total)).astype(BF16)
            mixed[r, spot] = dot_nn(probs, value).astype(BF16)
    for u in range(16):
        spot = pl.ds(u * 64, 64)
        out_ref[sources[u]] = lanes([mixed[0, spot], mixed[1, spot]])


def assemble_out_kernel(places, core, own, mate, out):
    here = core[0]
    for p in range(8):
        for s in range(2):
            rows = pl.ds(pl.multiple_of(places[p] * 128 + 64 * s, 64), 64)
            for j in range(4):
                out[rows, pl.ds(at128(4 * here + j), 128)] = own[p, s, j]
                out[rows, pl.ds(at128(4 - 4 * here + j), 128)] = mate[p, s, j]


def assemble_qkv_kernel(places, *refs):
    pieces, (qk, v) = refs[:9], refs[9:]

    def read(p, k):
        if p < 7:
            return pieces[p][k]
        return pieces[7][k] if k < 12 else pieces[8][k - 12]

    for p in range(8):
        for t in range(2):
            rows = pl.ds(pl.multiple_of(places[p] * 128 + 64 * t, 64), 64)
            for j in range(8):
                qk[rows, 128 * j : 128 * j + 128] = read(p, 8 * t + j)
        rows = pl.ds(pl.multiple_of(places[p] * 64, 64), 64)
        for j in range(8):
            v[rows, 128 * j : 128 * j + 128] = read(p, 16 + j)


def residual_kernel(heads, weight, trunk, gains, res_out, normed_out, mixed_out):
    scale_out = 4.0 * trunk.shape[1] ** -0.5
    for r in range(2):
        for j in range(8):
            pair = [heads[2 * j + i][:, 64 * r : 64 * r + 64] for i in range(2)]
            mixed_out[64 * r : 64 * r + 64, 128 * j : 128 * j + 128] = lanes(pair)
    residual = trunk[...] + dot_nt(mixed_out[...], weight[...]) * scale_out
    res_out[...] = residual
    scale = lax.rsqrt(jnp.mean(residual * residual, axis=-1, keepdims=True) + NORM_EPS)
    normed_out[...] = (residual * scale * gains[...]).astype(BF16)


def forward_back_kernel(places, normed, grad, bias, *refs):
    pieces = chip_pieces(refs[:9])
    grad_in, branch, hidden_out, pre_out, bias_out, w_up, w_down = refs[9:]
    width = w_up.shape[1]
    scale_in = width**-0.5
    scale_ff = (4 * width) ** -0.5
    for p, piece in enumerate(pieces):
        for s in range(2):
            rows = pl.ds(pl.multiple_of(places[p] * 128 + 64 * s, 64), 64)
            for j in range(8):
                w_up[rows, 128 * j : 128 * j + 128] = piece(s, j)
                w_down[rows, 128 * j : 128 * j + 128] = piece(s, 8 + j)
    x = normed[...]
    g = grad[...]
    block = 256
    for h in range(width // block):
        spot = slice(h * block, h * block + block)
        pre = dot_nt(x, w_up[spot, :]) * scale_in + bias[:, spot]
        cdf = normal_cdf(pre)
        hidden = (pre * cdf).astype(BF16)
        slope = cdf + pre * (jnp.exp(-0.5 * pre * pre) * (2.0 * math.pi) ** -0.5)
        grad_pre = slope * (dot_nn(g, w_down[:, spot]) * scale_ff)
        grad_pre = grad_pre.astype(BF16)
        hidden_out[:, spot] = hidden
        pre_out[:, spot] = grad_pre
        bias_out[:, spot] = jnp.sum(grad_pre.astype(F32), axis=0, keepdims=True)
        grad_part = dot_nn(grad_pre, w_up[spot, :])
        out_part = dot_nt(hidden, w_down[:, spot])
        if h == 0:
            grad_in[...] = grad_part
            branch[...] = out_part
        else:
            grad_in[...] += grad_part
            branch[...] += out_part
    grad_in[...] = grad_in[...] * scale_in
    branch[...] = branch[...] * scale_ff


def ff_weight_kernel(targets, normed, grad, hidden, pre, *outs):
    width = normed.shape[1]
    scale_in = width**-0.5
    scale_ff = (4 * width) ** -0.5

    def put(p, s, k, block):
        if p < 7:
            outs[p][s, k] = block
        else:
            outs[7 + s][k] = block

    for p in range(8):
        spot = pl.ds(at128(targets[p]), 128)
        up = (dot_tn(pre[:, spot], normed[...]) * scale_in).astype(BF16)
        down = (dot_tn(grad[:, spot], hidden[...]) * scale_ff).astype(BF16)
        for s in range(2):
            for j in range(8):
                part = (slice(64 * s, 64 * s + 64), slice(128 * j, 128 * j + 128))
                put(p, s, j, up[part])
                put(p, s, 8 + j, down[part])


def back_out_kernel(grad_sum, grad_far, residual, gains, grad_out, weight, grad_res, grad_att, heads, gain_out):
    width = residual.shape[1]
    g = grad_sum[...] + grad_far[...].astype(F32)
    x = residual[...]
    scale = lax.rsqrt(jnp.mean(x * x, axis=-1, keepdims=True) + NORM_EPS)
    gain_out[...] = jnp.sum(g * x * scale, axis=0, keepdims=True)
    inner = g * gains[...]
    slope = inner * scale - x * (scale * scale * scale * jnp.mean(inner * x, axis=-1, keepdims=True))
    total = grad_out[...].astype(F32) + slope
    grad_res[...] = total
    low = total.astype(BF16)
    grad_att[...] = low
    mixed = (dot_nn(low, weight[...]) * (4.0 * width**-0.5)).astype(BF16)
    for j in range(8):
        rows = [mixed[64 * r : 64 * r + 64, 128 * j : 128 * j + 128] for r in range(2)]
        heads[2 * j] = lanes([rows[0][:, :64], rows[1][:, :64]])
        heads[2 * j + 1] = lanes([rows[0][:, 64:], rows[1][:, 64:]])


def attend_back_kernel(sources, places, q_ref, k_ref, v_ref, grads, cosine, sine, seg_col, seg_row, out_ref, dq_ref, dk_ref, dv_ref, g_ref, acc_q, acc_k, acc_v):
    row_len = q_ref.shape[1]
    for u in range(16):
        spot = pl.ds(u * 64, 64)
        both = grads[sources[u]]
        g_ref[0, spot] = both[:, :64]
        g_ref[1, spot] = both[:, 64:]
    block = 256
    for r in range(2):
        key, value = k_ref[r], v_ref[r]
        for q in range(row_len // block):
            spot = pl.ds(q * block, block)
            query, grad = q_ref[r, spot], g_ref[r, spot]
            scores = dot_nt(key, query) * HEAD_DIM**-0.5
            same = seg_col[r] == seg_row[r, :, spot]
            scores = jnp.where(same, scores, MASKED_SCORE)
            top = jnp.max(scores, axis=0, keepdims=True)
            exponent = jnp.exp(scores - top)
            total = jnp.sum(exponent, axis=0, keepdims=True)
            probs = exponent * (1.0 / total)
            prob_grad = dot_nt(value, grad)
            inner = jnp.sum(probs * prob_grad, axis=0, keepdims=True)
            score_grad = (probs * (prob_grad - inner)).astype(BF16)
            acc_q[r, spot] = dot_tn(score_grad, key)
            key_part = dot_nn(score_grad, query)
            value_part = dot_nn(probs.astype(BF16), grad)
            if q == 0:
                acc_k[r] = key_part
                acc_v[r] = value_part
            else:
                acc_k[r] += key_part
                acc_v[r] += value_part
        c, s = cosine[...], sine[...]
        for ref, acc in ((dq_ref, acc_q), (dk_ref, acc_k)):
            g = acc[r] * HEAD_DIM**-0.5
            ref[r] = (g * c + swap_halves(g * s)).astype(BF16)
        dv_ref[r] = acc_v[r].astype(BF16)
    for p in range(8):
        spots = [pl.ds((2 * p + m) * 64, 64) for m in range(2)]
        for m in range(2):
            for r in range(2):
                out_ref[places[p], pl.ds(128 * m + 64 * r, 64)] = lanes(
                    [dq_ref[r, spots[m]], dk_ref[r, spots[m]]]
                )
        for r in range(2):
            out_ref[places[p], pl.ds(256 + 64 * r, 64)] = lanes(
                [dv_ref[r, spots[0]], dv_ref[r, spots[1]]]
            )


def qkv_weight_kernel(dq_ref, dk_ref, dv_ref, *refs):
    normed, (out, x_ref, y_ref) = refs[:18], refs[18:]
    width = normed[0].shape[1]
    row_len = dq_ref.shape[1]
    for p in range(8):
        for m in range(2):
            u = 2 * p + m
            rows = frame_rows(normed, p, m)
            spot = pl.ds(u * 64, 64)
            for r in range(2):
                x_ref[pl.ds(r * row_len + u * 64, 64)] = rows[64 * r : 64 * r + 64]
                y_ref[pl.ds(r * row_len + u * 64, 64), 0:128] = lanes([dq_ref[r, spot], dk_ref[r, spot]])
                y_ref[pl.ds(r * row_len + u * 64, 64), 128:256] = lanes([dv_ref[r, spot], dv_ref[r, spot]])
    for t in range(2):
        grads = dot_tn(y_ref[:, 128 * t : 128 * t + 128], x_ref[...]) * width**-0.5
        grads = grads.astype(BF16)
        for i in range(2 - t):
            for j in range(8):
                out[16 * t + 8 * i + j] = grads[64 * i : 64 * i + 64, 128 * j : 128 * j + 128]


def back_qkv_kernel(grads, weight_qk, weight_v, own_out, mate_out):
    width = weight_qk.shape[1]
    qk = lanes([grads[c, 0:256] for c in range(8)])
    value = jnp.concatenate(
        [lanes([grads[c, 256:384][:, 64 * m : 64 * m + 64] for c in range(8)]) for m in range(2)], axis=0
    )
    total = (dot_nn(qk, weight_qk[...]) + dot_nn(value, weight_v[...])) * width**-0.5
    own_out[...] = total[:128]
    mate_out[...] = total[128:]


def back_norm_kernel(own, mate, trunk, gamma, grad_res, out):
    g = own[...] + mate[...]
    x = trunk[...]
    scale = lax.rsqrt(jnp.mean(x * x, axis=-1, keepdims=True) + NORM_EPS)
    inner = g * (1.0 + gamma[...])
    slope = inner * scale - x * (scale * scale * scale * jnp.mean(inner * x, axis=-1, keepdims=True))
    out[0] = (grad_res[...] + slope).astype(BF16)
    out[1] = (g * (x * scale)).astype(BF16)


def input_weight_kernel(targets, own_x, mate_x, own_y, mate_y, *outs, which, scales):
    def put(p, s, k, block):
        if p < 7:
            outs[p][s, k] = block
        else:
            outs[7 + s][k] = block

    x = [jnp.concatenate([own_x[t], mate_x[t]], axis=0) for t in range(len(which))]
    for p in range(8):
        spot = pl.ds(at128(targets[p]), 128)
        y = [
            jnp.concatenate([own_y[i, :, spot], mate_y[i, :, spot]], axis=0)
            for i in range(max(which) + 1)
        ]
        for t, i in enumerate(which):
            block = (dot_tn(y[i], x[t]) * scales[t]).astype(BF16)
            for s in range(2):
                for j in range(4):
                    put(p, s, 4 * t + j, block[64 * s : 64 * s + 64, 128 * j : 128 * j + 128])


def back_input_kernel(places, own_y, mate_y, *refs):
    pieces, (own_out, mate_out, w) = chip_pieces(refs[:9]), refs[9:]
    width = own_y.shape[2]
    scale_in = width**-0.5
    for p, piece in enumerate(pieces):
        for s in range(2):
            rows = pl.ds(pl.multiple_of(places[p] * 128 + 64 * s, 64), 64)
            for t in range(3):
                for j in range(4):
                    w[t, rows, 128 * j : 128 * j + 128] = piece(s, 4 * t + j)
    y = [jnp.concatenate([own_y[i], mate_y[i]], axis=0) for i in range(2)]
    for t in range(3):
        grad = dot_nn(y[t // 2], w[t]) * (scale_in if t < 2 else 0.5 * scale_in)
        own_out[t] = grad[:128]
        mate_out[t] = grad[128:]


def adam(weight, gradient, first, second, rate):
    first = BETA_ONE * first + (1.0 - BETA_ONE) * gradient
    second = BETA_TWO * second + (1.0 - BETA_TWO) * gradient * gradient
    fix_one = 1.0 - BETA_ONE**STEP
    fix_two = 1.0 - BETA_TWO**STEP
    update = first / fix_one / (jnp.sqrt(second / fix_two) + ADAM_EPS)
    return weight - rate * (update + WEIGHT_DECAY * weight), first, second


def adam_kernel(source, held, in_own, in_far, qkv_own, qkv_far, ff, master, first, second, new_first, new_second, new_master, new_low):
    step = pl.program_id(0)
    count = master.shape[0]
    for i in range(count):
        slot = step * count + i
        k = source[slot]
        live = (slot < held[0]).astype(F32)
        k_in = jnp.where(k < 24, k, jnp.clip(k - 24, 24, 31))
        from_in = in_own[k_in].astype(F32) + in_far[k_in].astype(F32)
        k_qkv = jnp.clip(k - 24, 0, 23)
        from_qkv = qkv_own[k_qkv].astype(F32) + qkv_far[k_qkv].astype(F32)
        from_ff = ff[jnp.clip(k - 56, 0, 63)].astype(F32)
        is_in = jnp.logical_or(k < 24, jnp.logical_and(k >= 48, k < 56))
        gradient = jnp.where(k >= 56, from_ff, jnp.where(is_in, from_in, from_qkv))
        weight, one, two = adam(master[i], gradient, first[i], second[i], LEARN_RATE)
        weight = weight * live
        new_first[i] = one * live
        new_second[i] = two * live
        new_master[i] = weight
        new_low[i] = weight.astype(BF16)


def ring_order(chips):
    return list(range(0, chips, 2)) + list(range(chips - 1, 0, -2))


def ring_shift(x, chips, step):
    order = ring_order(chips)
    pairs = [
        (2 * order[i] + k, 2 * order[(i + step) % chips] + k) for i in range(chips) for k in range(2)
    ]
    return lax.ppermute(x, "seq", pairs)


def to_mate(x, chips):
    return lax.ppermute(x, "seq", [(i, i ^ 1) for i in range(2 * chips)])


def to_far(x):
    return lax.ppermute(x, "batch", [(0, 1), (1, 0)])


def ring_gather(x, chips):
    half = chips // 2
    pieces = [x]
    ahead = back = x
    for _ in range(1, half):
        ahead = ring_shift(ahead, chips, 1)
        back = ring_shift(back, chips, -1)
        pieces += [ahead, back]
    cut = x.shape[0] // 2
    pieces.append(ring_shift(ahead[:cut], chips, 1))
    pieces.append(ring_shift(back[cut:], chips, -1))
    return pieces


def add_low(a, b):
    return (a.astype(F32) + b.astype(F32)).astype(BF16)


def ring_reduce(parts, chips):
    half = chips // 2
    ahead = ring_shift(parts[-2], chips, 1)
    back = ring_shift(parts[-1], chips, -1)
    for d in range(half - 1, 0, -1):
        mine_ahead, mine_back = parts[2 * d - 1], parts[2 * d]
        if d == half - 1:
            ahead = jnp.stack([add_low(ahead, mine_ahead[0]), mine_ahead[1]])
            back = jnp.stack([mine_back[0], add_low(back, mine_back[1])])
        else:
            ahead, back = add_low(ahead, mine_ahead), add_low(back, mine_back)
        ahead = ring_shift(ahead, chips, 1)
        back = ring_shift(back, chips, -1)
    return (parts[0].astype(F32) + ahead.astype(F32) + back.astype(F32)).astype(BF16)


def gather_small(x, count):
    out = x[None]
    index = lax.axis_index("seq")
    step = 1
    while step < count:
        other = lax.ppermute(out, "seq", [(i, i ^ step) for i in range(count)])
        first = (index & step) == 0
        out = jnp.where(first, jnp.concatenate([out, other]), jnp.concatenate([other, out]))
        step *= 2
    return out


def sum_small(x, count):
    x = x + to_far(x)
    step = 1
    while step < count:
        x = x + lax.ppermute(x, "seq", [(i, i ^ step) for i in range(count)])
        step *= 2
    return x


def fast_shards(
    frames, skip_frames, time_embed, cotangent, segments, owners, master, moment_one, moment_two,
    norm_gains, ff_biases, small_first, small_second,
):
    row_count, seg_len, width = frames.shape
    width_ff = ff_biases.shape[0] - width
    count = row_count * seg_len
    capacity = master.shape[0]
    seq_count = lax.axis_size("seq")
    chips = seq_count // 2
    half_width = width // 2
    group = lax.axis_index("batch")
    here = lax.axis_index("seq")
    chip, core = here // 2, here % 2
    order = jnp.array(ring_order(chips), jnp.int32)
    position = jnp.argmax(order == chip).astype(jnp.int32)
    rel = jnp.array([0, 1, -1, 2, -2, 3, -3, 4], jnp.int32)
    places = order[(position - rel) % chips]
    targets = order[(position + rel) % chips]
    sources = jnp.stack([2 * places + core, 2 * places + 1 - core], axis=1).reshape(-1)
    core_one = core[None]

    def by_core(own, mate):
        return jnp.where(core == 0, jnp.stack([own, mate]), jnp.stack([mate, own]))

    ids = jnp.arange(owners.shape[0], dtype=jnp.int32)
    slots = jnp.sum(
        ((owners[None, :] == owners[:, None]) & (ids[None, :] < ids[:, None])).astype(jnp.int32), axis=1
    )
    cols = width // seq_count
    turned = jnp.swapaxes(master, 1, 2)
    block = (cols, master.shape[1])
    mine_in, mine_qkv, mine_out, ff_keep, ff_send = kernel_call(
        pick_kernel,
        [((24,) + block, BF16), ((24,) + block, BF16), ((8,) + block, BF16), ((2, 16) + block, BF16), ((2, 16) + block, BF16)],
        turned, scalars=(slots, group[None]),
    )
    held = owners == group

    def owned(mask, mine, far):
        return jnp.where(mask.reshape(mask.shape + (1, 1)), mine, far)

    x_own = jnp.stack([frames.reshape(count, width), skip_frames.reshape(count, width), time_embed.reshape(count, width)])
    x_half = lax.dynamic_slice_in_dim(x_own, core * half_width, half_width, 2)
    x_mate = to_mate(lax.dynamic_slice_in_dim(x_own, (1 - core) * half_width, half_width, 2), chips)

    def half_blocks(blocks):
        split = blocks.reshape((-1, 2, 4) + block)
        keep = lax.dynamic_index_in_dim(split, core, 1, False)
        give = lax.dynamic_index_in_dim(split, 1 - core, 1, False)
        got = to_mate(give, chips)
        return by_core(keep, got).reshape((2, -1) + block)

    w_in = owned(held[:24], mine_in, to_far(mine_in))
    in_pieces = ring_gather(half_blocks(w_in), chips)
    w_qkv = owned(held[24:48], mine_qkv, to_far(mine_qkv))
    w_out = owned(held[48:56], mine_out, to_far(mine_out))
    ff_held = jnp.concatenate([held[56:88].reshape(4, 8), held[88:].reshape(4, 8)], axis=1)
    ff_held = lax.dynamic_slice_in_dim(ff_held, 2 * group, 2, 0)
    w_ff = owned(ff_held, ff_keep, to_far(ff_send))

    seg_all = gather_small(segments, seq_count)
    seg_rel = jnp.take(seg_all, sources, axis=0).transpose(1, 0, 2).reshape(row_count, -1)
    seg_col, seg_row = seg_rel[:, :, None], seg_rel[:, None, :]
    half_size = HEAD_DIM // 2
    spot = (sources[:, None] * seg_len + jnp.arange(seg_len, dtype=jnp.int32)[None, :]).reshape(-1).astype(F32)
    inverse = 10000.0 ** (-jnp.arange(half_size, dtype=jnp.int32).astype(F32) / half_size)
    phases = spot[:, None] * inverse[None, :]
    cosine, sine = jnp.cos(phases), jnp.sin(phases)
    cosine = jnp.concatenate([cosine, cosine], axis=1)
    sine = jnp.concatenate([-sine, sine], axis=1)

    part = ((2, count, width), F32)
    own_part, mate_part = kernel_call(
        trunk_kernel, [part, part], x_half, x_mate, *in_pieces, scalars=(places,),
        flops=2 * 3 * 2 * count * width * half_width,
    )
    trunk, gamma, normed = kernel_call(
        norm_kernel, [((count, width), F32), ((count, width), F32), ((count, width), BF16)],
        own_part, to_mate(mate_part, chips),
    )
    normed_pieces = ring_gather(normed, chips)
    normed_pieces = normed_pieces + [to_mate(piece, chips) for piece in normed_pieces]

    row_len = seq_count * seg_len
    head_rows = ((row_count, row_len, HEAD_DIM), BF16)
    queries, keys, values, mixed = kernel_call(
        attend_kernel, [head_rows, head_rows, head_rows, ((seq_count, seg_len, 2 * HEAD_DIM), BF16)],
        w_qkv, cosine, sine, seg_col, seg_row, *normed_pieces, scalars=(sources,),
        scratch=[pltpu.VMEM(*head_rows)], flops=2 * 2 * row_len * (192 * width + 2 * row_len * 64),
    )
    heads = lax.all_to_all(mixed, "seq", 0, 0, tiled=True)

    out_pieces = ring_gather(half_blocks(w_out), chips)
    out_own = jnp.concatenate([jnp.stack(out_pieces[:7]), jnp.concatenate(out_pieces[7:])[None]])
    (w_six,) = kernel_call(
        assemble_out_kernel, [((width, width), BF16)], out_own, to_mate(out_own, chips), scalars=(places, core_one),
    )
    ff_mine = lax.dynamic_index_in_dim(w_ff, core, 0, False)
    ff_give = lax.dynamic_index_in_dim(w_ff, 1 - core, 0, False)
    ff_pieces = ring_gather(by_core(ff_mine, to_mate(ff_give, chips)), chips)

    valid = (segments < UTTS).astype(F32).reshape(count, 1)
    grad_branch = (cotangent.reshape(count, width).astype(F32) * valid).astype(BF16)

    def four(x):
        pair = jnp.stack([x, to_far(x)])
        return jnp.concatenate([pair, to_mate(pair, chips)])

    grad_four = four(grad_branch)

    residual, normed_two, mixed_rows = kernel_call(
        residual_kernel, [((count, width), F32), ((count, width), BF16), ((count, width), BF16)],
        heads, w_six, trunk, norm_gains[None], flops=2 * count * width * width,
    )
    normed_four = four(normed_two).reshape(4 * count, width)
    grad_four = grad_four.reshape(4 * count, width)
    pair_index = 2 * group + core
    up_bias = lax.dynamic_slice_in_dim(ff_biases, pair_index * width, width, 0)[None]
    wide, wide_low = ((4 * count, width), F32), ((4 * count, width), BF16)
    grad_in, branch, hidden, grad_pre, grad_up = kernel_call(
        forward_back_kernel, [wide, wide, wide_low, wide_low, ((1, width), F32)],
        normed_four, grad_four, up_bias, *ff_pieces, scalars=(places,),
        scratch=[pltpu.VMEM((width, width), BF16)] * 2, flops=4 * 2 * 4 * count * width * width,
    )

    def from_four(x):
        x = x.reshape(4, count, width)
        x = x[:2] + to_mate(x[2:], chips)
        return x[0], to_far(x[1].astype(BF16))

    grad_sum, grad_far = from_four(grad_in)
    grad_res, grad_att, grad_heads, grad_gains = kernel_call(
        back_out_kernel,
        [((count, width), F32), ((count, width), BF16), ((seq_count, seg_len, 2 * HEAD_DIM), BF16), ((1, width), F32)],
        grad_sum, grad_far, residual, norm_gains[None], grad_branch, w_six, flops=2 * count * width * width,
    )
    head_grads = lax.all_to_all(grad_heads, "seq", 0, 0, tiled=True)

    qkv_grads, grad_q, grad_k, grad_v = kernel_call(
        attend_back_kernel, [((chips, 6 * seg_len, 2 * HEAD_DIM), BF16), head_rows, head_rows, head_rows],
        queries, keys, values, head_grads, cosine, sine, seg_col, seg_row, scalars=(sources, places),
        scratch=[pltpu.VMEM(*head_rows)] + [pltpu.VMEM((row_count, row_len, HEAD_DIM), F32)] * 3,
        flops=2 * 2 * row_len * row_len * 64 * 5,
    )
    groups = [[2 * c + k for c in range(chips)] for k in range(2)]
    qkv_back = lax.all_to_all(qkv_grads, "seq", 0, 0, tiled=True, axis_index_groups=groups)
    qkv_pieces = ring_gather(w_qkv, chips)
    w_qk, w_v = kernel_call(
        assemble_qkv_kernel, [((width, width), BF16), ((half_width, width), BF16)], *qkv_pieces, scalars=(places,),
    )
    frame_part = ((count, width), F32)
    own_norm, mate_norm = kernel_call(
        back_qkv_kernel, [frame_part, frame_part], qkv_back, w_qk, w_v, flops=2 * 2 * count * width * 3 * half_width,
    )
    (trunk_grads,) = kernel_call(
        back_norm_kernel, [((2, count, width), BF16)], own_norm, to_mate(mate_norm, chips), trunk, gamma, grad_res,
    )
    trunk_mate = to_mate(trunk_grads, chips)

    def half_of(x, which):
        return lax.dynamic_slice_in_dim(x, which * half_width, half_width, 1)[None]

    def piece_outs(blocks):
        return [((2, blocks) + block, BF16)] * 7 + [((blocks,) + block, BF16)] * 2

    scale_in = width**-0.5
    in_parts = kernel_call(
        functools.partial(input_weight_kernel, which=(0, 0, 1), scales=(scale_in, scale_in, 0.5 * scale_in)),
        piece_outs(12), x_half, x_mate, trunk_grads, trunk_mate, scalars=(targets,),
        flops=2 * 3 * 2 * count * width * half_width,
    )
    ff_parts = kernel_call(
        ff_weight_kernel, piece_outs(16), normed_four, grad_four, hidden, grad_pre, scalars=(targets,),
        flops=2 * 2 * 4 * count * width * width,
    )
    (qkv_sum,) = kernel_call(
        qkv_weight_kernel, [((24,) + block, BF16)], grad_q, grad_k, grad_v, *normed_pieces,
        scratch=[pltpu.VMEM((row_count * row_len, width), BF16), pltpu.VMEM((row_count * row_len, 256), BF16)],
        flops=2 * 2 * row_len * 192 * width,
    )
    mixed_mate = to_mate(half_of(mixed_rows, 1 - core), chips)
    att_mate = to_mate(grad_att, chips)
    out_parts = kernel_call(
        functools.partial(input_weight_kernel, which=(0,), scales=(4.0 * scale_in,)),
        piece_outs(4), half_of(mixed_rows, core), mixed_mate, grad_att[None], att_mate[None], scalars=(targets,),
        flops=2 * 2 * count * width * half_width,
    )

    def whole_tiles(total):
        keep = lax.dynamic_index_in_dim(total, core, 0, False).reshape((-1, 4) + block)
        give = lax.dynamic_index_in_dim(total, 1 - core, 0, False).reshape((-1, 4) + block)
        both = by_core(keep, to_mate(give, chips))
        return jnp.swapaxes(both, 0, 1).reshape((-1,) + block)

    ff_total = ring_reduce(ff_parts, chips)
    ff_keep_sum = lax.dynamic_index_in_dim(ff_total, core, 0, False)
    ff_give_sum = lax.dynamic_index_in_dim(ff_total, 1 - core, 0, False)
    ff_own = by_core(ff_keep_sum, to_mate(ff_give_sum, chips))
    ff_far = to_far(ff_own)
    ff_all = jnp.where(group == 0, jnp.concatenate([ff_own, ff_far]), jnp.concatenate([ff_far, ff_own]))
    ff_grads = jnp.concatenate([ff_all[:, :8].reshape((-1,) + block), ff_all[:, 8:].reshape((-1,) + block)])
    out_sum = whole_tiles(ring_reduce(out_parts, chips))
    qkv_far = to_far(qkv_sum)
    in_sum = whole_tiles(ring_reduce(in_parts, chips))
    in_own = jnp.concatenate([in_sum, out_sum])
    in_far = jnp.concatenate([to_far(in_sum), to_far(out_sum)])

    held_count = jnp.sum(held.astype(jnp.int32))
    match = held[None, :] & (slots[None, :] == jnp.arange(capacity, dtype=jnp.int32)[:, None])
    source = jnp.sum(jnp.where(match, ids[None, :], 0), axis=1)
    per_step = math.gcd(capacity, 10)
    state = pl.BlockSpec((per_step,) + block, lambda i, *_: (i, 0, 0))
    whole = lambda a: pl.BlockSpec(a.shape, lambda i, *_: (0,) * a.ndim)
    grads = (in_own, in_far, qkv_sum, qkv_far, ff_grads)
    stack = (capacity,) + block
    new_first, new_second, new_master, new_low = pl.pallas_call(
        adam_kernel,
        grid_spec=pltpu.PrefetchScalarGridSpec(
            num_scalar_prefetch=2, grid=(capacity // per_step,),
            in_specs=[whole(g) for g in grads] + [state] * 3, out_specs=[state] * 4,
        ),
        out_shape=[jax.ShapeDtypeStruct(stack, F32)] * 3 + [jax.ShapeDtypeStruct(stack, BF16)],
        compiler_params=pltpu.CompilerParams(vmem_limit_bytes=48 * MIB),
    )(source, held_count[None], *grads, turned, jnp.swapaxes(moment_one, 1, 2), jnp.swapaxes(moment_two, 1, 2))
    back = lambda a: jnp.swapaxes(a, 1, 2)

    grad_down = jnp.sum(grad_branch.astype(F32), axis=0)
    up_all = lax.dynamic_update_slice_in_dim(jnp.zeros((width_ff,), F32), grad_up[0], pair_index * width, 0)
    small_grad = jnp.concatenate([grad_gains[0], up_all, grad_down])
    small_grad = sum_small(small_grad.reshape(-1, 128), seq_count).reshape(-1)
    small_values = jnp.concatenate([norm_gains, ff_biases])
    small_new, small_one, small_two = adam(small_values, small_grad, small_first, small_second, SMALL_RATE)

    branch_sum, branch_far = from_four(branch)
    output = (residual + branch_sum + branch_far.astype(F32) + ff_biases[None, width_ff:]) * valid
    output = output.astype(BF16).reshape(row_count, seg_len, width)
    own_input, mate_input = kernel_call(
        back_input_kernel, [((3, count, half_width), F32)] * 2, trunk_grads, trunk_mate, *in_pieces, scalars=(places,),
        scratch=[pltpu.VMEM((3, width, half_width), BF16)], flops=2 * 3 * 2 * count * width * half_width,
    )
    got_input = to_mate(mate_input, chips)
    inputs = jnp.where(
        core == 0, jnp.concatenate([own_input, got_input], axis=2), jnp.concatenate([got_input, own_input], axis=2)
    ).reshape(3, row_count, seg_len, width)
    return (
        output, inputs[0], inputs[1], inputs[2],
        back(new_first), back(new_second), back(new_master), back(new_low),
        small_one, small_two, small_new,
    )


def slot_places(owners, group_count, capacity):
    one_hot = (owners[:, None] == jnp.arange(group_count, dtype=jnp.int32)[None, :]).astype(
        jnp.int32
    )
    before = jnp.cumsum(one_hot, axis=0) - one_hot
    slot_index = jnp.sum(before * one_hot, axis=1)
    return owners * capacity + slot_index


def rotate(tensor, offset):
    half_size = tensor.shape[-1] // 2
    position = (offset + jnp.arange(tensor.shape[1], dtype=jnp.int32)).astype(jnp.float32)
    inverse = 10000.0 ** (-jnp.arange(half_size, dtype=jnp.int32).astype(jnp.float32) / half_size)
    phases = position[:, None] * inverse[None, :]
    cosine = jnp.cos(phases)[None, :, None, :]
    sine_part = jnp.sin(phases)[None, :, None, :]
    front_half = tensor[..., :half_size]
    back_half = tensor[..., half_size:]
    return jnp.concatenate(
        [front_half * cosine - back_half * sine_part, front_half * sine_part + back_half * cosine],
        axis=-1,
    )


def adaptive_norm(trunk, gamma_map):
    return (
        trunk
        * lax.rsqrt(jnp.mean(trunk * trunk, axis=-1, keepdims=True) + NORM_EPS)
        * (1.0 + gamma_map)
    )


def root_norm(residual, norm_gains):
    return (
        residual
        * lax.rsqrt(jnp.mean(residual * residual, axis=-1, keepdims=True) + NORM_EPS)
        * norm_gains
    )


def gelu_exact(tensor):
    return jax.nn.gelu(tensor, approximate=False)


def adam_update(weight, gradient, first_moment, second_moment, step_rate):
    first_moment = BETA_ONE * first_moment + (1.0 - BETA_ONE) * gradient
    second_moment = BETA_TWO * second_moment + (1.0 - BETA_TWO) * gradient * gradient
    fix_one = 1.0 - BETA_ONE**STEP
    fix_two = 1.0 - BETA_TWO**STEP
    update = first_moment / fix_one / (jnp.sqrt(second_moment / fix_two) + ADAM_EPS)
    return (weight - step_rate * (update + WEIGHT_DECAY * weight), first_moment, second_moment)


def matmul(former, latter):
    return jnp.dot(former, latter, preferred_element_type=jnp.float32)


def contract_rows(former, latter):
    return lax.dot_general(
        former, latter, (((0,), (0,)), ((), ())), preferred_element_type=jnp.float32
    )


def contract_cols(former, latter):
    return lax.dot_general(
        former, latter, (((1,), (1,)), ((), ())), preferred_element_type=jnp.float32
    )


def score_block(queries, key_rows, same_utt):
    scores = jnp.einsum(
        "qhd,khd->hqk", queries, key_rows, preferred_element_type=jnp.float32
    ) * HEAD_DIM ** (-0.5)
    scores = jnp.where(same_utt[None], scores, MASKED_SCORE)
    row_max = jnp.max(scores, axis=-1, keepdims=True)
    exponent = jnp.exp(scores - row_max)
    total = jnp.sum(exponent, axis=-1, keepdims=True)
    return (exponent / total, row_max[..., 0], total[..., 0])


def attend(element):
    queries, key_rows, values, same_utt = element
    attn_probs, row_max, total = score_block(queries, key_rows, same_utt)
    mixed = jnp.einsum(
        "hqk,khd->qhd", attn_probs.astype(jnp.bfloat16), values, preferred_element_type=jnp.float32
    )
    return (mixed.astype(jnp.bfloat16), attn_probs, row_max, total)


def probs_only(element):
    return score_block(element[0], element[1], element[2])


def attend_query(element):
    queries, key_rows, values, attn_probs, grad_mixed = element
    prob_grad = jnp.einsum("qhd,khd->hqk", grad_mixed, values, preferred_element_type=jnp.float32)
    inner_sum = jnp.sum(attn_probs * prob_grad, axis=-1, keepdims=True)
    score_grad = (attn_probs * (prob_grad - inner_sum)).astype(jnp.bfloat16)
    query_grad = jnp.einsum(
        "hqk,khd->qhd", score_grad, key_rows, preferred_element_type=jnp.float32
    ) * HEAD_DIM ** (-0.5)
    return (query_grad, inner_sum[..., 0])


def attend_keys(element):
    query_all, grad_all, max_all, total_all, inner_all, seg_query, key_own, value_own, seg_own = (
        element
    )
    scores = jnp.einsum(
        "qhd,khd->hqk", query_all, key_own, preferred_element_type=jnp.float32
    ) * HEAD_DIM ** (-0.5)
    same_utt = seg_query[:, None] == seg_own[None, :]
    scores = jnp.where(same_utt[None], scores, MASKED_SCORE)
    attn_probs = jnp.exp(scores - max_all[..., None]) / total_all[..., None]
    prob_grad = jnp.einsum("qhd,khd->hqk", grad_all, value_own, preferred_element_type=jnp.float32)
    score_grad = (attn_probs * (prob_grad - inner_all[..., None])).astype(jnp.bfloat16)
    key_grad = jnp.einsum(
        "hqk,qhd->khd", score_grad, query_all, preferred_element_type=jnp.float32
    ) * HEAD_DIM ** (-0.5)
    value_grad = jnp.einsum(
        "hqk,qhd->khd",
        attn_probs.astype(jnp.bfloat16),
        grad_all,
        preferred_element_type=jnp.float32,
    )
    return (key_grad, value_grad)


def general_shards(
    frames,
    skip_frames,
    time_embed,
    cotangent,
    segments,
    owners,
    master,
    moment_one,
    moment_two,
    norm_gains,
    ff_biases,
    small_first,
    small_second,
):
    row_count, seg_len, model_width = frames.shape
    width_ff = ff_biases.shape[0] - model_width
    frame_count = row_count * seg_len
    group_count = lax.axis_size("batch")
    capacity = master.shape[0]
    block_rows = master.shape[1]
    scale_in = model_width ** (-0.5)
    scale_time = 0.5 * model_width ** (-0.5)
    scale_out = 4.0 * model_width ** (-0.5)
    scale_ff = width_ff ** (-0.5)
    places = slot_places(owners, group_count, capacity)
    low_master = master.astype(jnp.bfloat16)
    all_slots = lax.all_gather(low_master, "batch", axis=0, tiled=True)
    columns = jnp.take(all_slots, places, axis=0)
    tile_stack = lax.all_gather(columns, "seq", axis=2, tiled=True).reshape(15, model_width, model_width)
    up_weight = jnp.concatenate(
        [tile_stack[7], tile_stack[8], tile_stack[9], tile_stack[10]], axis=1
    )
    down_weight = tile_stack[11:15].reshape(width_ff, model_width)
    flat_frames = frames.reshape(frame_count, model_width)
    flat_skip = skip_frames.reshape(frame_count, model_width)
    flat_time = time_embed.reshape(frame_count, model_width)
    offset = lax.axis_index("seq") * seg_len

    def rotate_here(tensor):
        return rotate(tensor, offset)

    def split_heads(tensor):
        return tensor.reshape(row_count, seg_len, HEADS, HEAD_DIM)

    trunk = (matmul(flat_frames, tile_stack[0]) + matmul(flat_skip, tile_stack[1])) * scale_in
    gamma_map = matmul(flat_time, tile_stack[2]) * scale_time
    normed_f32, norm_pull = jax.vjp(adaptive_norm, trunk, gamma_map)
    normed = normed_f32.astype(jnp.bfloat16)
    query_rot, query_pull = jax.vjp(
        rotate_here, split_heads(matmul(normed, tile_stack[3]) * scale_in)
    )
    key_rot, key_pull = jax.vjp(rotate_here, split_heads(matmul(normed, tile_stack[4]) * scale_in))
    queries = query_rot.astype(jnp.bfloat16)
    key_local = key_rot.astype(jnp.bfloat16).reshape(row_count, seg_len, model_width)
    value_local = (
        (matmul(normed, tile_stack[5]) * scale_in)
        .astype(jnp.bfloat16)
        .reshape(row_count, seg_len, model_width)
    )
    seg_low = segments.astype(jnp.bfloat16)
    key_all, value_all, seg_all = (
        lax.all_gather(key_local, "seq", axis=1, tiled=True),
        lax.all_gather(value_local, "seq", axis=1, tiled=True),
        lax.all_gather(seg_low, "seq", axis=1, tiled=True),
    )
    key_total = key_all.shape[1]
    key_heads = key_all.reshape(row_count, key_total, HEADS, HEAD_DIM)
    value_heads = value_all.reshape(row_count, key_total, HEADS, HEAD_DIM)
    same_utt = seg_low[:, :, None] == seg_all[:, None, :]
    mixed_heads, probs_kept, max_kept, total_kept = lax.map(
        attend, (queries, key_heads, value_heads, same_utt)
    )
    mixed_rows = mixed_heads.reshape(frame_count, model_width)
    residual = trunk + matmul(mixed_rows, tile_stack[6]) * scale_out
    normed_two_f32, root_pull = jax.vjp(root_norm, residual, norm_gains)
    normed_two = normed_two_f32.astype(jnp.bfloat16)
    pre_act = matmul(normed_two, up_weight) * scale_in + ff_biases[:width_ff]
    activation, gelu_pull = jax.vjp(gelu_exact, pre_act)
    hidden = activation.astype(jnp.bfloat16)
    branch = matmul(hidden, down_weight) * scale_ff + ff_biases[width_ff:]
    valid_row = (segments < UTTS).astype(jnp.float32).reshape(frame_count, 1)
    output = (
        ((residual + branch) * valid_row)
        .astype(jnp.bfloat16)
        .reshape(row_count, seg_len, model_width)
    )
    grad_out = cotangent.reshape(frame_count, model_width).astype(jnp.float32) * valid_row
    grad_branch = grad_out.astype(jnp.bfloat16)
    grad_down_bias = jnp.sum(grad_branch.astype(jnp.float32), axis=0)
    down_grads = contract_rows(hidden, grad_branch) * scale_ff
    grad_hidden = contract_cols(grad_branch, down_weight) * scale_ff
    grad_pre = gelu_pull(grad_hidden)[0].astype(jnp.bfloat16)
    grad_up_bias = jnp.sum(grad_pre.astype(jnp.float32), axis=0)
    up_grads = contract_rows(normed_two, grad_pre) * scale_in
    grad_normed_two = contract_cols(grad_pre, up_weight) * scale_in
    grad_residual_norm, grad_gains = root_pull(grad_normed_two)
    grad_residual = grad_out + grad_residual_norm
    grad_attention = grad_residual.astype(jnp.bfloat16)
    out_grads = contract_rows(mixed_rows, grad_attention) * scale_out
    grad_mixed = (contract_cols(grad_attention, tile_stack[6]) * scale_out).astype(jnp.bfloat16)
    grad_mixed = grad_mixed.reshape(row_count, seg_len, HEADS, HEAD_DIM)
    key_again, value_again, seg_again = (
        lax.all_gather(key_local, "seq", axis=1, tiled=True),
        lax.all_gather(value_local, "seq", axis=1, tiled=True),
        lax.all_gather(seg_low, "seq", axis=1, tiled=True),
    )
    back_keys = key_again.reshape(row_count, key_total, HEADS, HEAD_DIM)
    back_values = value_again.reshape(row_count, key_total, HEADS, HEAD_DIM)
    same_again = seg_low[:, :, None] == seg_again[:, None, :]
    back_probs, back_max, back_total = lax.map(probs_only, (queries, back_keys, same_again))
    query_raw, inner_sum = lax.map(
        attend_query, (queries, back_keys, back_values, back_probs, grad_mixed)
    )
    query_all, grad_all = (
        lax.all_gather(queries, "seq", axis=1, tiled=True),
        lax.all_gather(grad_mixed, "seq", axis=1, tiled=True),
    )
    max_all, total_all, inner_all = (
        lax.all_gather(back_max, "seq", axis=2, tiled=True),
        lax.all_gather(back_total, "seq", axis=2, tiled=True),
        lax.all_gather(inner_sum, "seq", axis=2, tiled=True),
    )
    key_own = key_local.reshape(row_count, seg_len, HEADS, HEAD_DIM)
    value_own = value_local.reshape(row_count, seg_len, HEADS, HEAD_DIM)
    key_sum, value_sum = lax.map(
        attend_keys,
        (
            query_all,
            grad_all,
            max_all,
            total_all,
            inner_all,
            seg_again,
            key_own,
            value_own,
            seg_low,
        ),
    )
    grad_q = query_pull(query_raw)[0].reshape(frame_count, model_width).astype(jnp.bfloat16)
    grad_k = key_pull(key_sum)[0].reshape(frame_count, model_width).astype(jnp.bfloat16)
    grad_v = value_sum.reshape(frame_count, model_width).astype(jnp.bfloat16)
    query_grads = contract_rows(normed, grad_q) * scale_in
    key_grads = contract_rows(normed, grad_k) * scale_in
    value_grads = contract_rows(normed, grad_v) * scale_in
    grad_normed = (
        contract_cols(grad_q, tile_stack[3])
        + contract_cols(grad_k, tile_stack[4])
        + contract_cols(grad_v, tile_stack[5])
    ) * scale_in
    grad_trunk_norm, grad_gamma_f32 = norm_pull(grad_normed)
    grad_trunk = (grad_residual + grad_trunk_norm).astype(jnp.bfloat16)
    grad_gamma = grad_gamma_f32.astype(jnp.bfloat16)
    frame_grads = contract_rows(flat_frames, grad_trunk) * scale_in
    skip_grads = contract_rows(flat_skip, grad_trunk) * scale_in
    time_grads = contract_rows(flat_time, grad_gamma) * scale_time
    grad_frames = (contract_cols(grad_trunk, tile_stack[0]) * scale_in).reshape(
        row_count, seg_len, model_width
    )
    grad_skip = (contract_cols(grad_trunk, tile_stack[1]) * scale_in).reshape(
        row_count, seg_len, model_width
    )
    grad_time = (contract_cols(grad_gamma, tile_stack[2]) * scale_time).reshape(
        row_count, seg_len, model_width
    )
    first_tiles = jnp.stack(
        [frame_grads, skip_grads, time_grads, query_grads, key_grads, value_grads, out_grads]
    )
    up_tiles = up_grads.reshape(model_width, 4, model_width).transpose(1, 0, 2)
    down_tiles = down_grads.reshape(4, model_width, model_width)
    blocks = jnp.concatenate([first_tiles, up_tiles, down_tiles], axis=0).reshape(
        -1, block_rows, model_width
    )
    block_count = blocks.shape[0]
    partial_cols = lax.psum_scatter(
        blocks.astype(jnp.bfloat16), "seq", scatter_dimension=2, tiled=True
    )
    matches = places[None, :] == jnp.arange(group_count * capacity, dtype=jnp.int32)[:, None]
    source = jnp.sum(
        jnp.where(matches, jnp.arange(block_count, dtype=jnp.int32)[None, :], 0), axis=1
    )
    filled = jnp.any(matches, axis=1)
    placed = jnp.where(filled[:, None, None], jnp.take(partial_cols, source, axis=0), 0)
    reduced = lax.psum_scatter(placed, "batch", scatter_dimension=0, tiled=True).astype(
        jnp.float32
    )
    small_grad = jnp.concatenate([grad_gains, grad_up_bias, grad_down_bias])
    small_grad = lax.psum(small_grad, ("seq", "batch"))
    owner_index = lax.axis_index("batch")
    held_count = jnp.sum((owners == owner_index).astype(jnp.int32))
    live_slot = (jnp.arange(capacity, dtype=jnp.int32) < held_count).astype(jnp.float32)[
        :, None, None
    ]
    new_master, new_first, new_second = adam_update(
        master, reduced, moment_one, moment_two, LEARN_RATE
    )
    new_master = new_master * live_slot
    new_first = new_first * live_slot
    new_second = new_second * live_slot
    small_values = jnp.concatenate([norm_gains, ff_biases])
    small_new, small_first_new, small_second_new = adam_update(
        small_values, small_grad, small_first, small_second, SMALL_RATE
    )
    return (
        output,
        grad_frames,
        grad_skip,
        grad_time,
        new_first,
        new_second,
        new_master,
        new_master.astype(jnp.bfloat16),
        small_first_new,
        small_second_new,
        small_new,
    )


def solution(mesh):
    fast = mesh.shape["seq"] == HEADS and mesh.shape["batch"] == 2
    rows, slots, whole = P("batch", "seq", None), P("batch", None, "seq"), P()
    return jax.shard_map(
        fast_shards if fast else general_shards,
        mesh=mesh,
        in_specs=(rows, rows, rows, rows, P("batch", "seq"), whole, slots, slots, slots, whole, whole, whole, whole),
        out_specs=(rows, rows, rows, rows, slots, slots, slots, slots, whole, whole, whole),
        check_vma=False,
    )
```

```python
import functools
import math

import jax
import jax.numpy as jnp
from jax import lax
from jax.experimental import pallas as pl
from jax.experimental.pallas import tpu as pltpu
from jax.sharding import PartitionSpec as P

HEADS = 16
HEAD_DIM = 64
UTTS = 8
STEP = 10
NORM_EPS = 1e-06
MASKED_SCORE = -1e30
BETA_ONE = 0.9
BETA_TWO = 0.999
ADAM_EPS = 1e-08
WEIGHT_DECAY = 0.01
LEARN_RATE = 1.0
SMALL_RATE = 0.1

F32 = jnp.float32
BF16 = jnp.bfloat16
MIB = 1 << 20


def padded(shape, dtype):
    size = jnp.dtype(dtype).itemsize
    rows = 32 // size
    shape = (1,) * (2 - len(shape)) + tuple(shape)
    return math.prod(shape[:-2]) * (-(-shape[-2] // rows) * rows) * (-(-shape[-1] // 128) * 128) * size


def kernel_call(body, outs, *args, scalars=(), scratch=(), room=10, flops=0, far_in=(), far_out=()):
    n_in, n_out = len(args), len(outs)
    vmem, hbm = pl.BlockSpec(memory_space=pltpu.VMEM), pl.BlockSpec(memory_space=pltpu.HBM)
    specs = [pl.BlockSpec(memory_space=pltpu.SMEM) for _ in scalars]
    specs += [hbm if i in far_in else vmem for i in range(n_in)]
    moved = sum(padded(a.shape, a.dtype) for a in args) + sum(padded(s, d) for s, d in outs)
    held = moved + sum(padded(ref.shape, ref.dtype) for ref in scratch)
    far = [pltpu.VMEM(args[i].shape, args[i].dtype) for i in far_in] + [pltpu.VMEM(*outs[i]) for i in far_out]
    copies = [pltpu.SemaphoreType.DMA((len(far),))] if far else []

    def whole(*refs):
        refs = list(refs)
        first = len(scalars)
        if far:
            sems = refs.pop()
            held_refs = refs[len(refs) - len(far) :]
            refs = refs[: len(refs) - len(far)]
            pairs = []
            for n, i in enumerate(far_in):
                pairs.append(pltpu.make_async_copy(refs[first + i], held_refs[n], sems.at[n]))
                refs[first + i] = held_refs[n]
            results = []
            for n, i in enumerate(far_out, len(far_in)):
                results.append(pltpu.make_async_copy(held_refs[n], refs[first + n_in + i], sems.at[n]))
                refs[first + n_in + i] = held_refs[n]
            for copy in pairs:
                copy.start()
            for copy in pairs:
                copy.wait()
        body(*refs)
        if far:
            for copy in results:
                copy.start()
            for copy in results:
                copy.wait()

    return pl.pallas_call(
        whole,
        out_shape=[jax.ShapeDtypeStruct(shape, dtype) for shape, dtype in outs],
        in_specs=specs,
        out_specs=[hbm if i in far_out else vmem for i in range(n_out)],
        scratch_shapes=list(scratch) + far + copies,
        compiler_params=pltpu.CompilerParams(vmem_limit_bytes=min(held + room * MIB, 58 * MIB)),
        cost_estimate=pl.CostEstimate(flops=int(flops), bytes_accessed=int(moved), transcendentals=0),
    )(*scalars, *args)


def dot_nn(a, b):
    return jnp.dot(a, b, preferred_element_type=F32)


def dot_nt(a, b):
    return lax.dot_general(a, b, (((1,), (1,)), ((), ())), preferred_element_type=F32)


def dot_tn(a, b):
    return lax.dot_general(a, b, (((0,), (0,)), ((), ())), preferred_element_type=F32)


def lanes(blocks):
    return jnp.concatenate(blocks, axis=-1)


def at128(index):
    return pl.multiple_of(index * 128, 128)


def normal_cdf(x):
    return 0.5 * (1.0 + lax.erf(x * (2.0**-0.5)))


OUT_ROWS, SEG_ROWS, PIECE_ROWS, PIECE_CUT = 768, 1280, 1312, 640


def pick_kernel(slots, place, master, keep, far_send, give, heads, pair_own, pair_far, pair_mate, pair_diag):
    group, core = place[0], place[1]

    def low(k):
        return master[slots[k]].astype(BF16)

    def tile_pair(pair, j):
        return low((7 + pair) * 8 + j), low((11 + pair) * 8 + j)

    mine = pl.ds(pl.multiple_of(32 * group, 32), 32)
    other = pl.ds(pl.multiple_of(32 - 32 * group, 32), 32)
    for k in range(24):
        keep[32 * k : 32 * k + 32] = master[slots[k], mine].astype(BF16)
        far_send[32 * k : 32 * k + 32] = master[slots[k], other].astype(BF16)
    for j in range(4):
        rows = slice(OUT_ROWS + 64 * j, OUT_ROWS + 64 * j + 64)
        block = low(48 + 4 * core + j)
        keep[rows] = block
        far_send[rows] = block
        give[64 * j : 64 * j + 64] = low(52 - 4 * core + j)
    for k in range(24):
        heads[k] = low(24 + k)
    for j in range(8):
        pair_far[j], pair_far[8 + j] = tile_pair(2 - 2 * group + core, j)
        pair_own[j], pair_own[8 + j] = tile_pair(2 * group + core, j)
        pair_mate[j], pair_mate[8 + j] = tile_pair(2 * group + 1 - core, j)
        pair_diag[j], pair_diag[8 + j] = tile_pair(3 - 2 * group - core, j)


def select_in_kernel(held, place, own, far, mate, diag, seg_own, seg_mate, out):
    group, core = place[0], place[1]
    for k in range(24):
        rows = slice(32 * k, 32 * k + 32)
        out[rows] = jnp.where(held[k] == group, own[rows], far[rows])
    for j in range(4):
        mine = held[48 + 4 * core + j] == group
        rows, part = slice(OUT_ROWS + 64 * j, OUT_ROWS + 64 * j + 64), slice(64 * j, 64 * j + 64)
        out[rows] = jnp.where(mine, own[rows], far[rows])
        out[OUT_ROWS + 256 + 64 * j : OUT_ROWS + 320 + 64 * j] = jnp.where(mine, mate[part], diag[part])
    out[SEG_ROWS : SEG_ROWS + 16] = seg_own[...]
    out[SEG_ROWS + 16 : SEG_ROWS + 32] = seg_mate[...]


def select_heads_kernel(held, place, own, far, out):
    for k in range(24):
        out[k] = jnp.where(held[24 + k] == place[0], own[k], far[k])


def select_pairs_kernel(held, place, own, far, mate, diag, out):
    group, core = place[0], place[1]
    for half, first in ((0, 7), (1, 11)):
        for j in range(8):
            k = 8 * half + j
            mine = held[(first + 2 * group + core) * 8 + j] == group
            out[core, k] = jnp.where(mine, own[k], far[k])
            out[1 - core, k] = jnp.where(mine, mate[k], diag[k])


def ring_readers(refs):
    def last(first, count):
        if first < PIECE_CUT:
            return refs[7][first : first + count, :]
        return refs[8][first - PIECE_CUT : first - PIECE_CUT + count, :]

    return [lambda first, count, r=r: r[first : first + count, :] for r in refs[:7]] + [last]


def ring_blocks(refs):
    return [lambda s, k, r=r: r[s, k] for r in refs]


def trunk_kernel(places, own_x, far_x, mate_x, diag_x, *refs):
    pieces, outs, (seg_out, weight) = ring_readers(refs[:9]), refs[9:13], refs[13:]
    width = own_x.shape[-1]
    count = own_x.shape[1]
    scale_in = width**-0.5
    for p, piece in enumerate(pieces):
        rows = pl.ds(pl.multiple_of(32 * places[p], 32), 32)
        for t in range(3):
            for j in range(8):
                weight[t, rows, 128 * j : 128 * j + 128] = piece(256 * t + 32 * j, 32)
        ids = [piece(SEG_ROWS + 16 * m, 16).astype(F32)[0:8, 0:64] for m in range(2)]
        seg_out[:, 128 * p : 128 * p + 128] = lanes(ids)
    x = [jnp.concatenate([ref[t] for ref in (own_x, far_x, mate_x, diag_x)], axis=0) for t in range(3)]
    trunk = (dot_nt(x[0], weight[0]) + dot_nt(x[1], weight[1])) * scale_in
    gamma = dot_nt(x[2], weight[2]) * (0.5 * scale_in)
    for i, out in enumerate(outs):
        out[0] = trunk[i * count : i * count + count]
        out[1] = gamma[i * count : i * count + count]


def assemble_out_kernel(places, place, *refs):
    out = refs[9]
    core = place[1]
    for p, piece in enumerate(ring_readers(refs[:9])):
        for m in range(2):
            column = 64 * core if m == 0 else 64 - 64 * core
            rows = pl.ds(pl.multiple_of(places[p] * 128 + column, 64), 64)
            for j in range(4):
                out[rows, 128 * j : 128 * j + 128] = piece(OUT_ROWS + 256 * m + 64 * j, 64)


def by_quarter(parts, mine):
    found = []
    for q in range(4):
        low = jnp.where(mine == 0, parts[q], parts[q ^ 1])
        high = jnp.where(mine == 2, parts[q ^ 2], parts[q ^ 3])
        found.append(jnp.where(mine < 2, low, high))
    return found


def norm_kernel(place, own, far, mate, diag, trunk_out, gamma_out, normed_out):
    mine = 2 * place[1] + place[0]
    for i, out in enumerate((trunk_out, gamma_out)):
        parts = by_quarter([ref[i] for ref in (own, far, mate, diag)], mine)
        for c in range(8):
            out[:, 128 * c : 128 * c + 128] = lanes([part[:, 32 * c : 32 * c + 32] for part in parts])
    trunk = trunk_out[...]
    scale = lax.rsqrt(jnp.mean(trunk * trunk, axis=-1, keepdims=True) + NORM_EPS)
    normed_out[...] = (trunk * scale * (1.0 + gamma_out[...])).astype(BF16)


def swap_halves(x):
    half = HEAD_DIM // 2
    return jnp.concatenate([x[:, half:], x[:, :half]], axis=1)


def frame_rows(refs, p, m):
    base = 9 * m
    if p < 7:
        return refs[base + p][...]
    return jnp.concatenate([refs[base + 7][...], refs[base + 8][...]], axis=0)


def attend_kernel(sources, weight, cosine, sine, seg, *refs):
    normed = refs[:18]
    qkv_ref, out_ref, x_ref, mixed = refs[18:]
    q_ref, k_ref, v_ref = (qkv_ref.at[t] for t in range(3))
    width = normed[0].shape[1]
    scale_in = width**-0.5
    w = jnp.concatenate(
        [lanes([weight[8 * t + j] for j in range(8)]) for t in range(3)], axis=0
    )
    row_len = q_ref.shape[1]
    for p in range(8):
        for m in range(2):
            u = 2 * p + m
            spot = pl.ds(u * 64, 64)
            rows = frame_rows(normed, p, m)
            for r in range(2):
                x_ref[pl.ds(r * row_len + u * 64, 64)] = rows[64 * r : 64 * r + 64]
            qkv = dot_nt(rows, w) * scale_in
            c, s = cosine[spot], sine[spot]
            for r in range(2):
                part = qkv[64 * r : 64 * r + 64]
                for ref, lo in ((q_ref, 0), (k_ref, 64)):
                    x = part[:, lo : lo + 64]
                    ref[r, spot] = (x * c + swap_halves(x) * s).astype(BF16)
                v_ref[r, spot] = part[:, 128:192].astype(BF16)
    block = 256
    seg_cols = jnp.transpose(seg[...])
    for r in range(2):
        key, value = k_ref[r], v_ref[r]
        seg_keys = seg[r : r + 1, :]
        for q in range(row_len // block):
            spot = pl.ds(q * block, block)
            scores = dot_nt(q_ref[r, spot], key) * HEAD_DIM**-0.5
            same = seg_cols[q * block : q * block + block, r : r + 1] == seg_keys
            scores = jnp.where(same, scores, MASKED_SCORE)
            top = jnp.max(scores, axis=-1, keepdims=True)
            exponent = jnp.exp(scores - top)
            total = jnp.sum(exponent, axis=-1, keepdims=True)
            probs = (exponent * (1.0 / total)).astype(BF16)
            mixed[r, spot] = dot_nn(probs, value).astype(BF16)
    for u in range(16):
        spot = pl.ds(u * 64, 64)
        out_ref[sources[u]] = lanes([mixed[0, spot], mixed[1, spot]])


def residual_kernel(core, heads, w_own, w_mate, trunk, gains, res_out, normed_out, mixed_out):
    scale_out = 4.0 * trunk.shape[1] ** -0.5
    for r in range(2):
        for j in range(8):
            pair = [heads[2 * j + i][:, 64 * r : 64 * r + 64] for i in range(2)]
            mixed_out[64 * r : 64 * r + 64, 128 * j : 128 * j + 128] = lanes(pair)
    here = pl.ds(pl.multiple_of(core[0] * 512, 512), 512)
    there = pl.ds(pl.multiple_of(512 - core[0] * 512, 512), 512)
    attention = dot_nt(mixed_out[:, here], w_own[...]) + dot_nt(mixed_out[:, there], w_mate[...])
    residual = trunk[...] + attention * scale_out
    res_out[...] = residual
    scale = lax.rsqrt(jnp.mean(residual * residual, axis=-1, keepdims=True) + NORM_EPS)
    normed_out[...] = (residual * scale * gains[...]).astype(BF16)


def forward_back_kernel(places, *refs):
    normed, grad, bias, pieces, refs = refs[:4], refs[4:8], refs[8], ring_blocks(refs[9:17]), refs[17:]
    grad_in, branch, (hidden_out, pre_out, bias_out, w_up, w_down, branch_acc) = refs[:4], refs[4:8], refs[8:]
    width = w_up.shape[1]
    count = normed[0].shape[0]
    scale_in = width**-0.5
    scale_ff = (4 * width) ** -0.5
    for p, piece in enumerate(pieces):
        for s in range(2):
            rows = pl.ds(pl.multiple_of(places[p] * 128 + 64 * s, 64), 64)
            for j in range(8):
                w_up[rows, 128 * j : 128 * j + 128] = piece(s, j)
                w_down[rows, 128 * j : 128 * j + 128] = piece(s, 8 + j)
    x = jnp.concatenate([ref[...] for ref in normed], axis=0)
    g = jnp.concatenate([ref[...] for ref in grad], axis=0)
    block = 256
    for h in range(width // block):
        spot = slice(h * block, h * block + block)
        pre = dot_nt(x, w_up[spot, :]) * scale_in + bias[:, spot]
        cdf = normal_cdf(pre)
        hidden = (pre * cdf).astype(BF16)
        slope = cdf + pre * (jnp.exp(-0.5 * pre * pre) * (2.0 * math.pi) ** -0.5)
        grad_pre = slope * (dot_nn(g, w_down[:, spot]) * scale_ff)
        grad_pre = grad_pre.astype(BF16)
        hidden_out[:, spot] = hidden
        pre_out[:, spot] = grad_pre
        bias_out[:, spot] = jnp.sum(grad_pre.astype(F32), axis=0, keepdims=True)
        grad_part = dot_nn(grad_pre, w_up[spot, :]) * scale_in
        out_part = dot_nt(hidden, w_down[:, spot]) * scale_ff
        for i in range(4):
            rows = slice(i * count, i * count + count)
            if h == 0:
                grad_in[i][...] = grad_part[rows]
            else:
                grad_in[i][...] += grad_part[rows]
        if h == 0:
            branch_acc[...] = out_part
        else:
            branch_acc[...] += out_part
    for i in range(4):
        branch[i][...] = branch_acc[i * count : i * count + count, :].astype(BF16)


def ff_weight_kernel(targets, *refs):
    normed, grad, (hidden, pre), outs = refs[:4], refs[4:8], refs[8:10], refs[10:]
    width = hidden.shape[1]
    scale_in = width**-0.5
    scale_ff = (4 * width) ** -0.5
    x = jnp.concatenate([ref[...] for ref in normed], axis=0)
    for p in range(8):
        spot = pl.ds(at128(targets[p]), 128)
        g = jnp.concatenate([ref[:, spot] for ref in grad], axis=0)
        up = (dot_tn(pre[:, spot], x) * scale_in).astype(BF16)
        down = (dot_tn(g, hidden[...]) * scale_ff).astype(BF16)
        for s in range(2):
            rows = slice(64 * s, 64 * s + 64)
            for j in range(8):
                outs[p][s, j] = up[rows, 128 * j : 128 * j + 128]
                outs[p][s, 8 + j] = down[rows, 128 * j : 128 * j + 128]


def quarters(x, mine, outs):
    parts = [lanes([x[:, 128 * c + 32 * q : 128 * c + 32 * q + 32] for c in range(x.shape[1] // 128)]) for q in range(4)]
    for out, part in zip(outs, by_quarter(parts, mine)):
        out[...] = part


def back_out_kernel(place, grad_own, grad_mate, grad_far, residual, gains, grad_out, w_own, w_mate, grad_res, heads, gain_out, *att):
    width = residual.shape[1]
    g = grad_own[...] + grad_mate[...] + grad_far[...].astype(F32)
    x = residual[...]
    scale = lax.rsqrt(jnp.mean(x * x, axis=-1, keepdims=True) + NORM_EPS)
    gain_out[...] = jnp.sum(g * x * scale, axis=0, keepdims=True)
    inner = g * gains[...]
    slope = inner * scale - x * (scale * scale * scale * jnp.mean(inner * x, axis=-1, keepdims=True))
    total = grad_out[...].astype(F32) + slope
    grad_res[...] = total
    low = total.astype(BF16)
    quarters(low, 2 * place[1] + place[0], att)
    halves = [dot_nn(low, w[...]) * (4.0 * width**-0.5) for w in (w_own, w_mate)]
    mixed = jnp.where(place[1] == 0, lanes(halves), lanes(halves[::-1])).astype(BF16)
    for j in range(8):
        rows = [mixed[64 * r : 64 * r + 64, 128 * j : 128 * j + 128] for r in range(2)]
        heads[2 * j] = lanes([rows[0][:, :64], rows[1][:, :64]])
        heads[2 * j + 1] = lanes([rows[0][:, 64:], rows[1][:, 64:]])


def attend_back_kernel(sources, qkv_ref, grads, cosine, sine, seg, own_out, mate_out, done_ref, g_ref, acc_q, acc_k, acc_v):
    q_ref, k_ref, v_ref = (qkv_ref.at[t] for t in range(3))
    dq_ref, dk_ref, dv_ref = (done_ref.at[t] for t in range(3))
    row_len = q_ref.shape[1]
    for u in range(16):
        spot = pl.ds(u * 64, 64)
        both = grads[sources[u]]
        g_ref[0, spot] = both[:, :64]
        g_ref[1, spot] = both[:, 64:]
    block = 256
    seg_cols = jnp.transpose(seg[...])
    for r in range(2):
        key, value = k_ref[r], v_ref[r]
        for q in range(row_len // block):
            spot = pl.ds(q * block, block)
            query, grad = q_ref[r, spot], g_ref[r, spot]
            scores = dot_nt(key, query) * HEAD_DIM**-0.5
            same = seg_cols[:, r : r + 1] == seg[r : r + 1, q * block : q * block + block]
            scores = jnp.where(same, scores, MASKED_SCORE)
            top = jnp.max(scores, axis=0, keepdims=True)
            exponent = jnp.exp(scores - top)
            total = jnp.sum(exponent, axis=0, keepdims=True)
            probs = exponent * (1.0 / total)
            prob_grad = dot_nt(value, grad)
            inner = jnp.sum(probs * prob_grad, axis=0, keepdims=True)
            score_grad = (probs * (prob_grad - inner)).astype(BF16)
            acc_q[r, spot] = dot_tn(score_grad, key)
            key_part = dot_nn(score_grad, query)
            value_part = dot_nn(probs.astype(BF16), grad)
            if q == 0:
                acc_k[r] = key_part
                acc_v[r] = value_part
            else:
                acc_k[r] += key_part
                acc_v[r] += value_part
        c, s = cosine[...], sine[...]
        for ref, acc in ((dq_ref, acc_q), (dk_ref, acc_k)):
            g = acc[r] * HEAD_DIM**-0.5
            ref[r] = (g * c + swap_halves(g * s)).astype(BF16)
        dv_ref[r] = acc_v[r].astype(BF16)
    empty = jnp.zeros((64, HEAD_DIM), BF16)
    for p in range(8):
        for m, out in enumerate((own_out, mate_out)):
            spot = pl.ds((2 * p + m) * 64, 64)
            for r in range(2):
                rows = pl.ds(128 * p + 64 * r, 64)
                out[rows, 0:128] = lanes([dq_ref[r, spot], dk_ref[r, spot]])
                out[rows, 128:256] = lanes([dv_ref[r, spot], empty])


def qkv_weight_kernel(done_ref, x_ref, out):
    dq_ref, dk_ref, dv_ref = (done_ref.at[t] for t in range(3))
    width = x_ref.shape[1]
    rows = lambda ref: jnp.concatenate([ref[0], ref[1]], axis=0)
    both = [lanes([rows(dq_ref), rows(dk_ref)]), rows(dv_ref)]
    for t in range(2):
        grads = (dot_tn(both[t], x_ref[...]) * width**-0.5).astype(BF16)
        for i in range(2 - t):
            for j in range(8):
                out[16 * t + 8 * i + j] = grads[64 * i : 64 * i + 64, 128 * j : 128 * j + 128]


MIRROR = (0, 2, 1, 4, 3, 6, 5, 7)


def back_qkv_kernel(own_y, mate_y, own_w, mate_w, *refs):
    outs, w = refs[:9], refs[9]
    width = w.shape[1]
    for h, weight in enumerate((own_w, mate_w)):
        for j in range(8):
            spot = slice(128 * j, 128 * j + 128)
            for t in range(3):
                w[256 * h + 64 * t : 256 * h + 64 * t + 64, spot] = weight[8 * t + j]
            w[256 * h + 192 : 256 * h + 256, spot] = jnp.zeros((64, 128), BF16)
    for i, p in enumerate(MIRROR):
        rows = slice(128 * p, 128 * p + 128)
        part = (dot_nn(lanes([own_y[rows], mate_y[rows]]), w[...]) * width**-0.5).astype(BF16)
        for r in range(2):
            half = part[64 * r : 64 * r + 64]
            if i < 7:
                outs[i][r] = half
            else:
                outs[7 + r][0] = half


def back_norm_kernel(place, one, two, three, trunk, gamma, grad_res, *parts):
    sums = one[...].astype(F32) + two[...].astype(F32) + three[...].astype(F32)
    g = jnp.concatenate([sums[0], sums[1]], axis=0)
    x = trunk[...]
    scale = lax.rsqrt(jnp.mean(x * x, axis=-1, keepdims=True) + NORM_EPS)
    inner = g * (1.0 + gamma[...])
    slope = inner * scale - x * (scale * scale * scale * jnp.mean(inner * x, axis=-1, keepdims=True))
    grad_trunk = (grad_res[...] + slope).astype(BF16)
    grad_gamma = (g * (x * scale)).astype(BF16)
    both = jnp.concatenate([grad_trunk, grad_gamma], axis=0)
    quarters(both, 2 * place[1] + place[0], parts)


def input_weight_kernel(targets, *refs):
    x_refs, y_refs, m_refs, a_refs, refs = refs[:4], refs[4:8], refs[8:12], refs[12:16], refs[16:]
    outs, done = refs[:9], refs[9]
    count, width = m_refs[0].shape
    scale_in = width**-0.5
    stacked = lambda refs, cut: jnp.concatenate([ref[cut] for ref in refs], axis=0)
    trunk_grads = stacked(y_refs, slice(0, count))
    gamma_grads = stacked(y_refs, slice(count, 2 * count))
    done[0] = (dot_tn(trunk_grads, stacked(x_refs, 0)) * scale_in).astype(BF16)
    done[1] = (dot_tn(trunk_grads, stacked(x_refs, 1)) * scale_in).astype(BF16)
    done[2] = (dot_tn(gamma_grads, stacked(x_refs, 2)) * (0.5 * scale_in)).astype(BF16)
    done[3] = (dot_tn(stacked(a_refs, slice(None)), stacked(m_refs, slice(None))) * (4.0 * scale_in)).astype(BF16)
    for p in range(8):
        rows = pl.ds(pl.multiple_of(targets[p] * 32, 32), 32)
        for t in range(4):
            for j in range(8):
                value = done[t, rows, 128 * j : 128 * j + 128]
                if p < 7:
                    outs[p][8 * t + j] = value
                else:
                    outs[7 + t // 2][8 * (t % 2) + j] = value


def back_input_kernel(*refs):
    y_refs, w_refs, outs = refs[:4], refs[4:16], refs[16:]
    count, width = outs[0].shape
    scale_in = width**-0.5
    for t, out in enumerate(outs):
        rows = slice(0, count) if t < 2 else slice(count, 2 * count)
        total = dot_nn(y_refs[0][rows], w_refs[4 * t][...])
        for r in range(1, 4):
            total += dot_nn(y_refs[r][rows], w_refs[4 * t + r][...])
        out[...] = total * (scale_in if t < 2 else 0.5 * scale_in)


def adam(weight, gradient, first, second, rate):
    first = BETA_ONE * first + (1.0 - BETA_ONE) * gradient
    second = BETA_TWO * second + (1.0 - BETA_TWO) * gradient * gradient
    fix_one = 1.0 - BETA_ONE**STEP
    fix_two = 1.0 - BETA_TWO**STEP
    update = first / fix_one / (jnp.sqrt(second / fix_two) + ADAM_EPS)
    return weight - rate * (update + WEIGHT_DECAY * weight), first, second


def adam_kernel(source, held, group, in_own, in_far, rest, master, first, second, *refs, start, early):
    new_first, new_second, new_master, new_low = refs[-4:]
    step = pl.program_id(0)
    count = master.shape[0]
    for i in range(count):
        slot = start + step * count + i
        k = source[slot]
        live = (slot < held[0]).astype(F32)
        gradient = rest[jnp.where(k < 48, jnp.maximum(k - 24, 0), jnp.maximum(k - 32, 24))].astype(F32)
        if not early:
            k_in = jnp.where(k < 24, k, jnp.clip(k - 24, 24, 31))
            own, far = in_own[k_in].astype(F32), in_far[k_in].astype(F32)
            upper, lower = jnp.where(group[0] == 0, own, far), jnp.where(group[0] == 0, far, own)
            here = jnp.logical_or(k < 24, jnp.logical_and(k >= 48, k < 56))
            gradient = jnp.where(here, jnp.concatenate([upper, lower], axis=0), gradient)
        weight, one, two = adam(master[i], gradient, first[i], second[i], LEARN_RATE)
        weight = weight * live
        new_first[i] = one * live
        new_second[i] = two * live
        new_master[i] = weight
        new_low[i] = weight.astype(BF16)


def ring_order(chips):
    return list(range(0, chips, 2)) + list(range(chips - 1, 0, -2))


def ring_shift(x, chips, step):
    order = ring_order(chips)
    pairs = [
        (2 * order[i] + k, 2 * order[(i + step) % chips] + k) for i in range(chips) for k in range(2)
    ]
    return lax.ppermute(x, "seq", pairs)


def to_mate(x, chips):
    return lax.ppermute(x, "seq", [(i, i ^ 1) for i in range(2 * chips)])


def to_far(x):
    return lax.ppermute(x, "batch", [(0, 1), (1, 0)])


def after(x, *others):
    return lax.optimization_barrier((x, others))[0] if others else x


class RingGather:
    def __init__(self, x, chips, halves=True, cut=None):
        self.chips, self.halves = chips, halves
        self.cut = x.shape[0] // 2 if cut is None else cut
        self.pieces = [x]
        self.ahead = self.back = x
        self.left = chips // 2

    def hop(self, *gates):
        ahead, back = after((self.ahead, self.back), *gates)
        self.left -= 1
        if self.left == 0 and self.halves:
            ahead, back = ahead[: self.cut], back[self.cut :]
        self.ahead = ring_shift(ahead, self.chips, 1)
        got = [self.ahead]
        if self.left or self.halves:
            self.back = ring_shift(back, self.chips, -1)
            got.append(self.back)
        self.pieces += got
        return tuple(got)


def add_low(a, b):
    return (a.astype(F32) + b.astype(F32)).astype(BF16)


class RingSum:
    def __init__(self, parts, chips):
        self.parts, self.chips = parts, chips
        self.distance = chips // 2
        self.ahead = parts[chips - 1]
        self.back = parts[chips] if len(parts) > chips else None

    def hop(self, *gates):
        ahead, back = after((self.ahead, self.back), *gates)
        ahead = ring_shift(ahead, self.chips, 1)
        back = None if back is None else ring_shift(back, self.chips, -1)
        self.distance -= 1
        if self.distance:
            to_ahead, to_back = self.parts[2 * self.distance - 1], self.parts[2 * self.distance]
            if ahead.shape != to_ahead.shape:
                cut = ahead.shape[0]
                ahead = jnp.concatenate([add_low(ahead, to_ahead[:cut]), to_ahead[cut:]])
                back = jnp.concatenate([to_back[:cut], add_low(back, to_back[cut:])])
            else:
                ahead = add_low(ahead, to_ahead)
                back = to_back if back is None else add_low(back, to_back)
        self.ahead, self.back = ahead, back
        return ahead, back

    def terms(self):
        return self.parts[0], self.ahead, self.back


def sum_low(terms):
    return sum(term.astype(F32) for term in terms).astype(BF16)


def to_diag(x, chips):
    pairs = [(2 * i + b, 2 * (i ^ 1) + 1 - b) for i in range(2 * chips) for b in range(2)]
    return lax.ppermute(x, ("seq", "batch"), pairs)


def fast_shards(
    frames, skip_frames, time_embed, cotangent, segments, owners, master, moment_one, moment_two,
    norm_gains, ff_biases, small_first, small_second,
):
    row_count, seg_len, width = frames.shape
    width_ff = ff_biases.shape[0] - width
    count = row_count * seg_len
    capacity = master.shape[0]
    seq_count = lax.axis_size("seq")
    chips = seq_count // 2
    half_width = width // 2
    group = lax.axis_index("batch")
    here = lax.axis_index("seq")
    chip, core = here // 2, here % 2
    order = jnp.array(ring_order(chips), jnp.int32)
    position = jnp.argmax(order == chip).astype(jnp.int32)
    rel = jnp.array([0, 1, -1, 2, -2, 3, -3, 4], jnp.int32)
    places = order[(position - rel) % chips]
    targets = order[(position + rel) % chips]
    sources = jnp.stack([2 * places + core, 2 * places + 1 - core], axis=1).reshape(-1)

    def by_core(own, mate):
        return jnp.where(core == 0, jnp.stack([own, mate]), jnp.stack([mate, own]))

    def pick(x, which):
        return lax.dynamic_index_in_dim(x, which, 0, False)

    ids = jnp.arange(owners.shape[0], dtype=jnp.int32)
    slots = jnp.sum(
        ((owners[None, :] == owners[:, None]) & (ids[None, :] < ids[:, None])).astype(jnp.int32), axis=1
    )
    held = owners == group
    turned = jnp.swapaxes(master, 1, 2)
    block = turned.shape[1:]
    place = jnp.stack([group, core])
    stacks = lambda *counts: [((n,) + block, BF16) for n in counts]
    in_keep, in_send, in_give, head_own, pair_own, pair_far, pair_mate, pair_diag = kernel_call(
        pick_kernel, [((1024, block[1]), BF16)] * 2 + [((256, block[1]), BF16)] + stacks(24, 16, 16, 16, 16),
        turned, scalars=(slots, place), far_out=(3, 4, 5, 6, 7),
    )
    seg_own = jnp.zeros((16, 128), BF16).at[:row_count, :seg_len].set(segments.astype(BF16))
    (in_blocks,) = kernel_call(
        select_in_kernel, [((PIECE_ROWS, block[1]), BF16)],
        in_keep, to_far(in_send), to_mate(in_give, chips), to_diag(in_give, chips), seg_own, to_mate(seg_own, chips),
        scalars=(owners, place),
    )

    half_size = HEAD_DIM // 2
    spot = (sources[:, None] * seg_len + jnp.arange(seg_len, dtype=jnp.int32)[None, :]).reshape(-1).astype(F32)
    inverse = 10000.0 ** (-jnp.arange(half_size, dtype=jnp.int32).astype(F32) / half_size)
    phases = spot[:, None] * inverse[None, :]
    cosine, sine = jnp.cos(phases), jnp.sin(phases)
    cosine = jnp.concatenate([cosine, cosine], axis=1)
    sine = jnp.concatenate([-sine, sine], axis=1)

    def gather_four(parts):
        return [parts[0], to_far(parts[1]), to_mate(parts[2], chips), to_diag(parts[3], chips)]

    def same_four(x, far=None):
        far = to_far(x) if far is None else far
        return [x, far, to_mate(x, chips), to_mate(far, chips)]

    x_own = jnp.stack([frames.reshape(count, width), skip_frames.reshape(count, width), time_embed.reshape(count, width)])
    in_ring = RingGather(in_blocks, chips, cut=PIECE_CUT)
    in_ring.hop()
    x_far = to_far(after(x_own, in_blocks))
    second = in_ring.hop(cosine, sine)
    x_far = after(x_far, *second)
    x_four = [x_own, x_far, to_mate(x_own, chips), to_mate(x_far, chips)]
    third = in_ring.hop(x_four[3])
    pair_far, pair_mate, pair_diag = after((pair_far, pair_mate, pair_diag), x_four[3])
    (w_ff,) = kernel_call(
        select_pairs_kernel, [((2, 16) + block, BF16)],
        pair_own, to_far(pair_far), to_mate(pair_mate, chips), to_diag(pair_diag, chips), scalars=(owners, place),
    )
    (w_qkv,) = kernel_call(
        select_heads_kernel, stacks(24), head_own, to_far(after(head_own, w_ff)), scalars=(owners, place),
    )
    in_ring.hop(w_ff)
    in_pieces = in_ring.pieces

    valid = (segments < UTTS).astype(F32).reshape(count, 1)
    grad_branch = (cotangent.reshape(count, width).astype(F32) * valid).astype(BF16)

    ff_ring = RingGather(w_ff, chips, halves=False)
    ff_one = ff_ring.hop(*in_pieces[7:])
    quarter_part = ((2, count, width // 4), F32)
    *trunk_parts, seg, w_quarter = kernel_call(
        trunk_kernel, [quarter_part] * 4 + [((8, seq_count * seg_len), F32), ((3, width // 4, width), BF16)],
        *after(tuple(x_four), w_qkv), *in_pieces, scalars=(places,), flops=2 * 3 * 4 * count * width * width // 4, far_out=(5,),
    )
    trunk, gamma, normed = kernel_call(
        norm_kernel, [((count, width), F32), ((count, width), F32), ((count, width), BF16)],
        *after(tuple(gather_four(trunk_parts)), *ff_one), scalars=(place,), far_out=(0, 1),
    )

    normed_ring = RingGather(normed, chips)
    normed_ring.hop()
    (six_own,) = kernel_call(
        assemble_out_kernel, [((width, half_width), BF16)], *after(tuple(in_pieces), normed), scalars=(places, place),
    )
    six_mate = to_mate(six_own, chips)
    normed_ring.hop(six_mate)
    normed_ring.hop()
    grad_four = same_four(after(grad_branch, normed))
    w_qkv_mate = to_mate(after(w_qkv, normed), chips)
    normed_last = normed_ring.hop(w_qkv_mate, *grad_four)
    normed_pieces = normed_ring.pieces + [to_mate(piece, chips) for piece in normed_ring.pieces]

    row_len = seq_count * seg_len
    heads_out = ((3, row_count, row_len, HEAD_DIM), BF16)
    ff_two = ff_ring.hop(*normed_last)
    w_own = [w_quarter[t] for t in range(3)]

    def weight_four(t, *gates):
        return same_four(w_own[t], to_far(after(w_own[t], *gates)))

    w_fours = [weight_four(0, *normed_last)]
    qkv, mixed, normed_all = kernel_call(
        attend_kernel, [heads_out, ((seq_count, seg_len, 2 * HEAD_DIM), BF16), ((row_count * row_len, width), BF16)],
        w_qkv, cosine, sine, seg, *normed_pieces, scalars=(sources,), far_out=(0, 2),
        scratch=[pltpu.VMEM((row_count, row_len, HEAD_DIM), BF16)], flops=2 * 2 * row_len * (192 * width + 2 * row_len * 64),
    )
    heads = lax.all_to_all(after(mixed, *ff_two), "seq", 0, 0, tiled=True)
    ff_three = ff_ring.hop(mixed)
    w_fours.append(weight_four(1, mixed))
    residual, normed_two, mixed_rows = kernel_call(
        residual_kernel, [((count, width), F32), ((count, width), BF16), ((count, width), BF16)],
        after(heads, *ff_three, *w_fours[0][1:]), six_own, six_mate, trunk, norm_gains[None], scalars=(core[None],),
        flops=2 * count * width * width, far_in=(3,), far_out=(0, 2),
    )

    ff_ring.hop(heads)
    ff_pieces = ff_ring.pieces
    normed_far = to_far(normed_two)
    normed_four = [normed_two, normed_far, to_mate(normed_two, chips), to_mate(normed_far, chips)]
    pair_index = 2 * group + core
    up_bias = lax.dynamic_slice_in_dim(ff_biases, pair_index * width, width, 0)[None]
    frame_part, wide_low = ((count, width), F32), ((4 * count, width), BF16)
    ff_outs = kernel_call(
        forward_back_kernel, [frame_part] * 4 + [((count, width), BF16)] * 4 + [wide_low, wide_low, ((1, width), F32)],
        *normed_four, *grad_four, up_bias, *ff_pieces, scalars=(places,), far_in=tuple(range(17)), far_out=tuple(range(11)), room=60,
        scratch=[pltpu.VMEM((width, width), BF16)] * 2 + [pltpu.VMEM((4 * count, width), F32)],
        flops=4 * 2 * 4 * count * width * width,
    )
    hidden, grad_pre, grad_up = ff_outs[8:]

    def from_four(parts):
        own, far, mate, far_mate = parts
        far = (far + to_mate(far_mate, chips)).astype(BF16)
        return own, to_mate(mate, chips), to_far(far), far

    *grad_parts, grad_sent = from_four(ff_outs[:4])

    quarter = ((count, width // 4), BF16)
    grad_res, grad_heads, grad_gains, *att_parts = kernel_call(
        back_out_kernel,
        [((count, width), F32), ((seq_count, seg_len, 2 * HEAD_DIM), BF16), ((1, width), F32)] + [quarter] * 4,
        *grad_parts, residual, norm_gains[None], grad_branch, six_own, six_mate, scalars=(place,),
        flops=2 * count * width * width, far_in=(3,), far_out=(0, 3, 4, 5, 6),
    )
    head_grads = lax.all_to_all(grad_heads, "seq", 0, 0, tiled=True)

    hidden, grad_pre = after((hidden, grad_pre), grad_heads)
    ff_parts = kernel_call(
        ff_weight_kernel, [((2, 16) + block, BF16)] * 8, *normed_four, *grad_four, hidden, grad_pre, scalars=(targets,),
        flops=2 * 2 * 4 * count * width * width, far_in=tuple(range(10)), far_out=tuple(range(8)), room=60,
    )
    ff_sum_ring = RingSum(ff_parts, chips)
    ff_one = ff_sum_ring.hop()

    grad_down = jnp.sum(grad_branch.astype(F32), axis=0)
    up_all = lax.dynamic_update_slice_in_dim(jnp.zeros((width_ff,), F32), grad_up[0], pair_index * width, 0)
    small_grad = jnp.concatenate([grad_gains[0], up_all, grad_down]).reshape(-1, 128)

    def small_step(x, bit, *gates):
        x = after(x, *gates)
        return x + lax.ppermute(x, "seq", [(j, j ^ bit) for j in range(seq_count)])

    rows_out = ((chips * count, 256), BF16)
    qkv_grads, mate_grads, grad_qkv = kernel_call(
        attend_back_kernel, [rows_out, rows_out, heads_out], qkv, after(head_grads, ff_parts[7]), cosine, sine, seg,
        scalars=(sources,), far_in=(0,), far_out=(2,),
        scratch=[pltpu.VMEM((row_count, row_len, HEAD_DIM), BF16)] + [pltpu.VMEM((row_count, row_len, HEAD_DIM), F32)] * 3,
        flops=2 * 2 * row_len * row_len * 64 * 5,
    )
    ff_two = ff_sum_ring.hop(qkv_grads)
    w_fours.append(weight_four(2, head_grads))
    small_far = after(small_grad, head_grads)
    small_grad = small_grad + to_far(small_far)
    norm_piece = ((row_count, seg_len, width), BF16)
    norm_half = ((1, seg_len, width), BF16)
    norm_parts = kernel_call(
        back_qkv_kernel, [norm_piece] * 7 + [norm_half] * 2, qkv_grads,
        to_mate(after(mate_grads, small_grad, ff_one[0]), chips), w_qkv, w_qkv_mate,
        scratch=[pltpu.VMEM((512, width), BF16)], flops=2 * chips * count * 512 * width,
    )
    norm_ring = RingSum(norm_parts, chips)
    norm_ring.hop()
    att_four = gather_four(after(tuple(att_parts), norm_parts[0]))
    (qkv_sum,) = kernel_call(
        qkv_weight_kernel, [((24,) + block, BF16)], *after((grad_qkv, normed_all), norm_parts[0]),
        flops=2 * 2 * row_len * 192 * width, far_in=(0, 1), far_out=(0,),
    )
    second = norm_ring.hop(att_four, qkv_sum)
    mixed_four = same_four(after(mixed_rows, norm_parts[0]))
    third = norm_ring.hop(mixed_four)
    branch_four = gather_four(after(tuple(ff_outs[4:8]), mixed_four[3]))
    norm_ring.hop(ff_two[0])
    trunk_parts = kernel_call(
        back_norm_kernel, [((2 * count, width // 4), BF16)] * 4,
        *norm_ring.terms(), trunk, gamma, grad_res, scalars=(place,), far_in=(3, 4, 5),
    )
    trunk_four = gather_four(trunk_parts)
    ff_three = ff_sum_ring.hop(trunk_parts[0])
    qkv_far = to_far(after(qkv_sum, trunk_parts[0]))

    in_parts = kernel_call(
        input_weight_kernel, [((32, 32, block[1]), BF16)] * 7 + [((16, 32, block[1]), BF16)] * 2,
        *x_four, *trunk_four, *mixed_four, *att_four, scalars=(targets,), far_in=tuple(range(16)), far_out=tuple(range(9)), room=60,
        scratch=[pltpu.VMEM((4, width // 4, width), BF16)], flops=2 * 4 * 4 * count * width * width // 4,
    )
    in_sums = RingSum(in_parts, chips)
    first = in_sums.hop()
    ff_sum_ring.hop()
    ff_total = sum_low(ff_sum_ring.terms())
    second = in_sums.hop()
    ff_sum = by_core(pick(ff_total, core), to_mate(pick(ff_total, 1 - core), chips)).reshape((32,) + block)
    small_grad = small_step(small_grad, 1, *first)
    small_grad = small_step(small_grad, 2)
    third = in_sums.hop(ff_sum)
    small_grad = small_step(small_grad, 4, *third)
    small_grad = small_step(small_grad, 8)
    in_sums.hop()
    in_sum = sum_low(in_sums.terms())
    ff_far = to_far(ff_sum)
    in_far = to_far(in_sum)
    rest_grads = jnp.concatenate([add_low(qkv_sum, qkv_far), ff_sum, ff_far])

    held_count = jnp.sum(held.astype(jnp.int32))
    match = held[None, :] & (slots[None, :] == jnp.arange(capacity, dtype=jnp.int32)[:, None])
    tile, row = ids // 8 - 7, ids % 8
    pair = tile % 4
    ff_place = 56 + 32 * (pair // 2 != group).astype(jnp.int32) + 16 * (pair % 2) + 8 * (tile // 4) + row
    source = jnp.sum(jnp.where(match, jnp.where(ids < 56, ids, ff_place)[None, :], 0), axis=1)
    stack = (capacity,) + block
    states = (turned, jnp.swapaxes(moment_one, 1, 2), jnp.swapaxes(moment_two, 1, 2))
    first_slots = 60
    per_step = math.gcd(first_slots, capacity - first_slots)

    def update(grads, start, stop, done):
        state = pl.BlockSpec((per_step,) + block, lambda i, *_: (i + start // per_step, 0, 0))
        whole = [pl.BlockSpec(g.shape, lambda i, *_, n=g.ndim: (0,) * n) for g in grads]
        return pl.pallas_call(
            functools.partial(adam_kernel, start=start, early=not done),
            grid_spec=pltpu.PrefetchScalarGridSpec(
                num_scalar_prefetch=3, grid=((stop - start) // per_step,),
                in_specs=whole + [state] * 3 + [pl.BlockSpec(memory_space=pl.ANY)] * len(done), out_specs=[state] * 4,
            ),
            out_shape=[jax.ShapeDtypeStruct(stack, F32)] * 3 + [jax.ShapeDtypeStruct(stack, BF16)],
            input_output_aliases={9 + i: i for i in range(len(done))},
            compiler_params=pltpu.CompilerParams(vmem_limit_bytes=32 * MIB),
            cost_estimate=pl.CostEstimate(flops=0, bytes_accessed=(stop - start) * 8192 * 26, transcendentals=0),
        )(source, held_count[None], group[None], *grads, *states, *done)

    tiny = jnp.zeros((1, 32, block[1]), BF16)
    done = update((tiny, tiny, rest_grads), first_slots, capacity, ())
    new_first, new_second, new_master, new_low = update((in_sum, in_far, rest_grads), 0, first_slots, tuple(done))
    back = lambda a: jnp.swapaxes(a, 1, 2)

    small_grad = small_grad.reshape(-1)
    small_values = jnp.concatenate([norm_gains, ff_biases])
    small_new, small_one, small_two = adam(small_values, small_grad, small_first, small_second, SMALL_RATE)

    branch = sum(part.astype(F32) for part in branch_four)
    output = (residual + branch + ff_biases[None, width_ff:]) * valid
    output = output.astype(BF16).reshape(row_count, seg_len, width)
    inputs = kernel_call(
        back_input_kernel, [frame_part] * 3, *trunk_parts, *[w for four in w_fours for w in four],
        flops=2 * 3 * count * width * width,
    )
    inputs = [part.reshape(row_count, seg_len, width) for part in inputs]
    return (
        output, inputs[0], inputs[1], inputs[2],
        back(new_first), back(new_second), back(new_master), back(new_low),
        small_one, small_two, small_new,
    )


def slot_places(owners, group_count, capacity):
    one_hot = (owners[:, None] == jnp.arange(group_count, dtype=jnp.int32)[None, :]).astype(
        jnp.int32
    )
    before = jnp.cumsum(one_hot, axis=0) - one_hot
    slot_index = jnp.sum(before * one_hot, axis=1)
    return owners * capacity + slot_index


def rotate(tensor, offset):
    half_size = tensor.shape[-1] // 2
    position = (offset + jnp.arange(tensor.shape[1], dtype=jnp.int32)).astype(jnp.float32)
    inverse = 10000.0 ** (-jnp.arange(half_size, dtype=jnp.int32).astype(jnp.float32) / half_size)
    phases = position[:, None] * inverse[None, :]
    cosine = jnp.cos(phases)[None, :, None, :]
    sine_part = jnp.sin(phases)[None, :, None, :]
    front_half = tensor[..., :half_size]
    back_half = tensor[..., half_size:]
    return jnp.concatenate(
        [front_half * cosine - back_half * sine_part, front_half * sine_part + back_half * cosine],
        axis=-1,
    )


def adaptive_norm(trunk, gamma_map):
    return (
        trunk
        * lax.rsqrt(jnp.mean(trunk * trunk, axis=-1, keepdims=True) + NORM_EPS)
        * (1.0 + gamma_map)
    )


def root_norm(residual, norm_gains):
    return (
        residual
        * lax.rsqrt(jnp.mean(residual * residual, axis=-1, keepdims=True) + NORM_EPS)
        * norm_gains
    )


def gelu_exact(tensor):
    return jax.nn.gelu(tensor, approximate=False)


def adam_update(weight, gradient, first_moment, second_moment, step_rate):
    first_moment = BETA_ONE * first_moment + (1.0 - BETA_ONE) * gradient
    second_moment = BETA_TWO * second_moment + (1.0 - BETA_TWO) * gradient * gradient
    fix_one = 1.0 - BETA_ONE**STEP
    fix_two = 1.0 - BETA_TWO**STEP
    update = first_moment / fix_one / (jnp.sqrt(second_moment / fix_two) + ADAM_EPS)
    return (weight - step_rate * (update + WEIGHT_DECAY * weight), first_moment, second_moment)


def matmul(former, latter):
    return jnp.dot(former, latter, preferred_element_type=jnp.float32)


def contract_rows(former, latter):
    return lax.dot_general(
        former, latter, (((0,), (0,)), ((), ())), preferred_element_type=jnp.float32
    )


def contract_cols(former, latter):
    return lax.dot_general(
        former, latter, (((1,), (1,)), ((), ())), preferred_element_type=jnp.float32
    )


def score_block(queries, key_rows, same_utt):
    scores = jnp.einsum(
        "qhd,khd->hqk", queries, key_rows, preferred_element_type=jnp.float32
    ) * HEAD_DIM ** (-0.5)
    scores = jnp.where(same_utt[None], scores, MASKED_SCORE)
    row_max = jnp.max(scores, axis=-1, keepdims=True)
    exponent = jnp.exp(scores - row_max)
    total = jnp.sum(exponent, axis=-1, keepdims=True)
    return (exponent / total, row_max[..., 0], total[..., 0])


def attend(element):
    queries, key_rows, values, same_utt = element
    attn_probs, row_max, total = score_block(queries, key_rows, same_utt)
    mixed = jnp.einsum(
        "hqk,khd->qhd", attn_probs.astype(jnp.bfloat16), values, preferred_element_type=jnp.float32
    )
    return (mixed.astype(jnp.bfloat16), attn_probs, row_max, total)


def probs_only(element):
    return score_block(element[0], element[1], element[2])


def attend_query(element):
    queries, key_rows, values, attn_probs, grad_mixed = element
    prob_grad = jnp.einsum("qhd,khd->hqk", grad_mixed, values, preferred_element_type=jnp.float32)
    inner_sum = jnp.sum(attn_probs * prob_grad, axis=-1, keepdims=True)
    score_grad = (attn_probs * (prob_grad - inner_sum)).astype(jnp.bfloat16)
    query_grad = jnp.einsum(
        "hqk,khd->qhd", score_grad, key_rows, preferred_element_type=jnp.float32
    ) * HEAD_DIM ** (-0.5)
    return (query_grad, inner_sum[..., 0])


def attend_keys(element):
    query_all, grad_all, max_all, total_all, inner_all, seg_query, key_own, value_own, seg_own = (
        element
    )
    scores = jnp.einsum(
        "qhd,khd->hqk", query_all, key_own, preferred_element_type=jnp.float32
    ) * HEAD_DIM ** (-0.5)
    same_utt = seg_query[:, None] == seg_own[None, :]
    scores = jnp.where(same_utt[None], scores, MASKED_SCORE)
    attn_probs = jnp.exp(scores - max_all[..., None]) / total_all[..., None]
    prob_grad = jnp.einsum("qhd,khd->hqk", grad_all, value_own, preferred_element_type=jnp.float32)
    score_grad = (attn_probs * (prob_grad - inner_all[..., None])).astype(jnp.bfloat16)
    key_grad = jnp.einsum(
        "hqk,qhd->khd", score_grad, query_all, preferred_element_type=jnp.float32
    ) * HEAD_DIM ** (-0.5)
    value_grad = jnp.einsum(
        "hqk,qhd->khd",
        attn_probs.astype(jnp.bfloat16),
        grad_all,
        preferred_element_type=jnp.float32,
    )
    return (key_grad, value_grad)


def general_shards(
    frames,
    skip_frames,
    time_embed,
    cotangent,
    segments,
    owners,
    master,
    moment_one,
    moment_two,
    norm_gains,
    ff_biases,
    small_first,
    small_second,
):
    row_count, seg_len, model_width = frames.shape
    width_ff = ff_biases.shape[0] - model_width
    frame_count = row_count * seg_len
    group_count = lax.axis_size("batch")
    capacity = master.shape[0]
    block_rows = master.shape[1]
    scale_in = model_width ** (-0.5)
    scale_time = 0.5 * model_width ** (-0.5)
    scale_out = 4.0 * model_width ** (-0.5)
    scale_ff = width_ff ** (-0.5)
    places = slot_places(owners, group_count, capacity)
    low_master = master.astype(jnp.bfloat16)
    all_slots = lax.all_gather(low_master, "batch", axis=0, tiled=True)
    columns = jnp.take(all_slots, places, axis=0)
    tile_stack = lax.all_gather(columns, "seq", axis=2, tiled=True).reshape(15, model_width, model_width)
    up_weight = jnp.concatenate(
        [tile_stack[7], tile_stack[8], tile_stack[9], tile_stack[10]], axis=1
    )
    down_weight = tile_stack[11:15].reshape(width_ff, model_width)
    flat_frames = frames.reshape(frame_count, model_width)
    flat_skip = skip_frames.reshape(frame_count, model_width)
    flat_time = time_embed.reshape(frame_count, model_width)
    offset = lax.axis_index("seq") * seg_len

    def rotate_here(tensor):
        return rotate(tensor, offset)

    def split_heads(tensor):
        return tensor.reshape(row_count, seg_len, HEADS, HEAD_DIM)

    trunk = (matmul(flat_frames, tile_stack[0]) + matmul(flat_skip, tile_stack[1])) * scale_in
    gamma_map = matmul(flat_time, tile_stack[2]) * scale_time
    normed_f32, norm_pull = jax.vjp(adaptive_norm, trunk, gamma_map)
    normed = normed_f32.astype(jnp.bfloat16)
    query_rot, query_pull = jax.vjp(
        rotate_here, split_heads(matmul(normed, tile_stack[3]) * scale_in)
    )
    key_rot, key_pull = jax.vjp(rotate_here, split_heads(matmul(normed, tile_stack[4]) * scale_in))
    queries = query_rot.astype(jnp.bfloat16)
    key_local = key_rot.astype(jnp.bfloat16).reshape(row_count, seg_len, model_width)
    value_local = (
        (matmul(normed, tile_stack[5]) * scale_in)
        .astype(jnp.bfloat16)
        .reshape(row_count, seg_len, model_width)
    )
    seg_low = segments.astype(jnp.bfloat16)
    key_all, value_all, seg_all = (
        lax.all_gather(key_local, "seq", axis=1, tiled=True),
        lax.all_gather(value_local, "seq", axis=1, tiled=True),
        lax.all_gather(seg_low, "seq", axis=1, tiled=True),
    )
    key_total = key_all.shape[1]
    key_heads = key_all.reshape(row_count, key_total, HEADS, HEAD_DIM)
    value_heads = value_all.reshape(row_count, key_total, HEADS, HEAD_DIM)
    same_utt = seg_low[:, :, None] == seg_all[:, None, :]
    mixed_heads, probs_kept, max_kept, total_kept = lax.map(
        attend, (queries, key_heads, value_heads, same_utt)
    )
    mixed_rows = mixed_heads.reshape(frame_count, model_width)
    residual = trunk + matmul(mixed_rows, tile_stack[6]) * scale_out
    normed_two_f32, root_pull = jax.vjp(root_norm, residual, norm_gains)
    normed_two = normed_two_f32.astype(jnp.bfloat16)
    pre_act = matmul(normed_two, up_weight) * scale_in + ff_biases[:width_ff]
    activation, gelu_pull = jax.vjp(gelu_exact, pre_act)
    hidden = activation.astype(jnp.bfloat16)
    branch = matmul(hidden, down_weight) * scale_ff + ff_biases[width_ff:]
    valid_row = (segments < UTTS).astype(jnp.float32).reshape(frame_count, 1)
    output = (
        ((residual + branch) * valid_row)
        .astype(jnp.bfloat16)
        .reshape(row_count, seg_len, model_width)
    )
    grad_out = cotangent.reshape(frame_count, model_width).astype(jnp.float32) * valid_row
    grad_branch = grad_out.astype(jnp.bfloat16)
    grad_down_bias = jnp.sum(grad_branch.astype(jnp.float32), axis=0)
    down_grads = contract_rows(hidden, grad_branch) * scale_ff
    grad_hidden = contract_cols(grad_branch, down_weight) * scale_ff
    grad_pre = gelu_pull(grad_hidden)[0].astype(jnp.bfloat16)
    grad_up_bias = jnp.sum(grad_pre.astype(jnp.float32), axis=0)
    up_grads = contract_rows(normed_two, grad_pre) * scale_in
    grad_normed_two = contract_cols(grad_pre, up_weight) * scale_in
    grad_residual_norm, grad_gains = root_pull(grad_normed_two)
    grad_residual = grad_out + grad_residual_norm
    grad_attention = grad_residual.astype(jnp.bfloat16)
    out_grads = contract_rows(mixed_rows, grad_attention) * scale_out
    grad_mixed = (contract_cols(grad_attention, tile_stack[6]) * scale_out).astype(jnp.bfloat16)
    grad_mixed = grad_mixed.reshape(row_count, seg_len, HEADS, HEAD_DIM)
    key_again, value_again, seg_again = (
        lax.all_gather(key_local, "seq", axis=1, tiled=True),
        lax.all_gather(value_local, "seq", axis=1, tiled=True),
        lax.all_gather(seg_low, "seq", axis=1, tiled=True),
    )
    back_keys = key_again.reshape(row_count, key_total, HEADS, HEAD_DIM)
    back_values = value_again.reshape(row_count, key_total, HEADS, HEAD_DIM)
    same_again = seg_low[:, :, None] == seg_again[:, None, :]
    back_probs, back_max, back_total = lax.map(probs_only, (queries, back_keys, same_again))
    query_raw, inner_sum = lax.map(
        attend_query, (queries, back_keys, back_values, back_probs, grad_mixed)
    )
    query_all, grad_all = (
        lax.all_gather(queries, "seq", axis=1, tiled=True),
        lax.all_gather(grad_mixed, "seq", axis=1, tiled=True),
    )
    max_all, total_all, inner_all = (
        lax.all_gather(back_max, "seq", axis=2, tiled=True),
        lax.all_gather(back_total, "seq", axis=2, tiled=True),
        lax.all_gather(inner_sum, "seq", axis=2, tiled=True),
    )
    key_own = key_local.reshape(row_count, seg_len, HEADS, HEAD_DIM)
    value_own = value_local.reshape(row_count, seg_len, HEADS, HEAD_DIM)
    key_sum, value_sum = lax.map(
        attend_keys,
        (
            query_all,
            grad_all,
            max_all,
            total_all,
            inner_all,
            seg_again,
            key_own,
            value_own,
            seg_low,
        ),
    )
    grad_q = query_pull(query_raw)[0].reshape(frame_count, model_width).astype(jnp.bfloat16)
    grad_k = key_pull(key_sum)[0].reshape(frame_count, model_width).astype(jnp.bfloat16)
    grad_v = value_sum.reshape(frame_count, model_width).astype(jnp.bfloat16)
    query_grads = contract_rows(normed, grad_q) * scale_in
    key_grads = contract_rows(normed, grad_k) * scale_in
    value_grads = contract_rows(normed, grad_v) * scale_in
    grad_normed = (
        contract_cols(grad_q, tile_stack[3])
        + contract_cols(grad_k, tile_stack[4])
        + contract_cols(grad_v, tile_stack[5])
    ) * scale_in
    grad_trunk_norm, grad_gamma_f32 = norm_pull(grad_normed)
    grad_trunk = (grad_residual + grad_trunk_norm).astype(jnp.bfloat16)
    grad_gamma = grad_gamma_f32.astype(jnp.bfloat16)
    frame_grads = contract_rows(flat_frames, grad_trunk) * scale_in
    skip_grads = contract_rows(flat_skip, grad_trunk) * scale_in
    time_grads = contract_rows(flat_time, grad_gamma) * scale_time
    grad_frames = (contract_cols(grad_trunk, tile_stack[0]) * scale_in).reshape(
        row_count, seg_len, model_width
    )
    grad_skip = (contract_cols(grad_trunk, tile_stack[1]) * scale_in).reshape(
        row_count, seg_len, model_width
    )
    grad_time = (contract_cols(grad_gamma, tile_stack[2]) * scale_time).reshape(
        row_count, seg_len, model_width
    )
    first_tiles = jnp.stack(
        [frame_grads, skip_grads, time_grads, query_grads, key_grads, value_grads, out_grads]
    )
    up_tiles = up_grads.reshape(model_width, 4, model_width).transpose(1, 0, 2)
    down_tiles = down_grads.reshape(4, model_width, model_width)
    blocks = jnp.concatenate([first_tiles, up_tiles, down_tiles], axis=0).reshape(
        -1, block_rows, model_width
    )
    block_count = blocks.shape[0]
    partial_cols = lax.psum_scatter(
        blocks.astype(jnp.bfloat16), "seq", scatter_dimension=2, tiled=True
    )
    matches = places[None, :] == jnp.arange(group_count * capacity, dtype=jnp.int32)[:, None]
    source = jnp.sum(
        jnp.where(matches, jnp.arange(block_count, dtype=jnp.int32)[None, :], 0), axis=1
    )
    filled = jnp.any(matches, axis=1)
    placed = jnp.where(filled[:, None, None], jnp.take(partial_cols, source, axis=0), 0)
    reduced = lax.psum_scatter(placed, "batch", scatter_dimension=0, tiled=True).astype(
        jnp.float32
    )
    small_grad = jnp.concatenate([grad_gains, grad_up_bias, grad_down_bias])
    small_grad = lax.psum(small_grad, ("seq", "batch"))
    owner_index = lax.axis_index("batch")
    held_count = jnp.sum((owners == owner_index).astype(jnp.int32))
    live_slot = (jnp.arange(capacity, dtype=jnp.int32) < held_count).astype(jnp.float32)[
        :, None, None
    ]
    new_master, new_first, new_second = adam_update(
        master, reduced, moment_one, moment_two, LEARN_RATE
    )
    new_master = new_master * live_slot
    new_first = new_first * live_slot
    new_second = new_second * live_slot
    small_values = jnp.concatenate([norm_gains, ff_biases])
    small_new, small_first_new, small_second_new = adam_update(
        small_values, small_grad, small_first, small_second, SMALL_RATE
    )
    return (
        output,
        grad_frames,
        grad_skip,
        grad_time,
        new_first,
        new_second,
        new_master,
        new_master.astype(jnp.bfloat16),
        small_first_new,
        small_second_new,
        small_new,
    )


def solution(mesh):
    fast = mesh.shape["seq"] == HEADS and mesh.shape["batch"] == 2
    rows, slots, whole = P("batch", "seq", None), P("batch", None, "seq"), P()
    return jax.shard_map(
        fast_shards if fast else general_shards,
        mesh=mesh,
        in_specs=(rows, rows, rows, rows, P("batch", "seq"), whole, slots, slots, slots, whole, whole, whole, whole),
        out_specs=(rows, rows, rows, rows, slots, slots, slots, slots, whole, whole, whole),
        check_vma=False,
    )
```

```python
import functools
import math

import jax
import jax.numpy as jnp
from jax import lax
from jax.experimental import pallas as pl
from jax.experimental.pallas import tpu as pltpu
from jax.sharding import PartitionSpec as P

HEADS = 16
HEAD_DIM = 64
UTTS = 8
STEP = 10
NORM_EPS = 1e-06
MASKED_SCORE = -1e30
BETA_ONE = 0.9
BETA_TWO = 0.999
ADAM_EPS = 1e-08
WEIGHT_DECAY = 0.01
LEARN_RATE = 1.0
SMALL_RATE = 0.1

F32 = jnp.float32
BF16 = jnp.bfloat16
MIB = 1 << 20


def padded(shape, dtype):
    size = jnp.dtype(dtype).itemsize
    rows = 32 // size
    shape = (1,) * (2 - len(shape)) + tuple(shape)
    return math.prod(shape[:-2]) * (-(-shape[-2] // rows) * rows) * (-(-shape[-1] // 128) * 128) * size


def kernel_call(body, outs, *args, scalars=(), scratch=(), room=10, flops=0, far_in=(), far_out=(), lazy=False):
    n_in, n_out = len(args), len(outs)
    vmem, hbm = pl.BlockSpec(memory_space=pltpu.VMEM), pl.BlockSpec(memory_space=pltpu.HBM)
    specs = [pl.BlockSpec(memory_space=pltpu.SMEM) for _ in scalars]
    specs += [hbm if i in far_in else vmem for i in range(n_in)]
    moved = sum(padded(a.shape, a.dtype) for a in args) + sum(padded(s, d) for s, d in outs)
    held = moved + sum(padded(ref.shape, ref.dtype) for ref in scratch)
    far = [pltpu.VMEM(args[i].shape, args[i].dtype) for i in far_in] + [pltpu.VMEM(*outs[i]) for i in far_out]
    copies = [pltpu.SemaphoreType.DMA((len(far),))] if far else []

    def whole(*refs):
        refs = list(refs)
        first = len(scalars)
        if far:
            sems = refs.pop()
            held_refs = refs[len(refs) - len(far) :]
            refs = refs[: len(refs) - len(far)]
            pairs = []
            for n, i in enumerate(far_in):
                pairs.append(pltpu.make_async_copy(refs[first + i], held_refs[n], sems.at[n]))
                refs[first + i] = held_refs[n]
            results = []
            for n, i in enumerate(far_out, len(far_in)):
                results.append(pltpu.make_async_copy(held_refs[n], refs[first + n_in + i], sems.at[n]))
                refs[first + n_in + i] = held_refs[n]
            for copy in pairs:
                copy.start()
            if not lazy:
                for copy in pairs:
                    copy.wait()
        if lazy:
            body(*refs, wait=lambda i: pairs[far_in.index(i)].wait())
        else:
            body(*refs)
        if far:
            for copy in results:
                copy.start()
            for copy in results:
                copy.wait()

    return pl.pallas_call(
        whole,
        out_shape=[jax.ShapeDtypeStruct(shape, dtype) for shape, dtype in outs],
        in_specs=specs,
        out_specs=[hbm if i in far_out else vmem for i in range(n_out)],
        scratch_shapes=list(scratch) + far + copies,
        compiler_params=pltpu.CompilerParams(vmem_limit_bytes=min(held + room * MIB, 58 * MIB)),
        cost_estimate=pl.CostEstimate(flops=int(flops), bytes_accessed=int(moved), transcendentals=0),
    )(*scalars, *args)


def dot_nn(a, b):
    return jnp.dot(a, b, preferred_element_type=F32)


def dot_nt(a, b):
    return lax.dot_general(a, b, (((1,), (1,)), ((), ())), preferred_element_type=F32)


def dot_tn(a, b):
    return lax.dot_general(a, b, (((0,), (0,)), ((), ())), preferred_element_type=F32)


def lanes(blocks):
    return jnp.concatenate(blocks, axis=-1)


def at128(index):
    return pl.multiple_of(index * 128, 128)


def normal_cdf(x):
    return 0.5 * (1.0 + lax.erf(x * (2.0**-0.5)))


OUT_ROWS, SEG_ROWS, PIECE_ROWS, PIECE_CUT = 768, 1280, 1312, 640


def pick_kernel(slots, place, master, keep, far_send, give, heads, pair_own, pair_far, pair_mate, pair_diag):
    group, core = place[0], place[1]

    def low(k):
        return master[slots[k]].astype(BF16)

    def tile_pair(pair, j):
        return low((7 + pair) * 8 + j), low((11 + pair) * 8 + j)

    mine = pl.ds(pl.multiple_of(32 * group, 32), 32)
    other = pl.ds(pl.multiple_of(32 - 32 * group, 32), 32)
    for k in range(24):
        keep[32 * k : 32 * k + 32] = master[slots[k], mine].astype(BF16)
        far_send[32 * k : 32 * k + 32] = master[slots[k], other].astype(BF16)
    for j in range(4):
        rows = slice(OUT_ROWS + 64 * j, OUT_ROWS + 64 * j + 64)
        block = low(48 + 4 * core + j)
        keep[rows] = block
        far_send[rows] = block
        give[64 * j : 64 * j + 64] = low(52 - 4 * core + j)
    for k in range(24):
        heads[k] = low(24 + k)
    for j in range(8):
        pair_far[j], pair_far[8 + j] = tile_pair(2 - 2 * group + core, j)
        pair_own[j], pair_own[8 + j] = tile_pair(2 * group + core, j)
        pair_mate[j], pair_mate[8 + j] = tile_pair(2 * group + 1 - core, j)
        pair_diag[j], pair_diag[8 + j] = tile_pair(3 - 2 * group - core, j)


def select_in_kernel(held, place, own, far, mate, diag, seg_own, seg_mate, out):
    group, core = place[0], place[1]
    for k in range(24):
        rows = slice(32 * k, 32 * k + 32)
        out[rows] = jnp.where(held[k] == group, own[rows], far[rows])
    for j in range(4):
        mine = held[48 + 4 * core + j] == group
        rows, part = slice(OUT_ROWS + 64 * j, OUT_ROWS + 64 * j + 64), slice(64 * j, 64 * j + 64)
        out[rows] = jnp.where(mine, own[rows], far[rows])
        out[OUT_ROWS + 256 + 64 * j : OUT_ROWS + 320 + 64 * j] = jnp.where(mine, mate[part], diag[part])
    out[SEG_ROWS : SEG_ROWS + 16] = seg_own[...]
    out[SEG_ROWS + 16 : SEG_ROWS + 32] = seg_mate[...]


def select_heads_kernel(held, place, own, far, out):
    for k in range(24):
        out[k] = jnp.where(held[24 + k] == place[0], own[k], far[k])


def select_pairs_kernel(held, place, own, far, mate, diag, out):
    group, core = place[0], place[1]
    for half, first in ((0, 7), (1, 11)):
        for j in range(8):
            k = 8 * half + j
            mine = held[(first + 2 * group + core) * 8 + j] == group
            out[core, k] = jnp.where(mine, own[k], far[k])
            out[1 - core, k] = jnp.where(mine, mate[k], diag[k])


def ring_readers(refs):
    def last(first, count):
        if first < PIECE_CUT:
            return refs[7][first : first + count, :]
        return refs[8][first - PIECE_CUT : first - PIECE_CUT + count, :]

    return [lambda first, count, r=r: r[first : first + count, :] for r in refs[:7]] + [last]


def ring_blocks(refs):
    return [lambda s, k, r=r: r[s, k] for r in refs]


def trunk_kernel(places, own_x, far_x, mate_x, diag_x, *refs):
    pieces, outs, seg_out, weight = ring_readers(refs[:9]), refs[9:13], refs[13], refs[14:]
    width = own_x.shape[-1]
    count = own_x.shape[1]
    scale_in = width**-0.5
    for p, piece in enumerate(pieces):
        rows = pl.ds(pl.multiple_of(32 * places[p], 32), 32)
        for t in range(3):
            for j in range(8):
                weight[t][rows, 128 * j : 128 * j + 128] = piece(256 * t + 32 * j, 32)
        ids = [piece(SEG_ROWS + 16 * m, 16).astype(F32)[0:8, 0:64] for m in range(2)]
        seg_out[:, 128 * p : 128 * p + 128] = lanes(ids)
    x = [jnp.concatenate([ref[t] for ref in (own_x, far_x, mate_x, diag_x)], axis=0) for t in range(3)]
    trunk = (dot_nt(x[0], weight[0][...]) + dot_nt(x[1], weight[1][...])) * scale_in
    gamma = dot_nt(x[2], weight[2][...]) * (0.5 * scale_in)
    for i, out in enumerate(outs):
        out[0] = trunk[i * count : i * count + count]
        out[1] = gamma[i * count : i * count + count]


def assemble_out_kernel(places, place, *refs):
    out = refs[9]
    core = place[1]
    for p, piece in enumerate(ring_readers(refs[:9])):
        for m in range(2):
            column = 64 * core if m == 0 else 64 - 64 * core
            rows = pl.ds(pl.multiple_of(places[p] * 128 + column, 64), 64)
            for j in range(4):
                out[rows, 128 * j : 128 * j + 128] = piece(OUT_ROWS + 256 * m + 64 * j, 64)


def by_quarter(parts, mine):
    found = []
    for q in range(4):
        low = jnp.where(mine == 0, parts[q], parts[q ^ 1])
        high = jnp.where(mine == 2, parts[q ^ 2], parts[q ^ 3])
        found.append(jnp.where(mine < 2, low, high))
    return found


def norm_kernel(place, own, far, mate, diag, trunk_out, gamma_out, normed_out):
    mine = 2 * place[1] + place[0]
    for i, out in enumerate((trunk_out, gamma_out)):
        parts = by_quarter([ref[i] for ref in (own, far, mate, diag)], mine)
        for c in range(8):
            out[:, 128 * c : 128 * c + 128] = lanes([part[:, 32 * c : 32 * c + 32] for part in parts])
    trunk = trunk_out[...]
    scale = lax.rsqrt(jnp.mean(trunk * trunk, axis=-1, keepdims=True) + NORM_EPS)
    normed_out[...] = (trunk * scale * (1.0 + gamma_out[...])).astype(BF16)


def swap_halves(x):
    half = HEAD_DIM // 2
    return jnp.concatenate([x[:, half:], x[:, :half]], axis=1)


def frame_rows(refs, p, m):
    base = 9 * m
    if p < 7:
        return refs[base + p][...]
    return jnp.concatenate([refs[base + 7][...], refs[base + 8][...]], axis=0)


def attend_kernel(sources, weight, cosine, sine, seg, *refs):
    normed = refs[:18]
    qkv_ref, out_ref, x_ref, mixed = refs[18:]
    q_ref, k_ref, v_ref = (qkv_ref.at[t] for t in range(3))
    width = normed[0].shape[1]
    scale_in = width**-0.5
    w = jnp.concatenate(
        [lanes([weight[8 * t + j] for j in range(8)]) for t in range(3)], axis=0
    )
    row_len = q_ref.shape[1]
    for p in range(8):
        for m in range(2):
            u = 2 * p + m
            spot = pl.ds(u * 64, 64)
            rows = frame_rows(normed, p, m)
            for r in range(2):
                x_ref[pl.ds(r * row_len + u * 64, 64)] = rows[64 * r : 64 * r + 64]
            qkv = dot_nt(rows, w) * scale_in
            c, s = cosine[spot], sine[spot]
            for r in range(2):
                part = qkv[64 * r : 64 * r + 64]
                for ref, lo, scale in ((q_ref, 0, HEAD_DIM**-0.5), (k_ref, 64, 1.0)):
                    x = part[:, lo : lo + 64]
                    ref[r, spot] = ((x * c + swap_halves(x) * s) * scale).astype(BF16)
                v_ref[r, spot] = part[:, 128:192].astype(BF16)
    block = 256
    seg_cols = jnp.transpose(seg[...])
    for r in range(2):
        key, value = k_ref[r], v_ref[r]
        seg_keys = seg[r : r + 1, :]
        for q in range(row_len // block):
            spot = pl.ds(q * block, block)
            scores = dot_nt(q_ref[r, spot], key)
            same = seg_cols[q * block : q * block + block, r : r + 1] == seg_keys
            scores = jnp.where(same, scores, MASKED_SCORE)
            top = jnp.max(scores, axis=-1, keepdims=True)
            exponent = jnp.exp(scores - top)
            total = jnp.sum(exponent, axis=-1, keepdims=True)
            probs = (exponent * (1.0 / total)).astype(BF16)
            mixed[r, spot] = dot_nn(probs, value).astype(BF16)
    for u in range(16):
        spot = pl.ds(u * 64, 64)
        out_ref[sources[u]] = lanes([mixed[0, spot], mixed[1, spot]])


def residual_kernel(core, heads, w_own, w_mate, trunk, gains, res_out, normed_out, mixed_out):
    scale_out = 4.0 * trunk.shape[1] ** -0.5
    for r in range(2):
        for j in range(8):
            pair = [heads[2 * j + i][:, 64 * r : 64 * r + 64] for i in range(2)]
            mixed_out[64 * r : 64 * r + 64, 128 * j : 128 * j + 128] = lanes(pair)
    here = pl.ds(pl.multiple_of(core[0] * 512, 512), 512)
    there = pl.ds(pl.multiple_of(512 - core[0] * 512, 512), 512)
    attention = dot_nt(mixed_out[:, here], w_own[...]) + dot_nt(mixed_out[:, there], w_mate[...])
    residual = trunk[...] + attention * scale_out
    res_out[...] = residual
    scale = lax.rsqrt(jnp.mean(residual * residual, axis=-1, keepdims=True) + NORM_EPS)
    normed_out[...] = (residual * scale * gains[...]).astype(BF16)


def forward_back_kernel(places, *refs, wait):
    normed, grad, bias, pieces, refs = refs[:4], refs[4:8], refs[8], ring_blocks(refs[9:17]), refs[17:]
    grad_in, branch, (hidden_out, pre_out, bias_out, w_up, w_down, branch_acc) = refs[:4], refs[4:8], refs[8:]
    width = w_up.shape[1]
    count = normed[0].shape[0]
    scale_in = width**-0.5
    scale_ff = (4 * width) ** -0.5
    for p, piece in enumerate(pieces):
        wait(9 + p)
        for s in range(2):
            rows = pl.ds(pl.multiple_of(places[p] * 128 + 64 * s, 64), 64)
            for j in range(8):
                w_up[rows, 128 * j : 128 * j + 128] = piece(s, j)
                w_down[rows, 128 * j : 128 * j + 128] = piece(s, 8 + j)
    for i in range(9):
        wait(i)
    x = jnp.concatenate([ref[...] for ref in normed], axis=0)
    g = jnp.concatenate([ref[...] for ref in grad], axis=0)
    block = 256
    for h in range(width // block):
        spot = slice(h * block, h * block + block)
        pre = dot_nt(x, w_up[spot, :]) * scale_in + bias[:, spot]
        cdf = normal_cdf(pre)
        hidden = (pre * cdf).astype(BF16)
        slope = cdf + pre * (jnp.exp(-0.5 * pre * pre) * (2.0 * math.pi) ** -0.5)
        grad_pre = slope * (dot_nn(g, w_down[:, spot]) * scale_ff)
        grad_pre = grad_pre.astype(BF16)
        hidden_out[:, spot] = hidden
        pre_out[:, spot] = grad_pre
        bias_out[:, spot] = jnp.sum(grad_pre.astype(F32), axis=0, keepdims=True)
        grad_part = dot_nn(grad_pre, w_up[spot, :]) * scale_in
        out_part = dot_nt(hidden, w_down[:, spot]) * scale_ff
        for i in range(4):
            rows = slice(i * count, i * count + count)
            if h == 0:
                grad_in[i][...] = grad_part[rows]
            else:
                grad_in[i][...] += grad_part[rows]
        if h == 0:
            branch_acc[...] = out_part
        else:
            branch_acc[...] += out_part
    for i in range(4):
        branch[i][...] = branch_acc[i * count : i * count + count, :].astype(BF16)


def ff_weight_kernel(targets, *refs):
    normed, grad, (hidden, pre), outs = refs[:4], refs[4:8], refs[8:10], refs[10:]
    width = hidden.shape[1]
    scale_in = width**-0.5
    scale_ff = (4 * width) ** -0.5
    x = jnp.concatenate([ref[...] for ref in normed], axis=0)
    for p in range(8):
        spot = pl.ds(at128(targets[p]), 128)
        g = jnp.concatenate([ref[:, spot] for ref in grad], axis=0)
        up = (dot_tn(pre[:, spot], x) * scale_in).astype(BF16)
        down = (dot_tn(g, hidden[...]) * scale_ff).astype(BF16)
        for s in range(2):
            rows = slice(64 * s, 64 * s + 64)
            for j in range(8):
                outs[p][s, j] = up[rows, 128 * j : 128 * j + 128]
                outs[p][s, 8 + j] = down[rows, 128 * j : 128 * j + 128]


def quarters(x, mine, outs):
    parts = [lanes([x[:, 128 * c + 32 * q : 128 * c + 32 * q + 32] for c in range(x.shape[1] // 128)]) for q in range(4)]
    for out, part in zip(outs, by_quarter(parts, mine)):
        out[...] = part


def back_out_kernel(place, grad_own, grad_mate, grad_far, residual, gains, grad_out, w_own, w_mate, grad_res, heads, gain_out, *att):
    width = residual.shape[1]
    g = grad_own[...] + grad_mate[...] + grad_far[...].astype(F32)
    x = residual[...]
    scale = lax.rsqrt(jnp.mean(x * x, axis=-1, keepdims=True) + NORM_EPS)
    gain_out[...] = jnp.sum(g * x * scale, axis=0, keepdims=True)
    inner = g * gains[...]
    slope = inner * scale - x * (scale * scale * scale * jnp.mean(inner * x, axis=-1, keepdims=True))
    total = grad_out[...].astype(F32) + slope
    grad_res[...] = total
    low = total.astype(BF16)
    quarters(low, 2 * place[1] + place[0], att)
    halves = [dot_nn(low, w[...]) * (4.0 * width**-0.5) for w in (w_own, w_mate)]
    mixed = jnp.where(place[1] == 0, lanes(halves), lanes(halves[::-1])).astype(BF16)
    for j in range(8):
        rows = [mixed[64 * r : 64 * r + 64, 128 * j : 128 * j + 128] for r in range(2)]
        heads[2 * j] = lanes([rows[0][:, :64], rows[1][:, :64]])
        heads[2 * j + 1] = lanes([rows[0][:, 64:], rows[1][:, 64:]])


def attend_back_kernel(sources, qkv_ref, grads, cosine, sine, seg, own_out, mate_out, done_ref, g_ref, acc_q, acc_k, acc_v):
    q_ref, k_ref, v_ref = (qkv_ref.at[t] for t in range(3))
    dq_ref, dk_ref, dv_ref = (done_ref.at[t] for t in range(3))
    row_len = q_ref.shape[1]
    for u in range(16):
        spot = pl.ds(u * 64, 64)
        both = grads[sources[u]]
        g_ref[0, spot] = both[:, :64]
        g_ref[1, spot] = both[:, 64:]
    block = 256
    seg_cols = jnp.transpose(seg[...])
    for r in range(2):
        key, value = k_ref[r], v_ref[r]
        for q in range(row_len // block):
            spot = pl.ds(q * block, block)
            query, grad = q_ref[r, spot], g_ref[r, spot]
            scores = dot_nt(key, query)
            same = seg_cols[:, r : r + 1] == seg[r : r + 1, q * block : q * block + block]
            scores = jnp.where(same, scores, MASKED_SCORE)
            top = jnp.max(scores, axis=0, keepdims=True)
            exponent = jnp.exp(scores - top)
            total = jnp.sum(exponent, axis=0, keepdims=True)
            probs = exponent * (1.0 / total)
            prob_grad = dot_nt(value, grad)
            inner = jnp.sum(probs * prob_grad, axis=0, keepdims=True)
            score_grad = (probs * (prob_grad - inner)).astype(BF16)
            acc_q[r, spot] = dot_tn(score_grad, key)
            key_part = dot_nn(score_grad, query)
            value_part = dot_nn(probs.astype(BF16), grad)
            if q == 0:
                acc_k[r] = key_part
                acc_v[r] = value_part
            else:
                acc_k[r] += key_part
                acc_v[r] += value_part
        c, s = cosine[...], sine[...]
        for ref, acc, scale in ((dq_ref, acc_q, HEAD_DIM**-0.5), (dk_ref, acc_k, 1.0)):
            g = acc[r] * scale
            ref[r] = (g * c + swap_halves(g * s)).astype(BF16)
        dv_ref[r] = acc_v[r].astype(BF16)
    empty = jnp.zeros((64, HEAD_DIM), BF16)
    for p in range(8):
        for m, out in enumerate((own_out, mate_out)):
            spot = pl.ds((2 * p + m) * 64, 64)
            for r in range(2):
                rows = pl.ds(128 * p + 64 * r, 64)
                out[rows, 0:128] = lanes([dq_ref[r, spot], dk_ref[r, spot]])
                out[rows, 128:256] = lanes([dv_ref[r, spot], empty])


def qkv_weight_kernel(done_ref, x_ref, out):
    dq_ref, dk_ref, dv_ref = (done_ref.at[t] for t in range(3))
    width = x_ref.shape[1]
    rows = lambda ref: jnp.concatenate([ref[0], ref[1]], axis=0)
    both = [lanes([rows(dq_ref), rows(dk_ref)]), rows(dv_ref)]
    for t in range(2):
        grads = (dot_tn(both[t], x_ref[...]) * width**-0.5).astype(BF16)
        for i in range(2 - t):
            for j in range(8):
                out[16 * t + 8 * i + j] = grads[64 * i : 64 * i + 64, 128 * j : 128 * j + 128]


MIRROR = (0, 2, 1, 4, 3, 6, 5, 7)


def back_qkv_kernel(own_y, mate_y, own_w, mate_w, *refs):
    outs, w = refs[:9], refs[9]
    width = w.shape[1]
    for h, weight in enumerate((own_w, mate_w)):
        for j in range(8):
            spot = slice(128 * j, 128 * j + 128)
            for t in range(3):
                w[256 * h + 64 * t : 256 * h + 64 * t + 64, spot] = weight[8 * t + j]
            w[256 * h + 192 : 256 * h + 256, spot] = jnp.zeros((64, 128), BF16)
    for i, p in enumerate(MIRROR):
        rows = slice(128 * p, 128 * p + 128)
        part = (dot_nn(lanes([own_y[rows], mate_y[rows]]), w[...]) * width**-0.5).astype(BF16)
        for r in range(2):
            half = part[64 * r : 64 * r + 64]
            if i < 7:
                outs[i][r] = half
            else:
                outs[7 + r][0] = half


def back_norm_kernel(place, one, two, three, trunk, gamma, grad_res, *parts):
    sums = one[...].astype(F32) + two[...].astype(F32) + three[...].astype(F32)
    g = jnp.concatenate([sums[0], sums[1]], axis=0)
    x = trunk[...]
    scale = lax.rsqrt(jnp.mean(x * x, axis=-1, keepdims=True) + NORM_EPS)
    inner = g * (1.0 + gamma[...])
    slope = inner * scale - x * (scale * scale * scale * jnp.mean(inner * x, axis=-1, keepdims=True))
    grad_trunk = (grad_res[...] + slope).astype(BF16)
    grad_gamma = (g * (x * scale)).astype(BF16)
    both = jnp.concatenate([grad_trunk, grad_gamma], axis=0)
    quarters(both, 2 * place[1] + place[0], parts)


def input_weight_kernel(targets, *refs, wait):
    x_refs, y_refs, m_refs, a_refs, refs = refs[:4], refs[4:8], refs[8:12], refs[12:16], refs[16:]
    outs, done = refs[:8], refs[8]
    count, width = m_refs[0].shape
    scale_in = width**-0.5
    stacked = lambda refs, cut: jnp.concatenate([ref[cut] for ref in refs], axis=0)
    for i in range(8, 16):
        wait(i)
    done[3] = (dot_tn(stacked(a_refs, slice(None)), stacked(m_refs, slice(None))) * (4.0 * scale_in)).astype(BF16)
    for i in range(8):
        wait(i)
    trunk_grads = stacked(y_refs, slice(0, count))
    gamma_grads = stacked(y_refs, slice(count, 2 * count))
    done[0] = (dot_tn(trunk_grads, stacked(x_refs, 0)) * scale_in).astype(BF16)
    done[1] = (dot_tn(trunk_grads, stacked(x_refs, 1)) * scale_in).astype(BF16)
    done[2] = (dot_tn(gamma_grads, stacked(x_refs, 2)) * (0.5 * scale_in)).astype(BF16)
    for p in range(8):
        rows = pl.ds(pl.multiple_of(targets[p] * 32, 32), 32)
        for t in range(4):
            for j in range(8):
                value = done[t, rows, 128 * j : 128 * j + 128]
                outs[p][8 * t + j] = value


def back_input_kernel(*refs):
    y_refs, w_refs, outs = refs[:4], refs[4:16], refs[16:]
    count, width = outs[0].shape
    scale_in = width**-0.5
    for t, out in enumerate(outs):
        rows = slice(0, count) if t < 2 else slice(count, 2 * count)
        total = dot_nn(y_refs[0][rows], w_refs[4 * t][...])
        for r in range(1, 4):
            total += dot_nn(y_refs[r][rows], w_refs[4 * t + r][...])
        out[...] = total * (scale_in if t < 2 else 0.5 * scale_in)


def adam(weight, gradient, first, second, rate):
    first = BETA_ONE * first + (1.0 - BETA_ONE) * gradient
    second = BETA_TWO * second + (1.0 - BETA_TWO) * gradient * gradient
    fix_one = 1.0 - BETA_ONE**STEP
    fix_two = 1.0 - BETA_TWO**STEP
    update = first / fix_one / (jnp.sqrt(second / fix_two) + ADAM_EPS)
    return weight - rate * (update + WEIGHT_DECAY * weight), first, second


def adam_kernel(source, held, group, in_own, in_far, rest, master, first, second, *refs, start, early):
    new_first, new_second, new_master, new_low = refs[-4:]
    step = pl.program_id(0)
    count = master.shape[0]
    for i in range(count):
        slot = start + step * count + i
        k = source[slot]
        live = (slot < held[0]).astype(F32)
        gradient = rest[jnp.where(k < 48, jnp.maximum(k - 24, 0), jnp.maximum(k - 32, 24))].astype(F32)
        if not early:
            k_in = jnp.where(k < 24, k, jnp.clip(k - 24, 24, 31))
            own, far = in_own[k_in].astype(F32), in_far[k_in].astype(F32)
            upper, lower = jnp.where(group[0] == 0, own, far), jnp.where(group[0] == 0, far, own)
            here = jnp.logical_or(k < 24, jnp.logical_and(k >= 48, k < 56))
            gradient = jnp.where(here, jnp.concatenate([upper, lower], axis=0), gradient)
        weight, one, two = adam(master[i], gradient, first[i], second[i], LEARN_RATE)
        weight = weight * live
        new_first[i] = one * live
        new_second[i] = two * live
        new_master[i] = weight
        new_low[i] = weight.astype(BF16)


def ring_order(chips):
    return list(range(0, chips, 2)) + list(range(chips - 1, 0, -2))


def ring_shift(x, chips, step):
    order = ring_order(chips)
    pairs = [
        (2 * order[i] + k, 2 * order[(i + step) % chips] + k) for i in range(chips) for k in range(2)
    ]
    return lax.ppermute(x, "seq", pairs)


def to_mate(x, chips):
    return lax.ppermute(x, "seq", [(i, i ^ 1) for i in range(2 * chips)])


def to_far(x):
    return lax.ppermute(x, "batch", [(0, 1), (1, 0)])


def after(x, *others):
    return lax.optimization_barrier((x, others))[0] if others else x


class RingGather:
    def __init__(self, x, chips, halves=True, cut=None):
        self.chips, self.halves = chips, halves
        self.cut = x.shape[0] // 2 if cut is None else cut
        self.pieces = [x]
        self.ahead = self.back = x
        self.left = chips // 2

    def hop(self, *gates):
        ahead, back = after((self.ahead, self.back), *gates)
        self.left -= 1
        if self.left == 0 and self.halves:
            ahead, back = ahead[: self.cut], back[self.cut :]
        self.ahead = ring_shift(ahead, self.chips, 1)
        got = [self.ahead]
        if self.left or self.halves:
            self.back = ring_shift(back, self.chips, -1)
            got.append(self.back)
        self.pieces += got
        return tuple(got)


def add_low(a, b):
    return (a.astype(F32) + b.astype(F32)).astype(BF16)


class RingSum:
    def __init__(self, parts, chips):
        self.parts, self.chips = parts, chips
        self.distance = chips // 2
        self.ahead = parts[chips - 1]
        self.back = parts[chips] if len(parts) > chips else None

    def hop(self, *gates):
        ahead, back = after((self.ahead, self.back), *gates)
        ahead = ring_shift(ahead, self.chips, 1)
        back = None if back is None else ring_shift(back, self.chips, -1)
        self.distance -= 1
        if self.distance:
            to_ahead, to_back = self.parts[2 * self.distance - 1], self.parts[2 * self.distance]
            if ahead.shape != to_ahead.shape:
                cut = ahead.shape[0]
                ahead = jnp.concatenate([add_low(ahead, to_ahead[:cut]), to_ahead[cut:]])
                back = jnp.concatenate([to_back[:cut], add_low(back, to_back[cut:])])
            else:
                ahead = add_low(ahead, to_ahead)
                back = to_back if back is None else add_low(back, to_back)
        self.ahead, self.back = ahead, back
        return ahead, back

    def terms(self):
        return self.parts[0], self.ahead, self.back


def sum_low(terms):
    return sum(term.astype(F32) for term in terms).astype(BF16)


def to_diag(x, chips):
    pairs = [(2 * i + b, 2 * (i ^ 1) + 1 - b) for i in range(2 * chips) for b in range(2)]
    return lax.ppermute(x, ("seq", "batch"), pairs)


PLAN = {
    "tables": (0, 1),
    "x_far": (0, 3),
    "pairs": (2, 4),
    "heads_far": (7, 9),
    "heads": (9, 11),
    "heads_mate": (9, 11),
    "out_grad_far": (8, 10),
    "out_grad": (9, 11),
    "ff_hop0": (4, 6),
    "ff_hop1": (11, 99),
    "ff_hop2": (12, 99),
    "ff_hop3": (13, 15),
    "six": (9, 10),
    "six_mate": (9, 8),
    "w_far0": (11, 13),
    "w_four0": (12, 13),
    "w_far1": (12, 99),
    "w_four1": (13, 15),
    "w_far2": (20, 99),
    "w_four2": (20, 99),
    "ff_parts": (19, 20),
    "ff_sum0": (19, 21),
    "ff_sum1": (21, 24),
    "ff_sum2": (27, 99),
    "ff_sum3": (27, 99),
    "small0": (20, 21),
    "small1": (30, 99),
    "small2": (30, 99),
    "small3": (32, 99),
    "small4": (33, 34),
    "att": (22, 23),
    "qkv_sum": (25, 23),
    "mixed_far": (22, 24),
    "mixed": (22, 24),
    "branch": (19, 21),
    "qkv_far": (27, 30),
    "inputs": (28, 31),
    "ff_total": (29, 31),
    "ff_far": (29, 32),
    "early": (29, 99),
}
ROOM = {'pick': {}, 'attend': {'room': 53}, 'residual': {}, 'back': {'room': 60}, 'attend_back': {}, 'ff': {'room': 60}, 'ff_weight': {'room': 60}, 'in_weight': {'room': 60}}


class Flow:
    def __init__(self, plan):
        self.plan = plan
        self.step, self.arrays = -1, ()
        self.ready, self.results = {}, {}

    def add(self, name, action):
        self.ready[name] = action
        if self.plan[name][0] <= self.step:
            self.run(name)

    def run(self, name):
        arrays = self.arrays if self.plan[name][0] == self.step else ()
        self.results[name] = self.ready.pop(name)(lambda x: after(x, *arrays))

    def get(self, name):
        if name in self.ready:
            self.run(name)
        return self.results[name]

    def cross(self, step, *arrays):
        self.step, self.arrays = step, arrays
        for name in [n for n in self.ready if self.plan[n][0] <= step]:
            self.run(name)
        waits = [self.get(n) for n, place in self.plan.items() if place[1] == step and (n in self.ready or n in self.results)]
        if waits:
            arrays = lax.optimization_barrier((arrays, waits))[0]
        return arrays if len(arrays) > 1 else arrays[0]


def fast_shards(
    frames, skip_frames, time_embed, cotangent, segments, owners, master, moment_one, moment_two,
    norm_gains, ff_biases, small_first, small_second,
):
    row_count, seg_len, width = frames.shape
    width_ff = ff_biases.shape[0] - width
    count = row_count * seg_len
    capacity = master.shape[0]
    seq_count = lax.axis_size("seq")
    chips = seq_count // 2
    half_width = width // 2
    group = lax.axis_index("batch")
    here = lax.axis_index("seq")
    chip, core = here // 2, here % 2
    order = jnp.array(ring_order(chips), jnp.int32)
    position = jnp.argmax(order == chip).astype(jnp.int32)
    rel = jnp.array([0, 1, -1, 2, -2, 3, -3, 4], jnp.int32)
    places = order[(position - rel) % chips]
    targets = order[(position + rel) % chips]
    sources = jnp.stack([2 * places + core, 2 * places + 1 - core], axis=1).reshape(-1)
    flow = Flow(PLAN)
    add, get, cross = flow.add, flow.get, flow.cross

    def by_core(own, mate):
        return jnp.where(core == 0, jnp.stack([own, mate]), jnp.stack([mate, own]))

    def pick(x, which):
        return lax.dynamic_index_in_dim(x, which, 0, False)

    def gather_four(parts):
        return [parts[0], to_far(parts[1]), to_mate(parts[2], chips), to_diag(parts[3], chips)]

    def same_four(x, far):
        return [x, far, to_mate(x, chips), to_mate(far, chips)]

    ids = jnp.arange(owners.shape[0], dtype=jnp.int32)
    slots = jnp.sum(
        ((owners[None, :] == owners[:, None]) & (ids[None, :] < ids[:, None])).astype(jnp.int32), axis=1
    )
    held = owners == group
    turned = jnp.swapaxes(master, 1, 2)
    block = turned.shape[1:]
    place = jnp.stack([group, core])
    stacks = lambda *counts: [((n,) + block, BF16) for n in counts]
    in_keep, in_send, in_give, head_own, pair_own, pair_far, pair_mate, pair_diag = kernel_call(
        pick_kernel, [((1024, block[1]), BF16)] * 2 + [((256, block[1]), BF16)] + stacks(24, 16, 16, 16, 16),
        turned, scalars=(slots, place), far_out=(3, 4, 5, 6, 7), **ROOM["pick"],
    )
    seg_own = jnp.zeros((16, 128), BF16).at[:row_count, :seg_len].set(segments.astype(BF16))
    (in_blocks,) = kernel_call(
        select_in_kernel, [((PIECE_ROWS, block[1]), BF16)],
        in_keep, to_far(in_send), to_mate(in_give, chips), to_diag(in_give, chips), seg_own, to_mate(seg_own, chips),
        scalars=(owners, place),
    )

    half_size = HEAD_DIM // 2
    spot = (sources[:, None] * seg_len + jnp.arange(seg_len, dtype=jnp.int32)[None, :]).reshape(-1).astype(F32)
    inverse = 10000.0 ** (-jnp.arange(half_size, dtype=jnp.int32).astype(F32) / half_size)
    phases = spot[:, None] * inverse[None, :]
    cosine, sine = jnp.cos(phases), jnp.sin(phases)
    cosine = jnp.concatenate([cosine, cosine], axis=1)
    sine = jnp.concatenate([-sine, sine], axis=1)
    add("tables", lambda tie: (cosine, sine))
    x_own = jnp.stack([frames.reshape(count, width), skip_frames.reshape(count, width), time_embed.reshape(count, width)])
    valid = (segments < UTTS).astype(F32).reshape(count, 1)
    grad_branch = (cotangent.reshape(count, width).astype(F32) * valid).astype(BF16)

    add("x_far", lambda tie: to_far(tie(x_own)))

    def exchange_pairs(tie):
        far, mate, diag = tie((pair_far, pair_mate, pair_diag))
        return kernel_call(
            select_pairs_kernel, [((2, 16) + block, BF16)],
            pair_own, to_far(far), to_mate(mate, chips), to_diag(diag, chips), scalars=(owners, place),
        )[0]

    add("pairs", exchange_pairs)
    add("heads_far", lambda tie: to_far(tie(head_own)))
    add("heads", lambda tie: kernel_call(
        select_heads_kernel, stacks(24), head_own, tie(get("heads_far")), scalars=(owners, place),
    )[0])
    add("heads_mate", lambda tie: to_mate(tie(get("heads")), chips))
    add("out_grad_far", lambda tie: to_far(tie(grad_branch)))
    add("out_grad", lambda tie: same_four(grad_branch, tie(get("out_grad_far"))))

    in_ring = RingGather(cross(0, in_blocks), chips, cut=PIECE_CUT)
    in_ring.hop()
    for hop in range(1, 4):
        in_ring.ahead, in_ring.back = cross(hop, in_ring.ahead, in_ring.back)
        in_ring.pieces[2 * hop - 1 : 2 * hop + 1] = [in_ring.ahead, in_ring.back]
        in_ring.hop()
    in_pieces = in_ring.pieces
    in_pieces[7:] = cross(4, *in_pieces[7:])

    ff_ring = RingGather(get("pairs"), chips, halves=False)

    def ff_hop(tie):
        ff_ring.ahead, ff_ring.back = tie((ff_ring.ahead, ff_ring.back))
        return ff_ring.hop()

    for hop in range(4):
        add("ff_hop%d" % hop, ff_hop)

    x_far = get("x_far")
    x_four = [x_own, x_far, to_mate(x_own, chips), to_mate(x_far, chips)]
    quarter_part = ((2, count, width // 4), F32)
    *trunk_parts, seg, w_zero, w_one, w_two = kernel_call(
        trunk_kernel, [quarter_part] * 4 + [((8, seq_count * seg_len), F32)] + [((width // 4, width), BF16)] * 3,
        *x_four, *in_pieces, scalars=(places,), flops=2 * 3 * 4 * count * width * width // 4, far_out=(5, 6, 7),
    )
    for t, w in enumerate((w_zero, w_one, w_two)):
        add("w_far%d" % t, lambda tie, w=w: to_far(tie(w)))
        add("w_four%d" % t, lambda tie, w=w, t=t: same_four(w, tie(get("w_far%d" % t))))
    add("six", lambda tie: kernel_call(
        assemble_out_kernel, [((width, half_width), BF16)], *tie(tuple(in_pieces)), scalars=(places, place),
    )[0])
    add("six_mate", lambda tie: to_mate(tie(get("six")), chips))
    trunk_parts = cross(5, *trunk_parts)
    trunk, gamma, normed = kernel_call(
        norm_kernel, [((count, width), F32), ((count, width), F32), ((count, width), BF16)],
        *cross(6, *gather_four(trunk_parts)), scalars=(place,), far_out=(0, 1),
    )

    normed_ring = RingGather(cross(7, normed), chips)
    normed_ring.hop()
    for hop in range(1, 4):
        normed_ring.ahead, normed_ring.back = cross(7 + hop, normed_ring.ahead, normed_ring.back)
        normed_ring.pieces[2 * hop - 1 : 2 * hop + 1] = [normed_ring.ahead, normed_ring.back]
        normed_ring.hop()
    normed_ring.pieces[7:] = cross(11, *normed_ring.pieces[7:])
    normed_pieces = normed_ring.pieces + [to_mate(piece, chips) for piece in normed_ring.pieces]

    row_len = seq_count * seg_len
    heads_out = ((3, row_count, row_len, HEAD_DIM), BF16)
    cosine, sine = get("tables")
    w_qkv = get("heads")
    qkv, mixed, normed_all = kernel_call(
        attend_kernel, [heads_out, ((seq_count, seg_len, 2 * HEAD_DIM), BF16), ((row_count * row_len, width), BF16)],
        w_qkv, cosine, sine, seg, *normed_pieces, scalars=(sources,), far_out=(0, 2), **ROOM["attend"],
        scratch=[pltpu.VMEM((row_count, row_len, HEAD_DIM), BF16)], flops=2 * 2 * row_len * (192 * width + 2 * row_len * 64),
    )
    heads = cross(13, lax.all_to_all(cross(12, mixed), "seq", 0, 0, tiled=True))
    residual, normed_two, mixed_rows = kernel_call(
        residual_kernel, [((count, width), F32), ((count, width), BF16), ((count, width), BF16)],
        heads, get("six"), get("six_mate"), trunk, norm_gains[None], scalars=(core[None],), flops=2 * count * width * width,
        far_in=(3,), far_out=(0, 2), **ROOM["residual"],
    )
    add("mixed_far", lambda tie: to_far(tie(mixed_rows)))
    add("mixed", lambda tie: same_four(mixed_rows, tie(get("mixed_far"))))

    normed_two = cross(14, normed_two)
    normed_far = to_far(normed_two)
    normed_four = cross(15, normed_two, normed_far, to_mate(normed_two, chips), to_mate(normed_far, chips))
    pair_index = 2 * group + core
    up_bias = lax.dynamic_slice_in_dim(ff_biases, pair_index * width, width, 0)[None]
    frame_part, frame_low, wide_low = ((count, width), F32), ((count, width), BF16), ((4 * count, width), BF16)
    for hop in range(4):
        get("ff_hop%d" % hop)
    grad_four = get("out_grad")
    *ff_outs, hidden, grad_pre, grad_up = kernel_call(
        forward_back_kernel, [frame_part] * 4 + [frame_low] * 4 + [wide_low, wide_low, ((1, width), F32)],
        *normed_four, *grad_four, up_bias, *ff_ring.pieces, scalars=(places,), far_in=tuple(range(17)), far_out=tuple(range(11)),
        lazy=True, **ROOM["ff"], scratch=[pltpu.VMEM((width, width), BF16)] * 2 + [pltpu.VMEM((4 * count, width), F32)],
        flops=4 * 2 * 4 * count * width * width,
    )
    add("branch", lambda tie: gather_four(tie(tuple(ff_outs[4:]))))

    def weight_parts(tie):
        return kernel_call(
            ff_weight_kernel, [((2, 16) + block, BF16)] * 8, *normed_four, *grad_four, *tie((hidden, grad_pre)),
            scalars=(targets,), flops=2 * 2 * 4 * count * width * width, far_in=tuple(range(10)), far_out=tuple(range(8)), **ROOM["ff_weight"],
        )

    add("ff_parts", weight_parts)
    grad_own, grad_far, grad_mate, grad_diag = cross(16, *ff_outs[:4])
    grad_sent = cross(17, (grad_far + to_mate(grad_diag, chips)).astype(BF16))
    grad_parts = cross(18, grad_own, to_mate(grad_mate, chips), to_far(grad_sent))
    quarter = ((count, width // 4), BF16)
    grad_res, grad_heads, grad_gains, *att_parts = kernel_call(
        back_out_kernel,
        [((count, width), F32), ((seq_count, seg_len, 2 * HEAD_DIM), BF16), ((1, width), F32)] + [quarter] * 4,
        *grad_parts, residual, norm_gains[None], grad_branch, get("six"), get("six_mate"), scalars=(place,),
        flops=2 * count * width * width, far_in=(3,), far_out=(0, 3, 4, 5, 6), **ROOM["back"],
    )
    add("att", lambda tie: gather_four(tie(tuple(att_parts))))

    grad_down = jnp.sum(grad_branch.astype(F32), axis=0)
    up_all = lax.dynamic_update_slice_in_dim(jnp.zeros((width_ff,), F32), grad_up[0], pair_index * width, 0)
    small = [jnp.concatenate([grad_gains[0], up_all, grad_down]).reshape(-1, 128)]

    def small_step(tie, bit):
        x = tie(small[-1])
        if bit == 0:
            got = to_far(x)
        else:
            got = lax.ppermute(x, "seq", [(j, j ^ bit) for j in range(seq_count)])
        small.append(x + got)
        return small[-1]

    for n, bit in enumerate((0, 1, 2, 4, 8)):
        add("small%d" % n, lambda tie, bit=bit: small_step(tie, bit))

    grad_heads = cross(19, grad_heads)
    ff_sums = []

    def ff_sum_hop(tie):
        if not ff_sums:
            ff_sums.append(RingSum(get("ff_parts"), chips))
        ring = ff_sums[0]
        if ring.back is None:
            ring.ahead = tie(ring.ahead)
        else:
            ring.ahead, ring.back = tie((ring.ahead, ring.back))
        return ring.hop()

    for hop in range(4):
        add("ff_sum%d" % hop, ff_sum_hop)
    rows_out = ((chips * count, 256), BF16)
    head_grads = cross(20, lax.all_to_all(grad_heads, "seq", 0, 0, tiled=True))
    qkv_grads, mate_grads, grad_qkv = kernel_call(
        attend_back_kernel, [rows_out, rows_out, heads_out], qkv, head_grads, cosine, sine, seg,
        scalars=(sources,), far_in=(0,), far_out=(2,), **ROOM["attend_back"],
        scratch=[pltpu.VMEM((row_count, row_len, HEAD_DIM), BF16)] + [pltpu.VMEM((row_count, row_len, HEAD_DIM), F32)] * 3,
        flops=2 * 2 * row_len * row_len * 64 * 5,
    )
    add("qkv_sum", lambda tie: kernel_call(
        qkv_weight_kernel, [((24,) + block, BF16)], *tie((grad_qkv, normed_all)), flops=2 * 2 * row_len * 192 * width,
        far_in=(0, 1), far_out=(0,),
    )[0])
    add("qkv_far", lambda tie: to_far(tie(get("qkv_sum"))))
    mate_grads = cross(21, mate_grads)
    norm_parts = kernel_call(
        back_qkv_kernel, [((row_count, seg_len, width), BF16)] * 7 + [((1, seg_len, width), BF16)] * 2,
        qkv_grads, to_mate(mate_grads, chips), w_qkv, get("heads_mate"),
        scratch=[pltpu.VMEM((512, width), BF16)], flops=2 * chips * count * 512 * width,
    )
    norm_ring = RingSum(norm_parts, chips)
    norm_ring.ahead, norm_ring.back = cross(22, norm_ring.ahead, norm_ring.back)
    norm_ring.hop()
    for hop in range(1, 4):
        norm_ring.ahead, norm_ring.back = cross(22 + hop, norm_ring.ahead, norm_ring.back)
        norm_ring.hop()
    trunk_parts = kernel_call(
        back_norm_kernel, [((2 * count, width // 4), BF16)] * 4,
        *cross(26, *norm_ring.terms()), trunk, gamma, grad_res, scalars=(place,), far_in=(3, 4, 5),
    )
    trunk_four = cross(28, *gather_four(cross(27, *trunk_parts)))

    in_parts = kernel_call(
        input_weight_kernel, [((32, 32, block[1]), BF16)] * 8,
        *x_four, *trunk_four, *get("mixed"), *get("att"), scalars=(targets,), far_in=tuple(range(16)), far_out=tuple(range(8)),
        lazy=True, **ROOM["in_weight"], scratch=[pltpu.VMEM((4, width // 4, width), BF16)], flops=2 * 4 * 4 * count * width * width // 4,
    )
    add("inputs", lambda tie: kernel_call(
        back_input_kernel, [frame_part] * 3, *tie(tuple(trunk_parts)), *[w for t in range(3) for w in get("w_four%d" % t)],
        flops=2 * 3 * count * width * width,
    ))

    def finish_ff(tie):
        for hop in range(4):
            get("ff_sum%d" % hop)
        total = sum_low(tie(ff_sums[0].terms()))
        return by_core(pick(total, core), to_mate(pick(total, 1 - core), chips)).reshape((32,) + block)

    add("ff_total", finish_ff)
    add("ff_far", lambda tie: to_far(tie(get("ff_total"))))
    in_sums = RingSum(in_parts, chips)
    in_sums.ahead, in_sums.back = cross(29, in_sums.ahead, in_sums.back)
    in_sums.hop()
    for hop in range(1, 4):
        in_sums.ahead, in_sums.back = cross(29 + hop, in_sums.ahead, in_sums.back)
        in_sums.hop()

    held_count = jnp.sum(held.astype(jnp.int32))
    match = held[None, :] & (slots[None, :] == jnp.arange(capacity, dtype=jnp.int32)[:, None])
    tile, row = ids // 8 - 7, ids % 8
    pair = tile % 4
    ff_place = 56 + 32 * (pair // 2 != group).astype(jnp.int32) + 16 * (pair % 2) + 8 * (tile // 4) + row
    source = jnp.sum(jnp.where(match, jnp.where(ids < 56, ids, ff_place)[None, :], 0), axis=1)
    stack = (capacity,) + block
    states = (turned, jnp.swapaxes(moment_one, 1, 2), jnp.swapaxes(moment_two, 1, 2))
    first_slots = 60
    per_step = math.gcd(first_slots, capacity - first_slots)

    def update(grads, start, stop, done):
        state = pl.BlockSpec((per_step,) + block, lambda i, *_: (i + start // per_step, 0, 0))
        whole = [pl.BlockSpec(g.shape, lambda i, *_, n=g.ndim: (0,) * n) for g in grads]
        return pl.pallas_call(
            functools.partial(adam_kernel, start=start, early=not done),
            grid_spec=pltpu.PrefetchScalarGridSpec(
                num_scalar_prefetch=3, grid=((stop - start) // per_step,),
                in_specs=whole + [state] * 3 + [pl.BlockSpec(memory_space=pl.ANY)] * len(done), out_specs=[state] * 4,
            ),
            out_shape=[jax.ShapeDtypeStruct(stack, F32)] * 3 + [jax.ShapeDtypeStruct(stack, BF16)],
            input_output_aliases={9 + i: i for i in range(len(done))},
            compiler_params=pltpu.CompilerParams(vmem_limit_bytes=32 * MIB),
            cost_estimate=pl.CostEstimate(flops=0, bytes_accessed=(stop - start) * 8192 * 26, transcendentals=0),
        )(source, held_count[None], group[None], *grads, *states, *done)

    def early_update(tie):
        qkv_own, ff_total = tie((get("qkv_sum"), get("ff_total")))
        rest = jnp.concatenate([add_low(qkv_own, get("qkv_far")), ff_total, get("ff_far")])
        tiny = jnp.zeros((1, 32, block[1]), BF16)
        return rest, tuple(update((tiny, tiny, rest), first_slots, capacity, ()))

    add("early", early_update)
    in_sum = cross(33, sum_low(in_sums.terms()))
    in_far = cross(34, to_far(in_sum))
    rest_grads, done = get("early")
    new_first, new_second, new_master, new_low = update((in_sum, in_far, rest_grads), 0, first_slots, done)
    back = lambda a: jnp.swapaxes(a, 1, 2)

    for n in range(5):
        get("small%d" % n)
    small_values = jnp.concatenate([norm_gains, ff_biases])
    small_new, small_one, small_two = adam(small_values, small[-1].reshape(-1), small_first, small_second, SMALL_RATE)

    branch = sum(part.astype(F32) for part in get("branch"))
    output = (residual + branch + ff_biases[None, width_ff:]) * valid
    output = output.astype(BF16).reshape(row_count, seg_len, width)
    inputs = [part.reshape(row_count, seg_len, width) for part in get("inputs")]
    return (
        output, inputs[0], inputs[1], inputs[2],
        back(new_first), back(new_second), back(new_master), back(new_low),
        small_one, small_two, small_new,
    )


def slot_places(owners, group_count, capacity):
    one_hot = (owners[:, None] == jnp.arange(group_count, dtype=jnp.int32)[None, :]).astype(
        jnp.int32
    )
    before = jnp.cumsum(one_hot, axis=0) - one_hot
    slot_index = jnp.sum(before * one_hot, axis=1)
    return owners * capacity + slot_index


def rotate(tensor, offset):
    half_size = tensor.shape[-1] // 2
    position = (offset + jnp.arange(tensor.shape[1], dtype=jnp.int32)).astype(jnp.float32)
    inverse = 10000.0 ** (-jnp.arange(half_size, dtype=jnp.int32).astype(jnp.float32) / half_size)
    phases = position[:, None] * inverse[None, :]
    cosine = jnp.cos(phases)[None, :, None, :]
    sine_part = jnp.sin(phases)[None, :, None, :]
    front_half = tensor[..., :half_size]
    back_half = tensor[..., half_size:]
    return jnp.concatenate(
        [front_half * cosine - back_half * sine_part, front_half * sine_part + back_half * cosine],
        axis=-1,
    )


def adaptive_norm(trunk, gamma_map):
    return (
        trunk
        * lax.rsqrt(jnp.mean(trunk * trunk, axis=-1, keepdims=True) + NORM_EPS)
        * (1.0 + gamma_map)
    )


def root_norm(residual, norm_gains):
    return (
        residual
        * lax.rsqrt(jnp.mean(residual * residual, axis=-1, keepdims=True) + NORM_EPS)
        * norm_gains
    )


def gelu_exact(tensor):
    return jax.nn.gelu(tensor, approximate=False)


def adam_update(weight, gradient, first_moment, second_moment, step_rate):
    first_moment = BETA_ONE * first_moment + (1.0 - BETA_ONE) * gradient
    second_moment = BETA_TWO * second_moment + (1.0 - BETA_TWO) * gradient * gradient
    fix_one = 1.0 - BETA_ONE**STEP
    fix_two = 1.0 - BETA_TWO**STEP
    update = first_moment / fix_one / (jnp.sqrt(second_moment / fix_two) + ADAM_EPS)
    return (weight - step_rate * (update + WEIGHT_DECAY * weight), first_moment, second_moment)


def matmul(former, latter):
    return jnp.dot(former, latter, preferred_element_type=jnp.float32)


def contract_rows(former, latter):
    return lax.dot_general(
        former, latter, (((0,), (0,)), ((), ())), preferred_element_type=jnp.float32
    )


def contract_cols(former, latter):
    return lax.dot_general(
        former, latter, (((1,), (1,)), ((), ())), preferred_element_type=jnp.float32
    )


def score_block(queries, key_rows, same_utt):
    scores = jnp.einsum(
        "qhd,khd->hqk", queries, key_rows, preferred_element_type=jnp.float32
    ) * HEAD_DIM ** (-0.5)
    scores = jnp.where(same_utt[None], scores, MASKED_SCORE)
    row_max = jnp.max(scores, axis=-1, keepdims=True)
    exponent = jnp.exp(scores - row_max)
    total = jnp.sum(exponent, axis=-1, keepdims=True)
    return (exponent / total, row_max[..., 0], total[..., 0])


def attend(element):
    queries, key_rows, values, same_utt = element
    attn_probs, row_max, total = score_block(queries, key_rows, same_utt)
    mixed = jnp.einsum(
        "hqk,khd->qhd", attn_probs.astype(jnp.bfloat16), values, preferred_element_type=jnp.float32
    )
    return (mixed.astype(jnp.bfloat16), attn_probs, row_max, total)


def probs_only(element):
    return score_block(element[0], element[1], element[2])


def attend_query(element):
    queries, key_rows, values, attn_probs, grad_mixed = element
    prob_grad = jnp.einsum("qhd,khd->hqk", grad_mixed, values, preferred_element_type=jnp.float32)
    inner_sum = jnp.sum(attn_probs * prob_grad, axis=-1, keepdims=True)
    score_grad = (attn_probs * (prob_grad - inner_sum)).astype(jnp.bfloat16)
    query_grad = jnp.einsum(
        "hqk,khd->qhd", score_grad, key_rows, preferred_element_type=jnp.float32
    ) * HEAD_DIM ** (-0.5)
    return (query_grad, inner_sum[..., 0])


def attend_keys(element):
    query_all, grad_all, max_all, total_all, inner_all, seg_query, key_own, value_own, seg_own = (
        element
    )
    scores = jnp.einsum(
        "qhd,khd->hqk", query_all, key_own, preferred_element_type=jnp.float32
    ) * HEAD_DIM ** (-0.5)
    same_utt = seg_query[:, None] == seg_own[None, :]
    scores = jnp.where(same_utt[None], scores, MASKED_SCORE)
    attn_probs = jnp.exp(scores - max_all[..., None]) / total_all[..., None]
    prob_grad = jnp.einsum("qhd,khd->hqk", grad_all, value_own, preferred_element_type=jnp.float32)
    score_grad = (attn_probs * (prob_grad - inner_all[..., None])).astype(jnp.bfloat16)
    key_grad = jnp.einsum(
        "hqk,qhd->khd", score_grad, query_all, preferred_element_type=jnp.float32
    ) * HEAD_DIM ** (-0.5)
    value_grad = jnp.einsum(
        "hqk,qhd->khd",
        attn_probs.astype(jnp.bfloat16),
        grad_all,
        preferred_element_type=jnp.float32,
    )
    return (key_grad, value_grad)


def general_shards(
    frames,
    skip_frames,
    time_embed,
    cotangent,
    segments,
    owners,
    master,
    moment_one,
    moment_two,
    norm_gains,
    ff_biases,
    small_first,
    small_second,
):
    row_count, seg_len, model_width = frames.shape
    width_ff = ff_biases.shape[0] - model_width
    frame_count = row_count * seg_len
    group_count = lax.axis_size("batch")
    capacity = master.shape[0]
    block_rows = master.shape[1]
    scale_in = model_width ** (-0.5)
    scale_time = 0.5 * model_width ** (-0.5)
    scale_out = 4.0 * model_width ** (-0.5)
    scale_ff = width_ff ** (-0.5)
    places = slot_places(owners, group_count, capacity)
    low_master = master.astype(jnp.bfloat16)
    all_slots = lax.all_gather(low_master, "batch", axis=0, tiled=True)
    columns = jnp.take(all_slots, places, axis=0)
    tile_stack = lax.all_gather(columns, "seq", axis=2, tiled=True).reshape(15, model_width, model_width)
    up_weight = jnp.concatenate(
        [tile_stack[7], tile_stack[8], tile_stack[9], tile_stack[10]], axis=1
    )
    down_weight = tile_stack[11:15].reshape(width_ff, model_width)
    flat_frames = frames.reshape(frame_count, model_width)
    flat_skip = skip_frames.reshape(frame_count, model_width)
    flat_time = time_embed.reshape(frame_count, model_width)
    offset = lax.axis_index("seq") * seg_len

    def rotate_here(tensor):
        return rotate(tensor, offset)

    def split_heads(tensor):
        return tensor.reshape(row_count, seg_len, HEADS, HEAD_DIM)

    trunk = (matmul(flat_frames, tile_stack[0]) + matmul(flat_skip, tile_stack[1])) * scale_in
    gamma_map = matmul(flat_time, tile_stack[2]) * scale_time
    normed_f32, norm_pull = jax.vjp(adaptive_norm, trunk, gamma_map)
    normed = normed_f32.astype(jnp.bfloat16)
    query_rot, query_pull = jax.vjp(
        rotate_here, split_heads(matmul(normed, tile_stack[3]) * scale_in)
    )
    key_rot, key_pull = jax.vjp(rotate_here, split_heads(matmul(normed, tile_stack[4]) * scale_in))
    queries = query_rot.astype(jnp.bfloat16)
    key_local = key_rot.astype(jnp.bfloat16).reshape(row_count, seg_len, model_width)
    value_local = (
        (matmul(normed, tile_stack[5]) * scale_in)
        .astype(jnp.bfloat16)
        .reshape(row_count, seg_len, model_width)
    )
    seg_low = segments.astype(jnp.bfloat16)
    key_all, value_all, seg_all = (
        lax.all_gather(key_local, "seq", axis=1, tiled=True),
        lax.all_gather(value_local, "seq", axis=1, tiled=True),
        lax.all_gather(seg_low, "seq", axis=1, tiled=True),
    )
    key_total = key_all.shape[1]
    key_heads = key_all.reshape(row_count, key_total, HEADS, HEAD_DIM)
    value_heads = value_all.reshape(row_count, key_total, HEADS, HEAD_DIM)
    same_utt = seg_low[:, :, None] == seg_all[:, None, :]
    mixed_heads, probs_kept, max_kept, total_kept = lax.map(
        attend, (queries, key_heads, value_heads, same_utt)
    )
    mixed_rows = mixed_heads.reshape(frame_count, model_width)
    residual = trunk + matmul(mixed_rows, tile_stack[6]) * scale_out
    normed_two_f32, root_pull = jax.vjp(root_norm, residual, norm_gains)
    normed_two = normed_two_f32.astype(jnp.bfloat16)
    pre_act = matmul(normed_two, up_weight) * scale_in + ff_biases[:width_ff]
    activation, gelu_pull = jax.vjp(gelu_exact, pre_act)
    hidden = activation.astype(jnp.bfloat16)
    branch = matmul(hidden, down_weight) * scale_ff + ff_biases[width_ff:]
    valid_row = (segments < UTTS).astype(jnp.float32).reshape(frame_count, 1)
    output = (
        ((residual + branch) * valid_row)
        .astype(jnp.bfloat16)
        .reshape(row_count, seg_len, model_width)
    )
    grad_out = cotangent.reshape(frame_count, model_width).astype(jnp.float32) * valid_row
    grad_branch = grad_out.astype(jnp.bfloat16)
    grad_down_bias = jnp.sum(grad_branch.astype(jnp.float32), axis=0)
    down_grads = contract_rows(hidden, grad_branch) * scale_ff
    grad_hidden = contract_cols(grad_branch, down_weight) * scale_ff
    grad_pre = gelu_pull(grad_hidden)[0].astype(jnp.bfloat16)
    grad_up_bias = jnp.sum(grad_pre.astype(jnp.float32), axis=0)
    up_grads = contract_rows(normed_two, grad_pre) * scale_in
    grad_normed_two = contract_cols(grad_pre, up_weight) * scale_in
    grad_residual_norm, grad_gains = root_pull(grad_normed_two)
    grad_residual = grad_out + grad_residual_norm
    grad_attention = grad_residual.astype(jnp.bfloat16)
    out_grads = contract_rows(mixed_rows, grad_attention) * scale_out
    grad_mixed = (contract_cols(grad_attention, tile_stack[6]) * scale_out).astype(jnp.bfloat16)
    grad_mixed = grad_mixed.reshape(row_count, seg_len, HEADS, HEAD_DIM)
    key_again, value_again, seg_again = (
        lax.all_gather(key_local, "seq", axis=1, tiled=True),
        lax.all_gather(value_local, "seq", axis=1, tiled=True),
        lax.all_gather(seg_low, "seq", axis=1, tiled=True),
    )
    back_keys = key_again.reshape(row_count, key_total, HEADS, HEAD_DIM)
    back_values = value_again.reshape(row_count, key_total, HEADS, HEAD_DIM)
    same_again = seg_low[:, :, None] == seg_again[:, None, :]
    back_probs, back_max, back_total = lax.map(probs_only, (queries, back_keys, same_again))
    query_raw, inner_sum = lax.map(
        attend_query, (queries, back_keys, back_values, back_probs, grad_mixed)
    )
    query_all, grad_all = (
        lax.all_gather(queries, "seq", axis=1, tiled=True),
        lax.all_gather(grad_mixed, "seq", axis=1, tiled=True),
    )
    max_all, total_all, inner_all = (
        lax.all_gather(back_max, "seq", axis=2, tiled=True),
        lax.all_gather(back_total, "seq", axis=2, tiled=True),
        lax.all_gather(inner_sum, "seq", axis=2, tiled=True),
    )
    key_own = key_local.reshape(row_count, seg_len, HEADS, HEAD_DIM)
    value_own = value_local.reshape(row_count, seg_len, HEADS, HEAD_DIM)
    key_sum, value_sum = lax.map(
        attend_keys,
        (
            query_all,
            grad_all,
            max_all,
            total_all,
            inner_all,
            seg_again,
            key_own,
            value_own,
            seg_low,
        ),
    )
    grad_q = query_pull(query_raw)[0].reshape(frame_count, model_width).astype(jnp.bfloat16)
    grad_k = key_pull(key_sum)[0].reshape(frame_count, model_width).astype(jnp.bfloat16)
    grad_v = value_sum.reshape(frame_count, model_width).astype(jnp.bfloat16)
    query_grads = contract_rows(normed, grad_q) * scale_in
    key_grads = contract_rows(normed, grad_k) * scale_in
    value_grads = contract_rows(normed, grad_v) * scale_in
    grad_normed = (
        contract_cols(grad_q, tile_stack[3])
        + contract_cols(grad_k, tile_stack[4])
        + contract_cols(grad_v, tile_stack[5])
    ) * scale_in
    grad_trunk_norm, grad_gamma_f32 = norm_pull(grad_normed)
    grad_trunk = (grad_residual + grad_trunk_norm).astype(jnp.bfloat16)
    grad_gamma = grad_gamma_f32.astype(jnp.bfloat16)
    frame_grads = contract_rows(flat_frames, grad_trunk) * scale_in
    skip_grads = contract_rows(flat_skip, grad_trunk) * scale_in
    time_grads = contract_rows(flat_time, grad_gamma) * scale_time
    grad_frames = (contract_cols(grad_trunk, tile_stack[0]) * scale_in).reshape(
        row_count, seg_len, model_width
    )
    grad_skip = (contract_cols(grad_trunk, tile_stack[1]) * scale_in).reshape(
        row_count, seg_len, model_width
    )
    grad_time = (contract_cols(grad_gamma, tile_stack[2]) * scale_time).reshape(
        row_count, seg_len, model_width
    )
    first_tiles = jnp.stack(
        [frame_grads, skip_grads, time_grads, query_grads, key_grads, value_grads, out_grads]
    )
    up_tiles = up_grads.reshape(model_width, 4, model_width).transpose(1, 0, 2)
    down_tiles = down_grads.reshape(4, model_width, model_width)
    blocks = jnp.concatenate([first_tiles, up_tiles, down_tiles], axis=0).reshape(
        -1, block_rows, model_width
    )
    block_count = blocks.shape[0]
    partial_cols = lax.psum_scatter(
        blocks.astype(jnp.bfloat16), "seq", scatter_dimension=2, tiled=True
    )
    matches = places[None, :] == jnp.arange(group_count * capacity, dtype=jnp.int32)[:, None]
    source = jnp.sum(
        jnp.where(matches, jnp.arange(block_count, dtype=jnp.int32)[None, :], 0), axis=1
    )
    filled = jnp.any(matches, axis=1)
    placed = jnp.where(filled[:, None, None], jnp.take(partial_cols, source, axis=0), 0)
    reduced = lax.psum_scatter(placed, "batch", scatter_dimension=0, tiled=True).astype(
        jnp.float32
    )
    small_grad = jnp.concatenate([grad_gains, grad_up_bias, grad_down_bias])
    small_grad = lax.psum(small_grad, ("seq", "batch"))
    owner_index = lax.axis_index("batch")
    held_count = jnp.sum((owners == owner_index).astype(jnp.int32))
    live_slot = (jnp.arange(capacity, dtype=jnp.int32) < held_count).astype(jnp.float32)[
        :, None, None
    ]
    new_master, new_first, new_second = adam_update(
        master, reduced, moment_one, moment_two, LEARN_RATE
    )
    new_master = new_master * live_slot
    new_first = new_first * live_slot
    new_second = new_second * live_slot
    small_values = jnp.concatenate([norm_gains, ff_biases])
    small_new, small_first_new, small_second_new = adam_update(
        small_values, small_grad, small_first, small_second, SMALL_RATE
    )
    return (
        output,
        grad_frames,
        grad_skip,
        grad_time,
        new_first,
        new_second,
        new_master,
        new_master.astype(jnp.bfloat16),
        small_first_new,
        small_second_new,
        small_new,
    )


def solution(mesh):
    fast = mesh.shape["seq"] == HEADS and mesh.shape["batch"] == 2
    rows, slots, whole = P("batch", "seq", None), P("batch", None, "seq"), P()
    return jax.shard_map(
        fast_shards if fast else general_shards,
        mesh=mesh,
        in_specs=(rows, rows, rows, rows, P("batch", "seq"), whole, slots, slots, slots, whole, whole, whole, whole),
        out_specs=(rows, rows, rows, rows, slots, slots, slots, slots, whole, whole, whole),
        check_vma=False,
    )
```

```python
import functools
import math

import jax
import jax.numpy as jnp
from jax import lax
from jax.experimental import pallas as pl
from jax.experimental.pallas import tpu as pltpu
from jax.sharding import PartitionSpec as P

HEADS = 16
HEAD_DIM = 64
UTTS = 8
STEP = 10
NORM_EPS = 1e-06
MASKED_SCORE = -1e30
BETA_ONE = 0.9
BETA_TWO = 0.999
ADAM_EPS = 1e-08
WEIGHT_DECAY = 0.01
LEARN_RATE = 1.0
SMALL_RATE = 0.1

F32 = jnp.float32
BF16 = jnp.bfloat16
MIB = 1 << 20


def padded(shape, dtype):
    size = jnp.dtype(dtype).itemsize
    rows = 32 // size
    shape = (1,) * (2 - len(shape)) + tuple(shape)
    return math.prod(shape[:-2]) * (-(-shape[-2] // rows) * rows) * (-(-shape[-1] // 128) * 128) * size


def kernel_call(body, outs, *args, scalars=(), scratch=(), room=10, flops=0, far_in=(), far_out=(), lazy=False):
    n_in, n_out = len(args), len(outs)
    vmem, hbm = pl.BlockSpec(memory_space=pltpu.VMEM), pl.BlockSpec(memory_space=pltpu.HBM)
    specs = [pl.BlockSpec(memory_space=pltpu.SMEM) for _ in scalars]
    specs += [hbm if i in far_in else vmem for i in range(n_in)]
    moved = sum(padded(a.shape, a.dtype) for a in args) + sum(padded(s, d) for s, d in outs)
    held = moved + sum(padded(ref.shape, ref.dtype) for ref in scratch)
    far = [pltpu.VMEM(args[i].shape, args[i].dtype) for i in far_in] + [pltpu.VMEM(*outs[i]) for i in far_out]
    copies = [pltpu.SemaphoreType.DMA((len(far),))] if far else []

    def whole(*refs):
        refs = list(refs)
        first = len(scalars)
        if far:
            sems = refs.pop()
            held_refs = refs[len(refs) - len(far) :]
            refs = refs[: len(refs) - len(far)]
            pairs = []
            for n, i in enumerate(far_in):
                pairs.append(pltpu.make_async_copy(refs[first + i], held_refs[n], sems.at[n]))
                refs[first + i] = held_refs[n]
            results = []
            for n, i in enumerate(far_out, len(far_in)):
                results.append(pltpu.make_async_copy(held_refs[n], refs[first + n_in + i], sems.at[n]))
                refs[first + n_in + i] = held_refs[n]
            for copy in pairs:
                copy.start()
            if not lazy:
                for copy in pairs:
                    copy.wait()
        if lazy:
            body(*refs, wait=lambda i: pairs[far_in.index(i)].wait())
        else:
            body(*refs)
        if far:
            for copy in results:
                copy.start()
            for copy in results:
                copy.wait()

    return pl.pallas_call(
        whole,
        out_shape=[jax.ShapeDtypeStruct(shape, dtype) for shape, dtype in outs],
        in_specs=specs,
        out_specs=[hbm if i in far_out else vmem for i in range(n_out)],
        scratch_shapes=list(scratch) + far + copies,
        compiler_params=pltpu.CompilerParams(vmem_limit_bytes=min(held + room * MIB, 58 * MIB)),
        cost_estimate=pl.CostEstimate(flops=int(flops), bytes_accessed=int(moved), transcendentals=0),
    )(*scalars, *args)


def dot_nn(a, b):
    return jnp.dot(a, b, preferred_element_type=F32)


def dot_nt(a, b):
    return lax.dot_general(a, b, (((1,), (1,)), ((), ())), preferred_element_type=F32)


def dot_tn(a, b):
    return lax.dot_general(a, b, (((0,), (0,)), ((), ())), preferred_element_type=F32)


def lanes(blocks):
    return jnp.concatenate(blocks, axis=-1)


def at128(index):
    return pl.multiple_of(index * 128, 128)


def normal_cdf(x):
    return 0.5 * (1.0 + lax.erf(x * (2.0**-0.5)))


OUT_ROWS, SEG_ROWS, PIECE_ROWS, PIECE_CUT = 768, 1280, 1312, 640


def pick_kernel(slots, place, master, keep, far_send, give, heads, pair_own, pair_far, pair_mate, pair_diag):
    group, core = place[0], place[1]

    def low(k):
        return master[slots[k]].astype(BF16)

    def tile_pair(pair, j):
        return low((7 + pair) * 8 + j), low((11 + pair) * 8 + j)

    mine = pl.ds(pl.multiple_of(32 * group, 32), 32)
    other = pl.ds(pl.multiple_of(32 - 32 * group, 32), 32)
    for k in range(24):
        keep[32 * k : 32 * k + 32] = master[slots[k], mine].astype(BF16)
        far_send[32 * k : 32 * k + 32] = master[slots[k], other].astype(BF16)
    for j in range(4):
        rows = slice(OUT_ROWS + 64 * j, OUT_ROWS + 64 * j + 64)
        block = low(48 + 4 * core + j)
        keep[rows] = block
        far_send[rows] = block
        give[64 * j : 64 * j + 64] = low(52 - 4 * core + j)
    for k in range(24):
        heads[k] = low(24 + k)
    for j in range(8):
        pair_far[j], pair_far[8 + j] = tile_pair(2 - 2 * group + core, j)
        pair_own[j], pair_own[8 + j] = tile_pair(2 * group + core, j)
        pair_mate[j], pair_mate[8 + j] = tile_pair(2 * group + 1 - core, j)
        pair_diag[j], pair_diag[8 + j] = tile_pair(3 - 2 * group - core, j)


def select_in_kernel(held, place, own, far, mate, diag, seg_own, seg_mate, out):
    group, core = place[0], place[1]
    for k in range(24):
        rows = slice(32 * k, 32 * k + 32)
        out[rows] = jnp.where(held[k] == group, own[rows], far[rows])
    for j in range(4):
        mine = held[48 + 4 * core + j] == group
        rows, part = slice(OUT_ROWS + 64 * j, OUT_ROWS + 64 * j + 64), slice(64 * j, 64 * j + 64)
        out[rows] = jnp.where(mine, own[rows], far[rows])
        out[OUT_ROWS + 256 + 64 * j : OUT_ROWS + 320 + 64 * j] = jnp.where(mine, mate[part], diag[part])
    out[SEG_ROWS : SEG_ROWS + 16] = seg_own[...]
    out[SEG_ROWS + 16 : SEG_ROWS + 32] = seg_mate[...]


def select_heads_kernel(held, place, own, far, out):
    for k in range(24):
        out[k] = jnp.where(held[24 + k] == place[0], own[k], far[k])


def select_pairs_kernel(held, place, own, far, mate, diag, out):
    group, core = place[0], place[1]
    for half, first in ((0, 7), (1, 11)):
        for j in range(8):
            k = 8 * half + j
            mine = held[(first + 2 * group + core) * 8 + j] == group
            out[core, k] = jnp.where(mine, own[k], far[k])
            out[1 - core, k] = jnp.where(mine, mate[k], diag[k])


def ring_readers(refs):
    def last(first, count):
        if first < PIECE_CUT:
            return refs[7][first : first + count, :]
        return refs[8][first - PIECE_CUT : first - PIECE_CUT + count, :]

    return [lambda first, count, r=r: r[first : first + count, :] for r in refs[:7]] + [last]


def ring_blocks(refs):
    return [lambda s, k, r=r: r[s, k] for r in refs]


def trunk_kernel(places, own_x, far_x, mate_x, diag_x, *refs):
    pieces, outs, seg_out, weight = ring_readers(refs[:9]), refs[9:13], refs[13], refs[14:]
    width = own_x.shape[-1]
    count = own_x.shape[1]
    scale_in = width**-0.5
    for p, piece in enumerate(pieces):
        rows = pl.ds(pl.multiple_of(32 * places[p], 32), 32)
        for t in range(3):
            for j in range(8):
                weight[t][rows, 128 * j : 128 * j + 128] = piece(256 * t + 32 * j, 32)
        ids = [piece(SEG_ROWS + 16 * m, 16).astype(F32)[0:8, 0:64] for m in range(2)]
        seg_out[:, 128 * p : 128 * p + 128] = lanes(ids)
    x = [jnp.concatenate([ref[t] for ref in (own_x, far_x, mate_x, diag_x)], axis=0) for t in range(3)]
    trunk = (dot_nt(x[0], weight[0][...]) + dot_nt(x[1], weight[1][...])) * scale_in
    gamma = dot_nt(x[2], weight[2][...]) * (0.5 * scale_in)
    for i, out in enumerate(outs):
        out[0] = trunk[i * count : i * count + count]
        out[1] = gamma[i * count : i * count + count]


def assemble_out_kernel(places, place, *refs):
    out = refs[9]
    core = place[1]
    for p, piece in enumerate(ring_readers(refs[:9])):
        for m in range(2):
            column = 64 * core if m == 0 else 64 - 64 * core
            rows = pl.ds(pl.multiple_of(places[p] * 128 + column, 64), 64)
            for j in range(4):
                out[rows, 128 * j : 128 * j + 128] = piece(OUT_ROWS + 256 * m + 64 * j, 64)


def by_quarter(parts, mine):
    found = []
    for q in range(4):
        low = jnp.where(mine == 0, parts[q], parts[q ^ 1])
        high = jnp.where(mine == 2, parts[q ^ 2], parts[q ^ 3])
        found.append(jnp.where(mine < 2, low, high))
    return found


def norm_kernel(place, own, far, mate, diag, trunk_out, gamma_out, normed_out):
    mine = 2 * place[1] + place[0]
    for i, out in enumerate((trunk_out, gamma_out)):
        parts = by_quarter([ref[i] for ref in (own, far, mate, diag)], mine)
        for c in range(8):
            out[:, 128 * c : 128 * c + 128] = lanes([part[:, 32 * c : 32 * c + 32] for part in parts])
    trunk = trunk_out[...]
    scale = lax.rsqrt(jnp.mean(trunk * trunk, axis=-1, keepdims=True) + NORM_EPS)
    normed_out[...] = (trunk * scale * (1.0 + gamma_out[...])).astype(BF16)


def swap_halves(x):
    half = HEAD_DIM // 2
    return jnp.concatenate([x[:, half:], x[:, :half]], axis=1)


def frame_rows(refs, p, m):
    base = 9 * m
    if p < 7:
        return refs[base + p][...]
    return jnp.concatenate([refs[base + 7][...], refs[base + 8][...]], axis=0)


def attend_kernel(sources, weight, cosine, sine, seg, *refs):
    normed = refs[:18]
    qkv_ref, out_ref, x_ref, mixed = refs[18:]
    q_ref, k_ref, v_ref = (qkv_ref.at[t] for t in range(3))
    width = normed[0].shape[1]
    scale_in = width**-0.5
    w = jnp.concatenate(
        [lanes([weight[8 * t + j] for j in range(8)]) for t in range(3)], axis=0
    )
    row_len = q_ref.shape[1]
    for p in range(8):
        for m in range(2):
            u = 2 * p + m
            spot = pl.ds(u * 64, 64)
            rows = frame_rows(normed, p, m)
            for r in range(2):
                x_ref[pl.ds(r * row_len + u * 64, 64)] = rows[64 * r : 64 * r + 64]
            qkv = dot_nt(rows, w) * scale_in
            c, s = cosine[spot], sine[spot]
            for r in range(2):
                part = qkv[64 * r : 64 * r + 64]
                for ref, lo, scale in ((q_ref, 0, HEAD_DIM**-0.5), (k_ref, 64, 1.0)):
                    x = part[:, lo : lo + 64]
                    ref[r, spot] = ((x * c + swap_halves(x) * s) * scale).astype(BF16)
                v_ref[r, spot] = part[:, 128:192].astype(BF16)
    block = 256
    seg_cols = jnp.transpose(seg[...])
    for r in range(2):
        key, value = k_ref[r], v_ref[r]
        seg_keys = seg[r : r + 1, :]
        for q in range(row_len // block):
            spot = pl.ds(q * block, block)
            scores = dot_nt(q_ref[r, spot], key)
            same = seg_cols[q * block : q * block + block, r : r + 1] == seg_keys
            scores = jnp.where(same, scores, MASKED_SCORE)
            top = jnp.max(scores, axis=-1, keepdims=True)
            exponent = jnp.exp(scores - top)
            total = jnp.sum(exponent, axis=-1, keepdims=True)
            probs = (exponent * (1.0 / total)).astype(BF16)
            mixed[r, spot] = dot_nn(probs, value).astype(BF16)
    for u in range(16):
        spot = pl.ds(u * 64, 64)
        out_ref[sources[u]] = lanes([mixed[0, spot], mixed[1, spot]])


def residual_kernel(core, heads, w_own, w_mate, trunk, gains, res_out, normed_out, mixed_out):
    scale_out = 4.0 * trunk.shape[1] ** -0.5
    for r in range(2):
        for j in range(8):
            pair = [heads[2 * j + i][:, 64 * r : 64 * r + 64] for i in range(2)]
            mixed_out[64 * r : 64 * r + 64, 128 * j : 128 * j + 128] = lanes(pair)
    here = pl.ds(pl.multiple_of(core[0] * 512, 512), 512)
    there = pl.ds(pl.multiple_of(512 - core[0] * 512, 512), 512)
    attention = dot_nt(mixed_out[:, here], w_own[...]) + dot_nt(mixed_out[:, there], w_mate[...])
    residual = trunk[...] + attention * scale_out
    res_out[...] = residual
    scale = lax.rsqrt(jnp.mean(residual * residual, axis=-1, keepdims=True) + NORM_EPS)
    normed_out[...] = (residual * scale * gains[...]).astype(BF16)


def forward_back_kernel(places, *refs, wait):
    normed, grad, bias, pieces, refs = refs[:4], refs[4:8], refs[8], ring_blocks(refs[9:17]), refs[17:]
    grad_in, branch, (hidden_out, pre_out, bias_out, w_up, w_down, branch_acc) = refs[:4], refs[4:8], refs[8:]
    width = w_up.shape[1]
    count = normed[0].shape[0]
    scale_in = width**-0.5
    scale_ff = (4 * width) ** -0.5
    for p, piece in enumerate(pieces):
        wait(9 + p)
        for s in range(2):
            rows = pl.ds(pl.multiple_of(places[p] * 128 + 64 * s, 64), 64)
            for j in range(8):
                w_up[rows, 128 * j : 128 * j + 128] = piece(s, j)
                w_down[rows, 128 * j : 128 * j + 128] = piece(s, 8 + j)
    for i in range(9):
        wait(i)
    x = jnp.concatenate([ref[...] for ref in normed], axis=0)
    g = jnp.concatenate([ref[...] for ref in grad], axis=0)
    block = 256
    for h in range(width // block):
        spot = slice(h * block, h * block + block)
        pre = dot_nt(x, w_up[spot, :]) * scale_in + bias[:, spot]
        cdf = normal_cdf(pre)
        hidden = (pre * cdf).astype(BF16)
        slope = cdf + pre * (jnp.exp(-0.5 * pre * pre) * (2.0 * math.pi) ** -0.5)
        grad_pre = slope * (dot_nn(g, w_down[:, spot]) * scale_ff)
        grad_pre = grad_pre.astype(BF16)
        hidden_out[:, spot] = hidden
        pre_out[:, spot] = grad_pre
        bias_out[:, spot] = jnp.sum(grad_pre.astype(F32), axis=0, keepdims=True)
        grad_part = dot_nn(grad_pre, w_up[spot, :]) * scale_in
        out_part = dot_nt(hidden, w_down[:, spot]) * scale_ff
        for i in range(4):
            rows = slice(i * count, i * count + count)
            if h == 0:
                grad_in[i][...] = grad_part[rows]
            else:
                grad_in[i][...] += grad_part[rows]
        if h == 0:
            branch_acc[...] = out_part
        else:
            branch_acc[...] += out_part
    for i in range(4):
        branch[i][...] = branch_acc[i * count : i * count + count, :].astype(BF16)


def ff_weight_kernel(targets, *refs):
    normed, grad, (hidden, pre), outs = refs[:4], refs[4:8], refs[8:10], refs[10:]
    width = hidden.shape[1]
    scale_in = width**-0.5
    scale_ff = (4 * width) ** -0.5
    x = jnp.concatenate([ref[...] for ref in normed], axis=0)
    for p in range(8):
        spot = pl.ds(at128(targets[p]), 128)
        g = jnp.concatenate([ref[:, spot] for ref in grad], axis=0)
        up = (dot_tn(pre[:, spot], x) * scale_in).astype(BF16)
        down = (dot_tn(g, hidden[...]) * scale_ff).astype(BF16)
        for s in range(2):
            rows = slice(64 * s, 64 * s + 64)
            for j in range(8):
                outs[p][s, j] = up[rows, 128 * j : 128 * j + 128]
                outs[p][s, 8 + j] = down[rows, 128 * j : 128 * j + 128]


def quarters(x, mine, outs):
    parts = [lanes([x[:, 128 * c + 32 * q : 128 * c + 32 * q + 32] for c in range(x.shape[1] // 128)]) for q in range(4)]
    for out, part in zip(outs, by_quarter(parts, mine)):
        out[...] = part


def back_out_kernel(place, grad_own, grad_mate, grad_far, residual, gains, grad_out, w_own, w_mate, grad_res, heads, gain_out, *att):
    width = residual.shape[1]
    g = grad_own[...] + grad_mate[...] + grad_far[...].astype(F32)
    x = residual[...]
    scale = lax.rsqrt(jnp.mean(x * x, axis=-1, keepdims=True) + NORM_EPS)
    gain_out[...] = jnp.sum(g * x * scale, axis=0, keepdims=True)
    inner = g * gains[...]
    slope = inner * scale - x * (scale * scale * scale * jnp.mean(inner * x, axis=-1, keepdims=True))
    total = grad_out[...].astype(F32) + slope
    grad_res[...] = total
    low = total.astype(BF16)
    quarters(low, 2 * place[1] + place[0], att)
    halves = [dot_nn(low, w[...]) * (4.0 * width**-0.5) for w in (w_own, w_mate)]
    mixed = jnp.where(place[1] == 0, lanes(halves), lanes(halves[::-1])).astype(BF16)
    for j in range(8):
        rows = [mixed[64 * r : 64 * r + 64, 128 * j : 128 * j + 128] for r in range(2)]
        heads[2 * j] = lanes([rows[0][:, :64], rows[1][:, :64]])
        heads[2 * j + 1] = lanes([rows[0][:, 64:], rows[1][:, 64:]])


def attend_back_kernel(sources, qkv_ref, grads, cosine, sine, seg, own_out, mate_out, done_ref, g_ref, acc_q, acc_k, acc_v):
    q_ref, k_ref, v_ref = (qkv_ref.at[t] for t in range(3))
    dq_ref, dk_ref, dv_ref = (done_ref.at[t] for t in range(3))
    row_len = q_ref.shape[1]
    for u in range(16):
        spot = pl.ds(u * 64, 64)
        both = grads[sources[u]]
        g_ref[0, spot] = both[:, :64]
        g_ref[1, spot] = both[:, 64:]
    block = 256
    seg_cols = jnp.transpose(seg[...])
    for r in range(2):
        key, value = k_ref[r], v_ref[r]
        for q in range(row_len // block):
            spot = pl.ds(q * block, block)
            query, grad = q_ref[r, spot], g_ref[r, spot]
            scores = dot_nt(key, query)
            same = seg_cols[:, r : r + 1] == seg[r : r + 1, q * block : q * block + block]
            scores = jnp.where(same, scores, MASKED_SCORE)
            top = jnp.max(scores, axis=0, keepdims=True)
            exponent = jnp.exp(scores - top)
            total = jnp.sum(exponent, axis=0, keepdims=True)
            probs = exponent * (1.0 / total)
            prob_grad = dot_nt(value, grad)
            inner = jnp.sum(probs * prob_grad, axis=0, keepdims=True)
            score_grad = (probs * (prob_grad - inner)).astype(BF16)
            acc_q[r, spot] = dot_tn(score_grad, key)
            key_part = dot_nn(score_grad, query)
            value_part = dot_nn(probs.astype(BF16), grad)
            if q == 0:
                acc_k[r] = key_part
                acc_v[r] = value_part
            else:
                acc_k[r] += key_part
                acc_v[r] += value_part
        c, s = cosine[...], sine[...]
        for ref, acc, scale in ((dq_ref, acc_q, HEAD_DIM**-0.5), (dk_ref, acc_k, 1.0)):
            g = acc[r] * scale
            ref[r] = (g * c + swap_halves(g * s)).astype(BF16)
        dv_ref[r] = acc_v[r].astype(BF16)
    empty = jnp.zeros((64, HEAD_DIM), BF16)
    for p in range(8):
        for m, out in enumerate((own_out, mate_out)):
            spot = pl.ds((2 * p + m) * 64, 64)
            for r in range(2):
                rows = pl.ds(128 * p + 64 * r, 64)
                out[rows, 0:128] = lanes([dq_ref[r, spot], dk_ref[r, spot]])
                out[rows, 128:256] = lanes([dv_ref[r, spot], empty])


def qkv_weight_kernel(done_ref, x_ref, out):
    dq_ref, dk_ref, dv_ref = (done_ref.at[t] for t in range(3))
    width = x_ref.shape[1]
    rows = lambda ref: jnp.concatenate([ref[0], ref[1]], axis=0)
    both = [lanes([rows(dq_ref), rows(dk_ref)]), rows(dv_ref)]
    for t in range(2):
        grads = (dot_tn(both[t], x_ref[...]) * width**-0.5).astype(BF16)
        for i in range(2 - t):
            for j in range(8):
                out[16 * t + 8 * i + j] = grads[64 * i : 64 * i + 64, 128 * j : 128 * j + 128]


MIRROR = (0, 2, 1, 4, 3, 6, 5, 7)


def back_qkv_kernel(own_y, mate_y, own_w, mate_w, *refs):
    outs, w = refs[:9], refs[9]
    width = w.shape[1]
    for h, weight in enumerate((own_w, mate_w)):
        for j in range(8):
            spot = slice(128 * j, 128 * j + 128)
            for t in range(3):
                w[256 * h + 64 * t : 256 * h + 64 * t + 64, spot] = weight[8 * t + j]
            w[256 * h + 192 : 256 * h + 256, spot] = jnp.zeros((64, 128), BF16)
    for i, p in enumerate(MIRROR):
        rows = slice(128 * p, 128 * p + 128)
        part = (dot_nn(lanes([own_y[rows], mate_y[rows]]), w[...]) * width**-0.5).astype(BF16)
        for r in range(2):
            half = part[64 * r : 64 * r + 64]
            if i < 7:
                outs[i][r] = half
            else:
                outs[7 + r][0] = half


def back_norm_kernel(place, one, two, three, trunk, gamma, grad_res, *parts):
    sums = one[...].astype(F32) + two[...].astype(F32) + three[...].astype(F32)
    g = jnp.concatenate([sums[0], sums[1]], axis=0)
    x = trunk[...]
    scale = lax.rsqrt(jnp.mean(x * x, axis=-1, keepdims=True) + NORM_EPS)
    inner = g * (1.0 + gamma[...])
    slope = inner * scale - x * (scale * scale * scale * jnp.mean(inner * x, axis=-1, keepdims=True))
    grad_trunk = (grad_res[...] + slope).astype(BF16)
    grad_gamma = (g * (x * scale)).astype(BF16)
    both = jnp.concatenate([grad_trunk, grad_gamma], axis=0)
    quarters(both, 2 * place[1] + place[0], parts)


def input_weight_kernel(targets, *refs, wait):
    x_refs, y_refs, m_refs, a_refs, refs = refs[:4], refs[4:8], refs[8:12], refs[12:16], refs[16:]
    outs, done = refs[:8], refs[8]
    count, width = m_refs[0].shape
    scale_in = width**-0.5
    stacked = lambda refs, cut: jnp.concatenate([ref[cut] for ref in refs], axis=0)
    for i in range(8, 16):
        wait(i)
    done[3] = (dot_tn(stacked(a_refs, slice(None)), stacked(m_refs, slice(None))) * (4.0 * scale_in)).astype(BF16)
    for i in range(8):
        wait(i)
    trunk_grads = stacked(y_refs, slice(0, count))
    gamma_grads = stacked(y_refs, slice(count, 2 * count))
    done[0] = (dot_tn(trunk_grads, stacked(x_refs, 0)) * scale_in).astype(BF16)
    done[1] = (dot_tn(trunk_grads, stacked(x_refs, 1)) * scale_in).astype(BF16)
    done[2] = (dot_tn(gamma_grads, stacked(x_refs, 2)) * (0.5 * scale_in)).astype(BF16)
    for p in range(8):
        rows = pl.ds(pl.multiple_of(targets[p] * 32, 32), 32)
        for t in range(4):
            for j in range(8):
                value = done[t, rows, 128 * j : 128 * j + 128]
                outs[p][8 * t + j] = value


def back_input_kernel(*refs):
    y_refs, w_refs, outs = refs[:4], refs[4:16], refs[16:]
    count, width = outs[0].shape
    scale_in = width**-0.5
    for t, out in enumerate(outs):
        rows = slice(0, count) if t < 2 else slice(count, 2 * count)
        total = dot_nn(y_refs[0][rows], w_refs[4 * t][...])
        for r in range(1, 4):
            total += dot_nn(y_refs[r][rows], w_refs[4 * t + r][...])
        out[...] = total * (scale_in if t < 2 else 0.5 * scale_in)


def adam(weight, gradient, first, second, rate):
    first = BETA_ONE * first + (1.0 - BETA_ONE) * gradient
    second = BETA_TWO * second + (1.0 - BETA_TWO) * gradient * gradient
    fix_one = 1.0 - BETA_ONE**STEP
    fix_two = 1.0 - BETA_TWO**STEP
    update = first / fix_one / (jnp.sqrt(second / fix_two) + ADAM_EPS)
    return weight - rate * (update + WEIGHT_DECAY * weight), first, second


def adam_kernel(source, held, group, in_own, in_far, rest, master, first, second, *refs, start, early):
    new_first, new_second, new_master, new_low = refs[-4:]
    step = pl.program_id(0)
    count = master.shape[0]
    for i in range(count):
        slot = start + step * count + i
        k = source[slot]
        live = (slot < held[0]).astype(F32)
        gradient = rest[jnp.where(k < 48, jnp.maximum(k - 24, 0), jnp.maximum(k - 32, 24))].astype(F32)
        if not early:
            k_in = jnp.where(k < 24, k, jnp.clip(k - 24, 24, 31))
            own, far = in_own[k_in].astype(F32), in_far[k_in].astype(F32)
            upper, lower = jnp.where(group[0] == 0, own, far), jnp.where(group[0] == 0, far, own)
            here = jnp.logical_or(k < 24, jnp.logical_and(k >= 48, k < 56))
            gradient = jnp.where(here, jnp.concatenate([upper, lower], axis=0), gradient)
        weight, one, two = adam(master[i], gradient, first[i], second[i], LEARN_RATE)
        weight = weight * live
        new_first[i] = one * live
        new_second[i] = two * live
        new_master[i] = weight
        new_low[i] = weight.astype(BF16)


def ring_order(chips):
    return list(range(0, chips, 2)) + list(range(chips - 1, 0, -2))


def ring_shift(x, chips, step):
    order = ring_order(chips)
    pairs = [
        (2 * order[i] + k, 2 * order[(i + step) % chips] + k) for i in range(chips) for k in range(2)
    ]
    return lax.ppermute(x, "seq", pairs)


def to_mate(x, chips):
    return lax.ppermute(x, "seq", [(i, i ^ 1) for i in range(2 * chips)])


def to_far(x):
    return lax.ppermute(x, "batch", [(0, 1), (1, 0)])


def after(x, *others):
    return lax.optimization_barrier((x, others))[0] if others else x


class RingGather:
    def __init__(self, x, chips, halves=True, cut=None):
        self.chips, self.halves = chips, halves
        self.cut = x.shape[0] // 2 if cut is None else cut
        self.pieces = [x]
        self.ahead = self.back = x
        self.left = chips // 2

    def hop(self, *gates):
        ahead, back = after((self.ahead, self.back), *gates)
        self.left -= 1
        if self.left == 0 and self.halves:
            ahead, back = ahead[: self.cut], back[self.cut :]
        self.ahead = ring_shift(ahead, self.chips, 1)
        got = [self.ahead]
        if self.left or self.halves:
            self.back = ring_shift(back, self.chips, -1)
            got.append(self.back)
        self.pieces += got
        return tuple(got)


def add_low(a, b):
    return (a.astype(F32) + b.astype(F32)).astype(BF16)


class RingSum:
    def __init__(self, parts, chips):
        self.parts, self.chips = parts, chips
        self.distance = chips // 2
        self.ahead = parts[chips - 1]
        self.back = parts[chips] if len(parts) > chips else None

    def hop(self, *gates):
        ahead, back = after((self.ahead, self.back), *gates)
        ahead = ring_shift(ahead, self.chips, 1)
        back = None if back is None else ring_shift(back, self.chips, -1)
        self.distance -= 1
        if self.distance:
            to_ahead, to_back = self.parts[2 * self.distance - 1], self.parts[2 * self.distance]
            if ahead.shape != to_ahead.shape:
                cut = ahead.shape[0]
                ahead = jnp.concatenate([add_low(ahead, to_ahead[:cut]), to_ahead[cut:]])
                back = jnp.concatenate([to_back[:cut], add_low(back, to_back[cut:])])
            else:
                ahead = add_low(ahead, to_ahead)
                back = to_back if back is None else add_low(back, to_back)
        self.ahead, self.back = ahead, back
        return ahead, back

    def terms(self):
        return self.parts[0], self.ahead, self.back


def sum_low(terms):
    return sum(term.astype(F32) for term in terms).astype(BF16)


def to_diag(x, chips):
    pairs = [(2 * i + b, 2 * (i ^ 1) + 1 - b) for i in range(2 * chips) for b in range(2)]
    return lax.ppermute(x, ("seq", "batch"), pairs)


PLAN = {
    "tables": (0, 1),
    "x_far": (0, 3),
    "pairs": (2, 4),
    "heads_far": (7, 9),
    "heads": (9, 11),
    "heads_mate": (9, 11),
    "out_grad_far": (8, 10),
    "out_grad": (9, 11),
    "ff_hop0": (4, 6),
    "ff_hop1": (11, 99),
    "ff_hop2": (12, 99),
    "ff_hop3": (13, 15),
    "six": (9, 10),
    "six_mate": (9, 8),
    "w_far0": (11, 13),
    "w_four0": (12, 13),
    "w_far1": (12, 99),
    "w_four1": (13, 15),
    "w_far2": (20, 99),
    "w_four2": (20, 99),
    "ff_parts": (19, 20),
    "ff_sum0": (19, 21),
    "ff_sum1": (21, 24),
    "ff_sum2": (27, 99),
    "ff_sum3": (27, 99),
    "small0": (20, 21),
    "small1": (30, 99),
    "small2": (30, 99),
    "small3": (32, 99),
    "small4": (33, 34),
    "att": (22, 23),
    "qkv_sum": (25, 23),
    "mixed_far": (22, 24),
    "mixed": (22, 24),
    "branch": (19, 21),
    "qkv_far": (27, 30),
    "inputs": (28, 31),
    "ff_total": (29, 31),
    "ff_far": (29, 33),
    "early": (29, 99),
}
ROOM = {'pick': {}, 'attend': {'room': 50}, 'residual': {}, 'back': {'room': 60}, 'attend_back': {}, 'ff': {'room': 60}, 'ff_weight': {'room': 60}, 'in_weight': {'room': 60}}


class Flow:
    def __init__(self, plan):
        self.plan = plan
        self.step, self.arrays = -1, ()
        self.ready, self.results = {}, {}

    def add(self, name, action):
        self.ready[name] = action
        if self.plan[name][0] <= self.step:
            self.run(name)

    def run(self, name):
        arrays = self.arrays if self.plan[name][0] == self.step else ()
        self.results[name] = self.ready.pop(name)(lambda x: after(x, *arrays))

    def get(self, name):
        if name in self.ready:
            self.run(name)
        return self.results[name]

    def cross(self, step, *arrays):
        self.step, self.arrays = step, arrays
        for name in [n for n in self.ready if self.plan[n][0] <= step]:
            self.run(name)
        waits = [self.get(n) for n, place in self.plan.items() if place[1] == step and (n in self.ready or n in self.results)]
        if waits:
            arrays = lax.optimization_barrier((arrays, waits))[0]
        return arrays if len(arrays) > 1 else arrays[0]


def fast_shards(
    frames, skip_frames, time_embed, cotangent, segments, owners, master, moment_one, moment_two,
    norm_gains, ff_biases, small_first, small_second,
):
    row_count, seg_len, width = frames.shape
    width_ff = ff_biases.shape[0] - width
    count = row_count * seg_len
    capacity = master.shape[0]
    seq_count = lax.axis_size("seq")
    chips = seq_count // 2
    half_width = width // 2
    group = lax.axis_index("batch")
    here = lax.axis_index("seq")
    chip, core = here // 2, here % 2
    order = jnp.array(ring_order(chips), jnp.int32)
    position = jnp.argmax(order == chip).astype(jnp.int32)
    rel = jnp.array([0, 1, -1, 2, -2, 3, -3, 4], jnp.int32)
    places = order[(position - rel) % chips]
    targets = order[(position + rel) % chips]
    sources = jnp.stack([2 * places + core, 2 * places + 1 - core], axis=1).reshape(-1)
    flow = Flow(PLAN)
    add, get, cross = flow.add, flow.get, flow.cross

    def by_core(own, mate):
        return jnp.where(core == 0, jnp.stack([own, mate]), jnp.stack([mate, own]))

    def pick(x, which):
        return lax.dynamic_index_in_dim(x, which, 0, False)

    def gather_four(parts):
        return [parts[0], to_far(parts[1]), to_mate(parts[2], chips), to_diag(parts[3], chips)]

    def same_four(x, far):
        return [x, far, to_mate(x, chips), to_mate(far, chips)]

    ids = jnp.arange(owners.shape[0], dtype=jnp.int32)
    slots = jnp.sum(
        ((owners[None, :] == owners[:, None]) & (ids[None, :] < ids[:, None])).astype(jnp.int32), axis=1
    )
    held = owners == group
    turned = jnp.swapaxes(master, 1, 2)
    block = turned.shape[1:]
    place = jnp.stack([group, core])
    stacks = lambda *counts: [((n,) + block, BF16) for n in counts]
    in_keep, in_send, in_give, head_own, pair_own, pair_far, pair_mate, pair_diag = kernel_call(
        pick_kernel, [((1024, block[1]), BF16)] * 2 + [((256, block[1]), BF16)] + stacks(24, 16, 16, 16, 16),
        turned, scalars=(slots, place), far_out=(3, 4, 5, 6, 7), **ROOM["pick"],
    )
    seg_own = jnp.zeros((16, 128), BF16).at[:row_count, :seg_len].set(segments.astype(BF16))
    (in_blocks,) = kernel_call(
        select_in_kernel, [((PIECE_ROWS, block[1]), BF16)],
        in_keep, to_far(in_send), to_mate(in_give, chips), to_diag(in_give, chips), seg_own, to_mate(seg_own, chips),
        scalars=(owners, place),
    )

    half_size = HEAD_DIM // 2
    spot = (sources[:, None] * seg_len + jnp.arange(seg_len, dtype=jnp.int32)[None, :]).reshape(-1).astype(F32)
    inverse = 10000.0 ** (-jnp.arange(half_size, dtype=jnp.int32).astype(F32) / half_size)
    phases = spot[:, None] * inverse[None, :]
    cosine, sine = jnp.cos(phases), jnp.sin(phases)
    cosine = jnp.concatenate([cosine, cosine], axis=1)
    sine = jnp.concatenate([-sine, sine], axis=1)
    add("tables", lambda tie: (cosine, sine))
    x_own = jnp.stack([frames.reshape(count, width), skip_frames.reshape(count, width), time_embed.reshape(count, width)])
    valid = (segments < UTTS).astype(F32).reshape(count, 1)
    grad_branch = (cotangent.reshape(count, width).astype(F32) * valid).astype(BF16)

    add("x_far", lambda tie: to_far(tie(x_own)))

    def exchange_pairs(tie):
        far, mate, diag = tie((pair_far, pair_mate, pair_diag))
        return kernel_call(
            select_pairs_kernel, [((2, 16) + block, BF16)],
            pair_own, to_far(far), to_mate(mate, chips), to_diag(diag, chips), scalars=(owners, place),
        )[0]

    add("pairs", exchange_pairs)
    add("heads_far", lambda tie: to_far(tie(head_own)))
    add("heads", lambda tie: kernel_call(
        select_heads_kernel, stacks(24), head_own, tie(get("heads_far")), scalars=(owners, place),
    )[0])
    add("heads_mate", lambda tie: to_mate(tie(get("heads")), chips))
    add("out_grad_far", lambda tie: to_far(tie(grad_branch)))
    add("out_grad", lambda tie: same_four(grad_branch, tie(get("out_grad_far"))))

    in_ring = RingGather(cross(0, in_blocks), chips, cut=PIECE_CUT)
    in_ring.hop()
    for hop in range(1, 4):
        in_ring.ahead, in_ring.back = cross(hop, in_ring.ahead, in_ring.back)
        in_ring.pieces[2 * hop - 1 : 2 * hop + 1] = [in_ring.ahead, in_ring.back]
        in_ring.hop()
    in_pieces = in_ring.pieces
    in_pieces[7:] = cross(4, *in_pieces[7:])

    ff_ring = RingGather(get("pairs"), chips, halves=False)

    def ff_hop(tie):
        ff_ring.ahead, ff_ring.back = tie((ff_ring.ahead, ff_ring.back))
        return ff_ring.hop()

    for hop in range(4):
        add("ff_hop%d" % hop, ff_hop)

    x_far = get("x_far")
    x_four = [x_own, x_far, to_mate(x_own, chips), to_mate(x_far, chips)]
    quarter_part = ((2, count, width // 4), F32)
    *trunk_parts, seg, w_zero, w_one, w_two = kernel_call(
        trunk_kernel, [quarter_part] * 4 + [((8, seq_count * seg_len), F32)] + [((width // 4, width), BF16)] * 3,
        *x_four, *in_pieces, scalars=(places,), flops=2 * 3 * 4 * count * width * width // 4, far_out=(5, 6, 7),
    )
    for t, w in enumerate((w_zero, w_one, w_two)):
        add("w_far%d" % t, lambda tie, w=w: to_far(tie(w)))
        add("w_four%d" % t, lambda tie, w=w, t=t: same_four(w, tie(get("w_far%d" % t))))
    add("six", lambda tie: kernel_call(
        assemble_out_kernel, [((width, half_width), BF16)], *tie(tuple(in_pieces)), scalars=(places, place),
    )[0])
    add("six_mate", lambda tie: to_mate(tie(get("six")), chips))
    trunk_parts = cross(5, *trunk_parts)
    trunk, gamma, normed = kernel_call(
        norm_kernel, [((count, width), F32), ((count, width), F32), ((count, width), BF16)],
        *cross(6, *gather_four(trunk_parts)), scalars=(place,), far_out=(0, 1),
    )

    normed_ring = RingGather(cross(7, normed), chips)
    normed_ring.hop()
    for hop in range(1, 4):
        normed_ring.ahead, normed_ring.back = cross(7 + hop, normed_ring.ahead, normed_ring.back)
        normed_ring.pieces[2 * hop - 1 : 2 * hop + 1] = [normed_ring.ahead, normed_ring.back]
        normed_ring.hop()
    normed_ring.pieces[7:] = cross(11, *normed_ring.pieces[7:])
    normed_pieces = normed_ring.pieces + [to_mate(piece, chips) for piece in normed_ring.pieces]

    row_len = seq_count * seg_len
    heads_out = ((3, row_count, row_len, HEAD_DIM), BF16)
    cosine, sine = get("tables")
    w_qkv = get("heads")
    qkv, mixed, normed_all = kernel_call(
        attend_kernel, [heads_out, ((seq_count, seg_len, 2 * HEAD_DIM), BF16), ((row_count * row_len, width), BF16)],
        w_qkv, cosine, sine, seg, *normed_pieces, scalars=(sources,), far_out=(0, 2), **ROOM["attend"],
        scratch=[pltpu.VMEM((row_count, row_len, HEAD_DIM), BF16)], flops=2 * 2 * row_len * (192 * width + 2 * row_len * 64),
    )
    heads = cross(13, lax.all_to_all(cross(12, mixed), "seq", 0, 0, tiled=True))
    residual, normed_two, mixed_rows = kernel_call(
        residual_kernel, [((count, width), F32), ((count, width), BF16), ((count, width), BF16)],
        heads, get("six"), get("six_mate"), trunk, norm_gains[None], scalars=(core[None],), flops=2 * count * width * width,
        far_in=(3,), far_out=(0, 2), **ROOM["residual"],
    )
    add("mixed_far", lambda tie: to_far(tie(mixed_rows)))
    add("mixed", lambda tie: same_four(mixed_rows, tie(get("mixed_far"))))

    normed_two = cross(14, normed_two)
    normed_far = to_far(normed_two)
    normed_four = cross(15, normed_two, normed_far, to_mate(normed_two, chips), to_mate(normed_far, chips))
    pair_index = 2 * group + core
    up_bias = lax.dynamic_slice_in_dim(ff_biases, pair_index * width, width, 0)[None]
    frame_part, frame_low, wide_low = ((count, width), F32), ((count, width), BF16), ((4 * count, width), BF16)
    for hop in range(4):
        get("ff_hop%d" % hop)
    grad_four = get("out_grad")
    *ff_outs, hidden, grad_pre, grad_up = kernel_call(
        forward_back_kernel, [frame_part] * 4 + [frame_low] * 4 + [wide_low, wide_low, ((1, width), F32)],
        *normed_four, *grad_four, up_bias, *ff_ring.pieces, scalars=(places,), far_in=tuple(range(17)), far_out=tuple(range(11)),
        lazy=True, **ROOM["ff"], scratch=[pltpu.VMEM((width, width), BF16)] * 2 + [pltpu.VMEM((4 * count, width), F32)],
        flops=4 * 2 * 4 * count * width * width,
    )
    add("branch", lambda tie: gather_four(tie(tuple(ff_outs[4:]))))

    def weight_parts(tie):
        return kernel_call(
            ff_weight_kernel, [((2, 16) + block, BF16)] * 8, *normed_four, *grad_four, *tie((hidden, grad_pre)),
            scalars=(targets,), flops=2 * 2 * 4 * count * width * width, far_in=tuple(range(10)), far_out=tuple(range(8)), **ROOM["ff_weight"],
        )

    add("ff_parts", weight_parts)
    grad_own, grad_far, grad_mate, grad_diag = cross(16, *ff_outs[:4])
    grad_sent = cross(17, (grad_far + to_mate(grad_diag, chips)).astype(BF16))
    grad_parts = cross(18, grad_own, to_mate(grad_mate, chips), to_far(grad_sent))
    quarter = ((count, width // 4), BF16)
    grad_res, grad_heads, grad_gains, *att_parts = kernel_call(
        back_out_kernel,
        [((count, width), F32), ((seq_count, seg_len, 2 * HEAD_DIM), BF16), ((1, width), F32)] + [quarter] * 4,
        *grad_parts, residual, norm_gains[None], grad_branch, get("six"), get("six_mate"), scalars=(place,),
        flops=2 * count * width * width, far_in=(3,), far_out=(0, 3, 4, 5, 6), **ROOM["back"],
    )
    add("att", lambda tie: gather_four(tie(tuple(att_parts))))

    grad_down = jnp.sum(grad_branch.astype(F32), axis=0)
    up_all = lax.dynamic_update_slice_in_dim(jnp.zeros((width_ff,), F32), grad_up[0], pair_index * width, 0)
    small = [jnp.concatenate([grad_gains[0], up_all, grad_down]).reshape(-1, 128)]

    def small_step(tie, bit):
        x = tie(small[-1])
        if bit == 0:
            got = to_far(x)
        else:
            got = lax.ppermute(x, "seq", [(j, j ^ bit) for j in range(seq_count)])
        small.append(x + got)
        return small[-1]

    for n, bit in enumerate((0, 1, 2, 4, 8)):
        add("small%d" % n, lambda tie, bit=bit: small_step(tie, bit))

    grad_heads = cross(19, grad_heads)
    ff_sums = []

    def ff_sum_hop(tie):
        if not ff_sums:
            ff_sums.append(RingSum(get("ff_parts"), chips))
        ring = ff_sums[0]
        if ring.back is None:
            ring.ahead = tie(ring.ahead)
        else:
            ring.ahead, ring.back = tie((ring.ahead, ring.back))
        return ring.hop()

    for hop in range(4):
        add("ff_sum%d" % hop, ff_sum_hop)
    rows_out = ((chips * count, 256), BF16)
    head_grads = cross(20, lax.all_to_all(grad_heads, "seq", 0, 0, tiled=True))
    qkv_grads, mate_grads, grad_qkv = kernel_call(
        attend_back_kernel, [rows_out, rows_out, heads_out], qkv, head_grads, cosine, sine, seg,
        scalars=(sources,), far_in=(0,), far_out=(2,), **ROOM["attend_back"],
        scratch=[pltpu.VMEM((row_count, row_len, HEAD_DIM), BF16)] + [pltpu.VMEM((row_count, row_len, HEAD_DIM), F32)] * 3,
        flops=2 * 2 * row_len * row_len * 64 * 5,
    )
    add("qkv_sum", lambda tie: kernel_call(
        qkv_weight_kernel, [((24,) + block, BF16)], *tie((grad_qkv, normed_all)), flops=2 * 2 * row_len * 192 * width,
        far_in=(0, 1), far_out=(0,),
    )[0])
    add("qkv_far", lambda tie: to_far(tie(get("qkv_sum"))))
    mate_grads = cross(21, mate_grads)
    norm_parts = kernel_call(
        back_qkv_kernel, [((row_count, seg_len, width), BF16)] * 7 + [((1, seg_len, width), BF16)] * 2,
        qkv_grads, to_mate(mate_grads, chips), w_qkv, get("heads_mate"),
        scratch=[pltpu.VMEM((512, width), BF16)], flops=2 * chips * count * 512 * width,
    )
    norm_ring = RingSum(norm_parts, chips)
    norm_ring.ahead, norm_ring.back = cross(22, norm_ring.ahead, norm_ring.back)
    norm_ring.hop()
    for hop in range(1, 4):
        norm_ring.ahead, norm_ring.back = cross(22 + hop, norm_ring.ahead, norm_ring.back)
        norm_ring.hop()
    trunk_parts = kernel_call(
        back_norm_kernel, [((2 * count, width // 4), BF16)] * 4,
        *cross(26, *norm_ring.terms()), trunk, gamma, grad_res, scalars=(place,), far_in=(3, 4, 5),
    )
    trunk_four = cross(28, *gather_four(cross(27, *trunk_parts)))

    in_parts = kernel_call(
        input_weight_kernel, [((32, 32, block[1]), BF16)] * 8,
        *x_four, *trunk_four, *get("mixed"), *get("att"), scalars=(targets,), far_in=tuple(range(16)), far_out=tuple(range(8)),
        lazy=True, **ROOM["in_weight"], scratch=[pltpu.VMEM((4, width // 4, width), BF16)], flops=2 * 4 * 4 * count * width * width // 4,
    )
    add("inputs", lambda tie: kernel_call(
        back_input_kernel, [frame_part] * 3, *tie(tuple(trunk_parts)), *[w for t in range(3) for w in get("w_four%d" % t)],
        flops=2 * 3 * count * width * width,
    ))

    def finish_ff(tie):
        for hop in range(4):
            get("ff_sum%d" % hop)
        total = sum_low(tie(ff_sums[0].terms()))
        return by_core(pick(total, core), to_mate(pick(total, 1 - core), chips)).reshape((32,) + block)

    add("ff_total", finish_ff)
    add("ff_far", lambda tie: to_far(tie(get("ff_total"))))
    in_sums = RingSum(in_parts, chips)
    in_sums.ahead, in_sums.back = cross(29, in_sums.ahead, in_sums.back)
    in_sums.hop()
    for hop in range(1, 4):
        in_sums.ahead, in_sums.back = cross(29 + hop, in_sums.ahead, in_sums.back)
        in_sums.hop()

    held_count = jnp.sum(held.astype(jnp.int32))
    match = held[None, :] & (slots[None, :] == jnp.arange(capacity, dtype=jnp.int32)[:, None])
    tile, row = ids // 8 - 7, ids % 8
    pair = tile % 4
    ff_place = 56 + 32 * (pair // 2 != group).astype(jnp.int32) + 16 * (pair % 2) + 8 * (tile // 4) + row
    source = jnp.sum(jnp.where(match, jnp.where(ids < 56, ids, ff_place)[None, :], 0), axis=1)
    stack = (capacity,) + block
    states = (turned, jnp.swapaxes(moment_one, 1, 2), jnp.swapaxes(moment_two, 1, 2))
    first_slots = 60
    per_step = math.gcd(first_slots, capacity - first_slots)

    def update(grads, start, stop, done):
        state = pl.BlockSpec((per_step,) + block, lambda i, *_: (i + start // per_step, 0, 0))
        whole = [pl.BlockSpec(g.shape, lambda i, *_, n=g.ndim: (0,) * n) for g in grads]
        return pl.pallas_call(
            functools.partial(adam_kernel, start=start, early=not done),
            grid_spec=pltpu.PrefetchScalarGridSpec(
                num_scalar_prefetch=3, grid=((stop - start) // per_step,),
                in_specs=whole + [state] * 3 + [pl.BlockSpec(memory_space=pl.ANY)] * len(done), out_specs=[state] * 4,
            ),
            out_shape=[jax.ShapeDtypeStruct(stack, F32)] * 3 + [jax.ShapeDtypeStruct(stack, BF16)],
            input_output_aliases={9 + i: i for i in range(len(done))},
            compiler_params=pltpu.CompilerParams(vmem_limit_bytes=32 * MIB),
            cost_estimate=pl.CostEstimate(flops=0, bytes_accessed=(stop - start) * 8192 * 26, transcendentals=0),
        )(source, held_count[None], group[None], *grads, *states, *done)

    def early_update(tie):
        qkv_own, ff_total = tie((get("qkv_sum"), get("ff_total")))
        rest = jnp.concatenate([add_low(qkv_own, get("qkv_far")), ff_total, get("ff_far")])
        tiny = jnp.zeros((1, 32, block[1]), BF16)
        return rest, tuple(update((tiny, tiny, rest), first_slots, capacity, ()))

    add("early", early_update)
    in_sum = cross(33, sum_low(in_sums.terms()))
    in_far = cross(34, to_far(in_sum))
    rest_grads, done = get("early")
    new_first, new_second, new_master, new_low = update((in_sum, in_far, rest_grads), 0, first_slots, done)
    back = lambda a: jnp.swapaxes(a, 1, 2)

    for n in range(5):
        get("small%d" % n)
    small_values = jnp.concatenate([norm_gains, ff_biases])
    small_new, small_one, small_two = adam(small_values, small[-1].reshape(-1), small_first, small_second, SMALL_RATE)

    branch = sum(part.astype(F32) for part in get("branch"))
    output = (residual + branch + ff_biases[None, width_ff:]) * valid
    output = output.astype(BF16).reshape(row_count, seg_len, width)
    inputs = [part.reshape(row_count, seg_len, width) for part in get("inputs")]
    return (
        output, inputs[0], inputs[1], inputs[2],
        back(new_first), back(new_second), back(new_master), back(new_low),
        small_one, small_two, small_new,
    )


def slot_places(owners, group_count, capacity):
    one_hot = (owners[:, None] == jnp.arange(group_count, dtype=jnp.int32)[None, :]).astype(
        jnp.int32
    )
    before = jnp.cumsum(one_hot, axis=0) - one_hot
    slot_index = jnp.sum(before * one_hot, axis=1)
    return owners * capacity + slot_index


def rotate(tensor, offset):
    half_size = tensor.shape[-1] // 2
    position = (offset + jnp.arange(tensor.shape[1], dtype=jnp.int32)).astype(jnp.float32)
    inverse = 10000.0 ** (-jnp.arange(half_size, dtype=jnp.int32).astype(jnp.float32) / half_size)
    phases = position[:, None] * inverse[None, :]
    cosine = jnp.cos(phases)[None, :, None, :]
    sine_part = jnp.sin(phases)[None, :, None, :]
    front_half = tensor[..., :half_size]
    back_half = tensor[..., half_size:]
    return jnp.concatenate(
        [front_half * cosine - back_half * sine_part, front_half * sine_part + back_half * cosine],
        axis=-1,
    )


def adaptive_norm(trunk, gamma_map):
    return (
        trunk
        * lax.rsqrt(jnp.mean(trunk * trunk, axis=-1, keepdims=True) + NORM_EPS)
        * (1.0 + gamma_map)
    )


def root_norm(residual, norm_gains):
    return (
        residual
        * lax.rsqrt(jnp.mean(residual * residual, axis=-1, keepdims=True) + NORM_EPS)
        * norm_gains
    )


def gelu_exact(tensor):
    return jax.nn.gelu(tensor, approximate=False)


def adam_update(weight, gradient, first_moment, second_moment, step_rate):
    first_moment = BETA_ONE * first_moment + (1.0 - BETA_ONE) * gradient
    second_moment = BETA_TWO * second_moment + (1.0 - BETA_TWO) * gradient * gradient
    fix_one = 1.0 - BETA_ONE**STEP
    fix_two = 1.0 - BETA_TWO**STEP
    update = first_moment / fix_one / (jnp.sqrt(second_moment / fix_two) + ADAM_EPS)
    return (weight - step_rate * (update + WEIGHT_DECAY * weight), first_moment, second_moment)


def matmul(former, latter):
    return jnp.dot(former, latter, preferred_element_type=jnp.float32)


def contract_rows(former, latter):
    return lax.dot_general(
        former, latter, (((0,), (0,)), ((), ())), preferred_element_type=jnp.float32
    )


def contract_cols(former, latter):
    return lax.dot_general(
        former, latter, (((1,), (1,)), ((), ())), preferred_element_type=jnp.float32
    )


def score_block(queries, key_rows, same_utt):
    scores = jnp.einsum(
        "qhd,khd->hqk", queries, key_rows, preferred_element_type=jnp.float32
    ) * HEAD_DIM ** (-0.5)
    scores = jnp.where(same_utt[None], scores, MASKED_SCORE)
    row_max = jnp.max(scores, axis=-1, keepdims=True)
    exponent = jnp.exp(scores - row_max)
    total = jnp.sum(exponent, axis=-1, keepdims=True)
    return (exponent / total, row_max[..., 0], total[..., 0])


def attend(element):
    queries, key_rows, values, same_utt = element
    attn_probs, row_max, total = score_block(queries, key_rows, same_utt)
    mixed = jnp.einsum(
        "hqk,khd->qhd", attn_probs.astype(jnp.bfloat16), values, preferred_element_type=jnp.float32
    )
    return (mixed.astype(jnp.bfloat16), attn_probs, row_max, total)


def probs_only(element):
    return score_block(element[0], element[1], element[2])


def attend_query(element):
    queries, key_rows, values, attn_probs, grad_mixed = element
    prob_grad = jnp.einsum("qhd,khd->hqk", grad_mixed, values, preferred_element_type=jnp.float32)
    inner_sum = jnp.sum(attn_probs * prob_grad, axis=-1, keepdims=True)
    score_grad = (attn_probs * (prob_grad - inner_sum)).astype(jnp.bfloat16)
    query_grad = jnp.einsum(
        "hqk,khd->qhd", score_grad, key_rows, preferred_element_type=jnp.float32
    ) * HEAD_DIM ** (-0.5)
    return (query_grad, inner_sum[..., 0])


def attend_keys(element):
    query_all, grad_all, max_all, total_all, inner_all, seg_query, key_own, value_own, seg_own = (
        element
    )
    scores = jnp.einsum(
        "qhd,khd->hqk", query_all, key_own, preferred_element_type=jnp.float32
    ) * HEAD_DIM ** (-0.5)
    same_utt = seg_query[:, None] == seg_own[None, :]
    scores = jnp.where(same_utt[None], scores, MASKED_SCORE)
    attn_probs = jnp.exp(scores - max_all[..., None]) / total_all[..., None]
    prob_grad = jnp.einsum("qhd,khd->hqk", grad_all, value_own, preferred_element_type=jnp.float32)
    score_grad = (attn_probs * (prob_grad - inner_all[..., None])).astype(jnp.bfloat16)
    key_grad = jnp.einsum(
        "hqk,qhd->khd", score_grad, query_all, preferred_element_type=jnp.float32
    ) * HEAD_DIM ** (-0.5)
    value_grad = jnp.einsum(
        "hqk,qhd->khd",
        attn_probs.astype(jnp.bfloat16),
        grad_all,
        preferred_element_type=jnp.float32,
    )
    return (key_grad, value_grad)


def general_shards(
    frames,
    skip_frames,
    time_embed,
    cotangent,
    segments,
    owners,
    master,
    moment_one,
    moment_two,
    norm_gains,
    ff_biases,
    small_first,
    small_second,
):
    row_count, seg_len, model_width = frames.shape
    width_ff = ff_biases.shape[0] - model_width
    frame_count = row_count * seg_len
    group_count = lax.axis_size("batch")
    capacity = master.shape[0]
    block_rows = master.shape[1]
    scale_in = model_width ** (-0.5)
    scale_time = 0.5 * model_width ** (-0.5)
    scale_out = 4.0 * model_width ** (-0.5)
    scale_ff = width_ff ** (-0.5)
    places = slot_places(owners, group_count, capacity)
    low_master = master.astype(jnp.bfloat16)
    all_slots = lax.all_gather(low_master, "batch", axis=0, tiled=True)
    columns = jnp.take(all_slots, places, axis=0)
    tile_stack = lax.all_gather(columns, "seq", axis=2, tiled=True).reshape(15, model_width, model_width)
    up_weight = jnp.concatenate(
        [tile_stack[7], tile_stack[8], tile_stack[9], tile_stack[10]], axis=1
    )
    down_weight = tile_stack[11:15].reshape(width_ff, model_width)
    flat_frames = frames.reshape(frame_count, model_width)
    flat_skip = skip_frames.reshape(frame_count, model_width)
    flat_time = time_embed.reshape(frame_count, model_width)
    offset = lax.axis_index("seq") * seg_len

    def rotate_here(tensor):
        return rotate(tensor, offset)

    def split_heads(tensor):
        return tensor.reshape(row_count, seg_len, HEADS, HEAD_DIM)

    trunk = (matmul(flat_frames, tile_stack[0]) + matmul(flat_skip, tile_stack[1])) * scale_in
    gamma_map = matmul(flat_time, tile_stack[2]) * scale_time
    normed_f32, norm_pull = jax.vjp(adaptive_norm, trunk, gamma_map)
    normed = normed_f32.astype(jnp.bfloat16)
    query_rot, query_pull = jax.vjp(
        rotate_here, split_heads(matmul(normed, tile_stack[3]) * scale_in)
    )
    key_rot, key_pull = jax.vjp(rotate_here, split_heads(matmul(normed, tile_stack[4]) * scale_in))
    queries = query_rot.astype(jnp.bfloat16)
    key_local = key_rot.astype(jnp.bfloat16).reshape(row_count, seg_len, model_width)
    value_local = (
        (matmul(normed, tile_stack[5]) * scale_in)
        .astype(jnp.bfloat16)
        .reshape(row_count, seg_len, model_width)
    )
    seg_low = segments.astype(jnp.bfloat16)
    key_all, value_all, seg_all = (
        lax.all_gather(key_local, "seq", axis=1, tiled=True),
        lax.all_gather(value_local, "seq", axis=1, tiled=True),
        lax.all_gather(seg_low, "seq", axis=1, tiled=True),
    )
    key_total = key_all.shape[1]
    key_heads = key_all.reshape(row_count, key_total, HEADS, HEAD_DIM)
    value_heads = value_all.reshape(row_count, key_total, HEADS, HEAD_DIM)
    same_utt = seg_low[:, :, None] == seg_all[:, None, :]
    mixed_heads, probs_kept, max_kept, total_kept = lax.map(
        attend, (queries, key_heads, value_heads, same_utt)
    )
    mixed_rows = mixed_heads.reshape(frame_count, model_width)
    residual = trunk + matmul(mixed_rows, tile_stack[6]) * scale_out
    normed_two_f32, root_pull = jax.vjp(root_norm, residual, norm_gains)
    normed_two = normed_two_f32.astype(jnp.bfloat16)
    pre_act = matmul(normed_two, up_weight) * scale_in + ff_biases[:width_ff]
    activation, gelu_pull = jax.vjp(gelu_exact, pre_act)
    hidden = activation.astype(jnp.bfloat16)
    branch = matmul(hidden, down_weight) * scale_ff + ff_biases[width_ff:]
    valid_row = (segments < UTTS).astype(jnp.float32).reshape(frame_count, 1)
    output = (
        ((residual + branch) * valid_row)
        .astype(jnp.bfloat16)
        .reshape(row_count, seg_len, model_width)
    )
    grad_out = cotangent.reshape(frame_count, model_width).astype(jnp.float32) * valid_row
    grad_branch = grad_out.astype(jnp.bfloat16)
    grad_down_bias = jnp.sum(grad_branch.astype(jnp.float32), axis=0)
    down_grads = contract_rows(hidden, grad_branch) * scale_ff
    grad_hidden = contract_cols(grad_branch, down_weight) * scale_ff
    grad_pre = gelu_pull(grad_hidden)[0].astype(jnp.bfloat16)
    grad_up_bias = jnp.sum(grad_pre.astype(jnp.float32), axis=0)
    up_grads = contract_rows(normed_two, grad_pre) * scale_in
    grad_normed_two = contract_cols(grad_pre, up_weight) * scale_in
    grad_residual_norm, grad_gains = root_pull(grad_normed_two)
    grad_residual = grad_out + grad_residual_norm
    grad_attention = grad_residual.astype(jnp.bfloat16)
    out_grads = contract_rows(mixed_rows, grad_attention) * scale_out
    grad_mixed = (contract_cols(grad_attention, tile_stack[6]) * scale_out).astype(jnp.bfloat16)
    grad_mixed = grad_mixed.reshape(row_count, seg_len, HEADS, HEAD_DIM)
    key_again, value_again, seg_again = (
        lax.all_gather(key_local, "seq", axis=1, tiled=True),
        lax.all_gather(value_local, "seq", axis=1, tiled=True),
        lax.all_gather(seg_low, "seq", axis=1, tiled=True),
    )
    back_keys = key_again.reshape(row_count, key_total, HEADS, HEAD_DIM)
    back_values = value_again.reshape(row_count, key_total, HEADS, HEAD_DIM)
    same_again = seg_low[:, :, None] == seg_again[:, None, :]
    back_probs, back_max, back_total = lax.map(probs_only, (queries, back_keys, same_again))
    query_raw, inner_sum = lax.map(
        attend_query, (queries, back_keys, back_values, back_probs, grad_mixed)
    )
    query_all, grad_all = (
        lax.all_gather(queries, "seq", axis=1, tiled=True),
        lax.all_gather(grad_mixed, "seq", axis=1, tiled=True),
    )
    max_all, total_all, inner_all = (
        lax.all_gather(back_max, "seq", axis=2, tiled=True),
        lax.all_gather(back_total, "seq", axis=2, tiled=True),
        lax.all_gather(inner_sum, "seq", axis=2, tiled=True),
    )
    key_own = key_local.reshape(row_count, seg_len, HEADS, HEAD_DIM)
    value_own = value_local.reshape(row_count, seg_len, HEADS, HEAD_DIM)
    key_sum, value_sum = lax.map(
        attend_keys,
        (
            query_all,
            grad_all,
            max_all,
            total_all,
            inner_all,
            seg_again,
            key_own,
            value_own,
            seg_low,
        ),
    )
    grad_q = query_pull(query_raw)[0].reshape(frame_count, model_width).astype(jnp.bfloat16)
    grad_k = key_pull(key_sum)[0].reshape(frame_count, model_width).astype(jnp.bfloat16)
    grad_v = value_sum.reshape(frame_count, model_width).astype(jnp.bfloat16)
    query_grads = contract_rows(normed, grad_q) * scale_in
    key_grads = contract_rows(normed, grad_k) * scale_in
    value_grads = contract_rows(normed, grad_v) * scale_in
    grad_normed = (
        contract_cols(grad_q, tile_stack[3])
        + contract_cols(grad_k, tile_stack[4])
        + contract_cols(grad_v, tile_stack[5])
    ) * scale_in
    grad_trunk_norm, grad_gamma_f32 = norm_pull(grad_normed)
    grad_trunk = (grad_residual + grad_trunk_norm).astype(jnp.bfloat16)
    grad_gamma = grad_gamma_f32.astype(jnp.bfloat16)
    frame_grads = contract_rows(flat_frames, grad_trunk) * scale_in
    skip_grads = contract_rows(flat_skip, grad_trunk) * scale_in
    time_grads = contract_rows(flat_time, grad_gamma) * scale_time
    grad_frames = (contract_cols(grad_trunk, tile_stack[0]) * scale_in).reshape(
        row_count, seg_len, model_width
    )
    grad_skip = (contract_cols(grad_trunk, tile_stack[1]) * scale_in).reshape(
        row_count, seg_len, model_width
    )
    grad_time = (contract_cols(grad_gamma, tile_stack[2]) * scale_time).reshape(
        row_count, seg_len, model_width
    )
    first_tiles = jnp.stack(
        [frame_grads, skip_grads, time_grads, query_grads, key_grads, value_grads, out_grads]
    )
    up_tiles = up_grads.reshape(model_width, 4, model_width).transpose(1, 0, 2)
    down_tiles = down_grads.reshape(4, model_width, model_width)
    blocks = jnp.concatenate([first_tiles, up_tiles, down_tiles], axis=0).reshape(
        -1, block_rows, model_width
    )
    block_count = blocks.shape[0]
    partial_cols = lax.psum_scatter(
        blocks.astype(jnp.bfloat16), "seq", scatter_dimension=2, tiled=True
    )
    matches = places[None, :] == jnp.arange(group_count * capacity, dtype=jnp.int32)[:, None]
    source = jnp.sum(
        jnp.where(matches, jnp.arange(block_count, dtype=jnp.int32)[None, :], 0), axis=1
    )
    filled = jnp.any(matches, axis=1)
    placed = jnp.where(filled[:, None, None], jnp.take(partial_cols, source, axis=0), 0)
    reduced = lax.psum_scatter(placed, "batch", scatter_dimension=0, tiled=True).astype(
        jnp.float32
    )
    small_grad = jnp.concatenate([grad_gains, grad_up_bias, grad_down_bias])
    small_grad = lax.psum(small_grad, ("seq", "batch"))
    owner_index = lax.axis_index("batch")
    held_count = jnp.sum((owners == owner_index).astype(jnp.int32))
    live_slot = (jnp.arange(capacity, dtype=jnp.int32) < held_count).astype(jnp.float32)[
        :, None, None
    ]
    new_master, new_first, new_second = adam_update(
        master, reduced, moment_one, moment_two, LEARN_RATE
    )
    new_master = new_master * live_slot
    new_first = new_first * live_slot
    new_second = new_second * live_slot
    small_values = jnp.concatenate([norm_gains, ff_biases])
    small_new, small_first_new, small_second_new = adam_update(
        small_values, small_grad, small_first, small_second, SMALL_RATE
    )
    return (
        output,
        grad_frames,
        grad_skip,
        grad_time,
        new_first,
        new_second,
        new_master,
        new_master.astype(jnp.bfloat16),
        small_first_new,
        small_second_new,
        small_new,
    )


def solution(mesh):
    fast = mesh.shape["seq"] == HEADS and mesh.shape["batch"] == 2
    rows, slots, whole = P("batch", "seq", None), P("batch", None, "seq"), P()
    return jax.shard_map(
        fast_shards if fast else general_shards,
        mesh=mesh,
        in_specs=(rows, rows, rows, rows, P("batch", "seq"), whole, slots, slots, slots, whole, whole, whole, whole),
        out_specs=(rows, rows, rows, rows, slots, slots, slots, slots, whole, whole, whole),
        check_vma=False,
    )
```

```python
import functools
import math

import jax
import jax.numpy as jnp
from jax import lax
from jax.experimental import pallas as pl
from jax.experimental.pallas import tpu as pltpu
from jax.sharding import PartitionSpec as P

HEADS = 16
HEAD_DIM = 64
UTTS = 8
STEP = 10
NORM_EPS = 1e-06
MASKED_SCORE = -1e30
BETA_ONE = 0.9
BETA_TWO = 0.999
ADAM_EPS = 1e-08
WEIGHT_DECAY = 0.01
LEARN_RATE = 1.0
SMALL_RATE = 0.1

F32 = jnp.float32
BF16 = jnp.bfloat16
MIB = 1 << 20


def padded(shape, dtype):
    size = jnp.dtype(dtype).itemsize
    rows = 32 // size
    shape = (1,) * (2 - len(shape)) + tuple(shape)
    return math.prod(shape[:-2]) * (-(-shape[-2] // rows) * rows) * (-(-shape[-1] // 128) * 128) * size


def kernel_call(body, outs, *args, scalars=(), scratch=(), room=10, flops=0, far_in=(), far_out=(), lazy=False):
    n_in, n_out = len(args), len(outs)
    vmem, hbm = pl.BlockSpec(memory_space=pltpu.VMEM), pl.BlockSpec(memory_space=pltpu.HBM)
    specs = [pl.BlockSpec(memory_space=pltpu.SMEM) for _ in scalars]
    specs += [hbm if i in far_in else vmem for i in range(n_in)]
    moved = sum(padded(a.shape, a.dtype) for a in args) + sum(padded(s, d) for s, d in outs)
    held = moved + sum(padded(ref.shape, ref.dtype) for ref in scratch)
    far = [pltpu.VMEM(args[i].shape, args[i].dtype) for i in far_in] + [pltpu.VMEM(*outs[i]) for i in far_out]
    copies = [pltpu.SemaphoreType.DMA((len(far),))] if far else []

    def whole(*refs):
        refs = list(refs)
        first = len(scalars)
        if far:
            sems = refs.pop()
            held_refs = refs[len(refs) - len(far) :]
            refs = refs[: len(refs) - len(far)]
            pairs = []
            for n, i in enumerate(far_in):
                pairs.append(pltpu.make_async_copy(refs[first + i], held_refs[n], sems.at[n]))
                refs[first + i] = held_refs[n]
            results = []
            for n, i in enumerate(far_out, len(far_in)):
                results.append(pltpu.make_async_copy(held_refs[n], refs[first + n_in + i], sems.at[n]))
                refs[first + n_in + i] = held_refs[n]
            for copy in pairs:
                copy.start()
            if not lazy:
                for copy in pairs:
                    copy.wait()
        if lazy:
            body(*refs, wait=lambda i: pairs[far_in.index(i)].wait())
        else:
            body(*refs)
        if far:
            for copy in results:
                copy.start()
            for copy in results:
                copy.wait()

    return pl.pallas_call(
        whole,
        out_shape=[jax.ShapeDtypeStruct(shape, dtype) for shape, dtype in outs],
        in_specs=specs,
        out_specs=[hbm if i in far_out else vmem for i in range(n_out)],
        scratch_shapes=list(scratch) + far + copies,
        compiler_params=pltpu.CompilerParams(vmem_limit_bytes=min(held + room * MIB, 58 * MIB)),
        cost_estimate=pl.CostEstimate(flops=int(flops), bytes_accessed=int(moved), transcendentals=0),
    )(*scalars, *args)


def dot_nn(a, b):
    return jnp.dot(a, b, preferred_element_type=F32)


def dot_nt(a, b):
    return lax.dot_general(a, b, (((1,), (1,)), ((), ())), preferred_element_type=F32)


def dot_tn(a, b):
    return lax.dot_general(a, b, (((0,), (0,)), ((), ())), preferred_element_type=F32)


def lanes(blocks):
    return jnp.concatenate(blocks, axis=-1)


def at128(index):
    return pl.multiple_of(index * 128, 128)


def normal_cdf(x):
    return 0.5 * (1.0 + lax.erf(x * (2.0**-0.5)))


OUT_ROWS, SEG_ROWS, PIECE_ROWS, PIECE_CUT = 768, 1280, 1312, 640


def pick_kernel(slots, place, master, keep, far_send, give, heads, pair_own, pair_far, pair_mate, pair_diag):
    group, core = place[0], place[1]

    def low(k):
        return master[slots[k]].astype(BF16)

    def tile_pair(pair, j):
        return low((7 + pair) * 8 + j), low((11 + pair) * 8 + j)

    mine = pl.ds(pl.multiple_of(32 * group, 32), 32)
    other = pl.ds(pl.multiple_of(32 - 32 * group, 32), 32)
    for k in range(24):
        keep[32 * k : 32 * k + 32] = master[slots[k], mine].astype(BF16)
        far_send[32 * k : 32 * k + 32] = master[slots[k], other].astype(BF16)
    for j in range(4):
        rows = slice(OUT_ROWS + 64 * j, OUT_ROWS + 64 * j + 64)
        block = low(48 + 4 * core + j)
        keep[rows] = block
        far_send[rows] = block
        give[64 * j : 64 * j + 64] = low(52 - 4 * core + j)
    for k in range(24):
        heads[k] = low(24 + k)
    for j in range(8):
        pair_far[j], pair_far[8 + j] = tile_pair(2 - 2 * group + core, j)
        pair_own[j], pair_own[8 + j] = tile_pair(2 * group + core, j)
        pair_mate[j], pair_mate[8 + j] = tile_pair(2 * group + 1 - core, j)
        pair_diag[j], pair_diag[8 + j] = tile_pair(3 - 2 * group - core, j)


def select_in_kernel(held, place, own, far, mate, diag, seg_own, seg_mate, out):
    group, core = place[0], place[1]
    for k in range(24):
        rows = slice(32 * k, 32 * k + 32)
        out[rows] = jnp.where(held[k] == group, own[rows], far[rows])
    for j in range(4):
        mine = held[48 + 4 * core + j] == group
        rows, part = slice(OUT_ROWS + 64 * j, OUT_ROWS + 64 * j + 64), slice(64 * j, 64 * j + 64)
        out[rows] = jnp.where(mine, own[rows], far[rows])
        out[OUT_ROWS + 256 + 64 * j : OUT_ROWS + 320 + 64 * j] = jnp.where(mine, mate[part], diag[part])
    out[SEG_ROWS : SEG_ROWS + 16] = seg_own[...]
    out[SEG_ROWS + 16 : SEG_ROWS + 32] = seg_mate[...]


def select_heads_kernel(held, place, own, far, out):
    for k in range(24):
        out[k] = jnp.where(held[24 + k] == place[0], own[k], far[k])


def select_pairs_kernel(held, place, own, far, mate, diag, out):
    group, core = place[0], place[1]
    for half, first in ((0, 7), (1, 11)):
        for j in range(8):
            k = 8 * half + j
            mine = held[(first + 2 * group + core) * 8 + j] == group
            out[core, k] = jnp.where(mine, own[k], far[k])
            out[1 - core, k] = jnp.where(mine, mate[k], diag[k])


def ring_readers(refs):
    def last(first, count):
        if first < PIECE_CUT:
            return refs[7][first : first + count, :]
        return refs[8][first - PIECE_CUT : first - PIECE_CUT + count, :]

    return [lambda first, count, r=r: r[first : first + count, :] for r in refs[:7]] + [last]


def ring_blocks(refs):
    return [lambda s, k, r=r: r[s, k] for r in refs]


def trunk_kernel(places, own_x, far_x, mate_x, diag_x, *refs):
    pieces, outs, seg_out, weight = ring_readers(refs[:9]), refs[9:13], refs[13], refs[14:]
    width = own_x.shape[-1]
    count = own_x.shape[1]
    scale_in = width**-0.5
    for p, piece in enumerate(pieces):
        rows = pl.ds(pl.multiple_of(32 * places[p], 32), 32)
        for t in range(3):
            for j in range(8):
                weight[t][rows, 128 * j : 128 * j + 128] = piece(256 * t + 32 * j, 32)
        ids = [piece(SEG_ROWS + 16 * m, 16).astype(F32)[0:8, 0:64] for m in range(2)]
        seg_out[:, 128 * p : 128 * p + 128] = lanes(ids)
    x = [jnp.concatenate([ref[t] for ref in (own_x, far_x, mate_x, diag_x)], axis=0) for t in range(3)]
    trunk = (dot_nt(x[0], weight[0][...]) + dot_nt(x[1], weight[1][...])) * scale_in
    gamma = dot_nt(x[2], weight[2][...]) * (0.5 * scale_in)
    for i, out in enumerate(outs):
        out[0] = trunk[i * count : i * count + count]
        out[1] = gamma[i * count : i * count + count]


def assemble_out_kernel(places, place, *refs):
    out = refs[9]
    core = place[1]
    for p, piece in enumerate(ring_readers(refs[:9])):
        for m in range(2):
            column = 64 * core if m == 0 else 64 - 64 * core
            rows = pl.ds(pl.multiple_of(places[p] * 128 + column, 64), 64)
            for j in range(4):
                out[rows, 128 * j : 128 * j + 128] = piece(OUT_ROWS + 256 * m + 64 * j, 64)


def by_quarter(parts, mine):
    found = []
    for q in range(4):
        low = jnp.where(mine == 0, parts[q], parts[q ^ 1])
        high = jnp.where(mine == 2, parts[q ^ 2], parts[q ^ 3])
        found.append(jnp.where(mine < 2, low, high))
    return found


def norm_kernel(place, own, far, mate, diag, trunk_out, gamma_out, normed_out):
    mine = 2 * place[1] + place[0]
    for i, out in enumerate((trunk_out, gamma_out)):
        parts = by_quarter([ref[i] for ref in (own, far, mate, diag)], mine)
        for c in range(8):
            out[:, 128 * c : 128 * c + 128] = lanes([part[:, 32 * c : 32 * c + 32] for part in parts])
    trunk = trunk_out[...]
    scale = lax.rsqrt(jnp.mean(trunk * trunk, axis=-1, keepdims=True) + NORM_EPS)
    normed_out[...] = (trunk * scale * (1.0 + gamma_out[...])).astype(BF16)


def swap_halves(x):
    half = HEAD_DIM // 2
    return jnp.concatenate([x[:, half:], x[:, :half]], axis=1)


def frame_rows(refs, p, m):
    base = 9 * m
    if p < 7:
        return refs[base + p][...]
    return jnp.concatenate([refs[base + 7][...], refs[base + 8][...]], axis=0)


def attend_kernel(sources, weight, cosine, sine, seg, *refs):
    normed = refs[:18]
    qkv_ref, out_ref, x_ref, mixed = refs[18:]
    q_ref, k_ref, v_ref = (qkv_ref.at[t] for t in range(3))
    width = normed[0].shape[1]
    scale_in = width**-0.5
    w = jnp.concatenate(
        [lanes([weight[8 * t + j] for j in range(8)]) for t in range(3)], axis=0
    )
    row_len = q_ref.shape[1]
    for p in range(8):
        for m in range(2):
            u = 2 * p + m
            spot = pl.ds(u * 64, 64)
            rows = frame_rows(normed, p, m)
            for r in range(2):
                x_ref[pl.ds(r * row_len + u * 64, 64)] = rows[64 * r : 64 * r + 64]
            qkv = dot_nt(rows, w) * scale_in
            c, s = cosine[spot], sine[spot]
            for r in range(2):
                part = qkv[64 * r : 64 * r + 64]
                for ref, lo, scale in ((q_ref, 0, HEAD_DIM**-0.5), (k_ref, 64, 1.0)):
                    x = part[:, lo : lo + 64]
                    ref[r, spot] = ((x * c + swap_halves(x) * s) * scale).astype(BF16)
                v_ref[r, spot] = part[:, 128:192].astype(BF16)
    block = 256
    seg_cols = jnp.transpose(seg[...])
    for r in range(2):
        key, value = k_ref[r], v_ref[r]
        seg_keys = seg[r : r + 1, :]
        for q in range(row_len // block):
            spot = pl.ds(q * block, block)
            scores = dot_nt(q_ref[r, spot], key)
            same = seg_cols[q * block : q * block + block, r : r + 1] == seg_keys
            scores = jnp.where(same, scores, MASKED_SCORE)
            top = jnp.max(scores, axis=-1, keepdims=True)
            exponent = jnp.exp(scores - top)
            total = jnp.sum(exponent, axis=-1, keepdims=True)
            probs = (exponent * (1.0 / total)).astype(BF16)
            mixed[r, spot] = dot_nn(probs, value).astype(BF16)
    for u in range(16):
        spot = pl.ds(u * 64, 64)
        out_ref[sources[u]] = lanes([mixed[0, spot], mixed[1, spot]])


def residual_kernel(core, heads, w_own, w_mate, trunk, gains, res_out, normed_out, mixed_out):
    scale_out = 4.0 * trunk.shape[1] ** -0.5
    for r in range(2):
        for j in range(8):
            pair = [heads[2 * j + i][:, 64 * r : 64 * r + 64] for i in range(2)]
            mixed_out[64 * r : 64 * r + 64, 128 * j : 128 * j + 128] = lanes(pair)
    here = pl.ds(pl.multiple_of(core[0] * 512, 512), 512)
    there = pl.ds(pl.multiple_of(512 - core[0] * 512, 512), 512)
    attention = dot_nt(mixed_out[:, here], w_own[...]) + dot_nt(mixed_out[:, there], w_mate[...])
    residual = trunk[...] + attention * scale_out
    res_out[...] = residual
    scale = lax.rsqrt(jnp.mean(residual * residual, axis=-1, keepdims=True) + NORM_EPS)
    normed_out[...] = (residual * scale * gains[...]).astype(BF16)


def forward_back_kernel(places, *refs, wait):
    normed, grad, bias, pieces, refs = refs[:4], refs[4:8], refs[8], ring_blocks(refs[9:17]), refs[17:]
    grad_in, branch, (hidden_out, pre_out, bias_out, w_up, w_down, branch_acc) = refs[:4], refs[4:8], refs[8:]
    width = w_up.shape[1]
    count = normed[0].shape[0]
    scale_in = width**-0.5
    scale_ff = (4 * width) ** -0.5
    for p, piece in enumerate(pieces):
        wait(9 + p)
        for s in range(2):
            rows = pl.ds(pl.multiple_of(places[p] * 128 + 64 * s, 64), 64)
            for j in range(8):
                w_up[rows, 128 * j : 128 * j + 128] = piece(s, j)
                w_down[rows, 128 * j : 128 * j + 128] = piece(s, 8 + j)
    for i in range(9):
        wait(i)
    x = jnp.concatenate([ref[...] for ref in normed], axis=0)
    g = jnp.concatenate([ref[...] for ref in grad], axis=0)
    block = 256
    for h in range(width // block):
        spot = slice(h * block, h * block + block)
        pre = dot_nt(x, w_up[spot, :]) * scale_in + bias[:, spot]
        cdf = normal_cdf(pre)
        hidden = (pre * cdf).astype(BF16)
        slope = cdf + pre * (jnp.exp(-0.5 * pre * pre) * (2.0 * math.pi) ** -0.5)
        grad_pre = slope * (dot_nn(g, w_down[:, spot]) * scale_ff)
        grad_pre = grad_pre.astype(BF16)
        hidden_out[:, spot] = hidden
        pre_out[:, spot] = grad_pre
        bias_out[:, spot] = jnp.sum(grad_pre.astype(F32), axis=0, keepdims=True)
        grad_part = dot_nn(grad_pre, w_up[spot, :]) * scale_in
        out_part = dot_nt(hidden, w_down[:, spot]) * scale_ff
        for i in range(4):
            rows = slice(i * count, i * count + count)
            if h == 0:
                grad_in[i][...] = grad_part[rows]
            else:
                grad_in[i][...] += grad_part[rows]
        if h == 0:
            branch_acc[...] = out_part
        else:
            branch_acc[...] += out_part
    for i in range(4):
        branch[i][...] = branch_acc[i * count : i * count + count, :].astype(BF16)


def ff_weight_kernel(targets, *refs):
    normed, grad, (hidden, pre), outs = refs[:4], refs[4:8], refs[8:10], refs[10:]
    width = hidden.shape[1]
    scale_in = width**-0.5
    scale_ff = (4 * width) ** -0.5
    x = jnp.concatenate([ref[...] for ref in normed], axis=0)
    for p in range(8):
        spot = pl.ds(at128(targets[p]), 128)
        g = jnp.concatenate([ref[:, spot] for ref in grad], axis=0)
        up = (dot_tn(pre[:, spot], x) * scale_in).astype(BF16)
        down = (dot_tn(g, hidden[...]) * scale_ff).astype(BF16)
        for s in range(2):
            rows = slice(64 * s, 64 * s + 64)
            for j in range(8):
                outs[p][s, j] = up[rows, 128 * j : 128 * j + 128]
                outs[p][s, 8 + j] = down[rows, 128 * j : 128 * j + 128]


def quarters(x, mine, outs):
    parts = [lanes([x[:, 128 * c + 32 * q : 128 * c + 32 * q + 32] for c in range(x.shape[1] // 128)]) for q in range(4)]
    for out, part in zip(outs, by_quarter(parts, mine)):
        out[...] = part


def back_out_kernel(place, grad_own, grad_mate, grad_far, residual, gains, grad_out, w_own, w_mate, grad_res, heads, gain_out, *att):
    width = residual.shape[1]
    g = grad_own[...] + grad_mate[...] + grad_far[...].astype(F32)
    x = residual[...]
    scale = lax.rsqrt(jnp.mean(x * x, axis=-1, keepdims=True) + NORM_EPS)
    gain_out[...] = jnp.sum(g * x * scale, axis=0, keepdims=True)
    inner = g * gains[...]
    slope = inner * scale - x * (scale * scale * scale * jnp.mean(inner * x, axis=-1, keepdims=True))
    total = grad_out[...].astype(F32) + slope
    grad_res[...] = total
    low = total.astype(BF16)
    quarters(low, 2 * place[1] + place[0], att)
    halves = [dot_nn(low, w[...]) * (4.0 * width**-0.5) for w in (w_own, w_mate)]
    mixed = jnp.where(place[1] == 0, lanes(halves), lanes(halves[::-1])).astype(BF16)
    for j in range(8):
        rows = [mixed[64 * r : 64 * r + 64, 128 * j : 128 * j + 128] for r in range(2)]
        heads[2 * j] = lanes([rows[0][:, :64], rows[1][:, :64]])
        heads[2 * j + 1] = lanes([rows[0][:, 64:], rows[1][:, 64:]])


def attend_back_kernel(sources, qkv_ref, grads, cosine, sine, seg, own_out, mate_out, done_ref, g_ref, acc_q, acc_k, acc_v):
    q_ref, k_ref, v_ref = (qkv_ref.at[t] for t in range(3))
    dq_ref, dk_ref, dv_ref = (done_ref.at[t] for t in range(3))
    row_len = q_ref.shape[1]
    for u in range(16):
        spot = pl.ds(u * 64, 64)
        both = grads[sources[u]]
        g_ref[0, spot] = both[:, :64]
        g_ref[1, spot] = both[:, 64:]
    block = 256
    seg_cols = jnp.transpose(seg[...])
    for r in range(2):
        key, value = k_ref[r], v_ref[r]
        for q in range(row_len // block):
            spot = pl.ds(q * block, block)
            query, grad = q_ref[r, spot], g_ref[r, spot]
            scores = dot_nt(key, query)
            same = seg_cols[:, r : r + 1] == seg[r : r + 1, q * block : q * block + block]
            scores = jnp.where(same, scores, MASKED_SCORE)
            top = jnp.max(scores, axis=0, keepdims=True)
            exponent = jnp.exp(scores - top)
            total = jnp.sum(exponent, axis=0, keepdims=True)
            probs = exponent * (1.0 / total)
            prob_grad = dot_nt(value, grad)
            inner = jnp.sum(probs * prob_grad, axis=0, keepdims=True)
            score_grad = (probs * (prob_grad - inner)).astype(BF16)
            acc_q[r, spot] = dot_tn(score_grad, key)
            key_part = dot_nn(score_grad, query)
            value_part = dot_nn(probs.astype(BF16), grad)
            if q == 0:
                acc_k[r] = key_part
                acc_v[r] = value_part
            else:
                acc_k[r] += key_part
                acc_v[r] += value_part
        c, s = cosine[...], sine[...]
        for ref, acc, scale in ((dq_ref, acc_q, HEAD_DIM**-0.5), (dk_ref, acc_k, 1.0)):
            g = acc[r] * scale
            ref[r] = (g * c + swap_halves(g * s)).astype(BF16)
        dv_ref[r] = acc_v[r].astype(BF16)
    empty = jnp.zeros((64, HEAD_DIM), BF16)
    for p in range(8):
        for m, out in enumerate((own_out, mate_out)):
            spot = pl.ds((2 * p + m) * 64, 64)
            for r in range(2):
                rows = pl.ds(128 * p + 64 * r, 64)
                out[rows, 0:128] = lanes([dq_ref[r, spot], dk_ref[r, spot]])
                out[rows, 128:256] = lanes([dv_ref[r, spot], empty])


def qkv_weight_kernel(done_ref, x_ref, out):
    dq_ref, dk_ref, dv_ref = (done_ref.at[t] for t in range(3))
    width = x_ref.shape[1]
    rows = lambda ref: jnp.concatenate([ref[0], ref[1]], axis=0)
    both = [lanes([rows(dq_ref), rows(dk_ref)]), rows(dv_ref)]
    for t in range(2):
        grads = (dot_tn(both[t], x_ref[...]) * width**-0.5).astype(BF16)
        for i in range(2 - t):
            for j in range(8):
                out[16 * t + 8 * i + j] = grads[64 * i : 64 * i + 64, 128 * j : 128 * j + 128]


MIRROR = (0, 2, 1, 4, 3, 6, 5, 7)


def back_qkv_kernel(own_y, mate_y, own_w, mate_w, *refs):
    outs, w = refs[:9], refs[9]
    width = w.shape[1]
    for h, weight in enumerate((own_w, mate_w)):
        for j in range(8):
            spot = slice(128 * j, 128 * j + 128)
            for t in range(3):
                w[256 * h + 64 * t : 256 * h + 64 * t + 64, spot] = weight[8 * t + j]
            w[256 * h + 192 : 256 * h + 256, spot] = jnp.zeros((64, 128), BF16)
    for i, p in enumerate(MIRROR):
        rows = slice(128 * p, 128 * p + 128)
        part = (dot_nn(lanes([own_y[rows], mate_y[rows]]), w[...]) * width**-0.5).astype(BF16)
        for r in range(2):
            half = part[64 * r : 64 * r + 64]
            if i < 7:
                outs[i][r] = half
            else:
                outs[7 + r][0] = half


def back_norm_kernel(place, one, two, three, trunk, gamma, grad_res, *parts):
    sums = one[...].astype(F32) + two[...].astype(F32) + three[...].astype(F32)
    g = jnp.concatenate([sums[0], sums[1]], axis=0)
    x = trunk[...]
    scale = lax.rsqrt(jnp.mean(x * x, axis=-1, keepdims=True) + NORM_EPS)
    inner = g * (1.0 + gamma[...])
    slope = inner * scale - x * (scale * scale * scale * jnp.mean(inner * x, axis=-1, keepdims=True))
    grad_trunk = (grad_res[...] + slope).astype(BF16)
    grad_gamma = (g * (x * scale)).astype(BF16)
    both = jnp.concatenate([grad_trunk, grad_gamma], axis=0)
    quarters(both, 2 * place[1] + place[0], parts)


def input_weight_kernel(targets, *refs, wait):
    x_refs, y_refs, m_refs, a_refs, refs = refs[:4], refs[4:8], refs[8:12], refs[12:16], refs[16:]
    outs, done = refs[:8], refs[8]
    count, width = m_refs[0].shape
    scale_in = width**-0.5
    stacked = lambda refs, cut: jnp.concatenate([ref[cut] for ref in refs], axis=0)
    for i in range(8, 16):
        wait(i)
    done[3] = (dot_tn(stacked(a_refs, slice(None)), stacked(m_refs, slice(None))) * (4.0 * scale_in)).astype(BF16)
    for i in range(8):
        wait(i)
    trunk_grads = stacked(y_refs, slice(0, count))
    gamma_grads = stacked(y_refs, slice(count, 2 * count))
    done[0] = (dot_tn(trunk_grads, stacked(x_refs, 0)) * scale_in).astype(BF16)
    done[1] = (dot_tn(trunk_grads, stacked(x_refs, 1)) * scale_in).astype(BF16)
    done[2] = (dot_tn(gamma_grads, stacked(x_refs, 2)) * (0.5 * scale_in)).astype(BF16)
    for p in range(8):
        rows = pl.ds(pl.multiple_of(targets[p] * 32, 32), 32)
        for t in range(4):
            for j in range(8):
                value = done[t, rows, 128 * j : 128 * j + 128]
                outs[p][8 * t + j] = value


def back_input_kernel(*refs):
    y_refs, w_refs, outs = refs[:4], refs[4:16], refs[16:]
    count, width = outs[0].shape
    scale_in = width**-0.5
    for t, out in enumerate(outs):
        rows = slice(0, count) if t < 2 else slice(count, 2 * count)
        total = dot_nn(y_refs[0][rows], w_refs[4 * t][...])
        for r in range(1, 4):
            total += dot_nn(y_refs[r][rows], w_refs[4 * t + r][...])
        out[...] = total * (scale_in if t < 2 else 0.5 * scale_in)


def adam(weight, gradient, first, second, rate):
    first = BETA_ONE * first + (1.0 - BETA_ONE) * gradient
    second = BETA_TWO * second + (1.0 - BETA_TWO) * gradient * gradient
    fix_one = 1.0 - BETA_ONE**STEP
    fix_two = 1.0 - BETA_TWO**STEP
    update = first / fix_one / (jnp.sqrt(second / fix_two) + ADAM_EPS)
    return weight - rate * (update + WEIGHT_DECAY * weight), first, second


def adam_kernel(source, held, group, in_own, in_far, rest, master, first, second, *refs, start, early):
    new_first, new_second, new_master, new_low = refs[-4:]
    step = pl.program_id(0)
    count = master.shape[0]
    for i in range(count):
        slot = start + step * count + i
        k = source[slot]
        live = (slot < held[0]).astype(F32)
        gradient = rest[jnp.where(k < 48, jnp.maximum(k - 24, 0), jnp.maximum(k - 32, 24))].astype(F32)
        if not early:
            k_in = jnp.where(k < 24, k, jnp.clip(k - 24, 24, 31))
            own, far = in_own[k_in].astype(F32), in_far[k_in].astype(F32)
            upper, lower = jnp.where(group[0] == 0, own, far), jnp.where(group[0] == 0, far, own)
            here = jnp.logical_or(k < 24, jnp.logical_and(k >= 48, k < 56))
            gradient = jnp.where(here, jnp.concatenate([upper, lower], axis=0), gradient)
        weight, one, two = adam(master[i], gradient, first[i], second[i], LEARN_RATE)
        weight = weight * live
        new_first[i] = one * live
        new_second[i] = two * live
        new_master[i] = weight
        new_low[i] = weight.astype(BF16)


def ring_order(chips):
    return list(range(0, chips, 2)) + list(range(chips - 1, 0, -2))


def ring_shift(x, chips, step):
    order = ring_order(chips)
    pairs = [
        (2 * order[i] + k, 2 * order[(i + step) % chips] + k) for i in range(chips) for k in range(2)
    ]
    return lax.ppermute(x, "seq", pairs)


def to_mate(x, chips):
    return lax.ppermute(x, "seq", [(i, i ^ 1) for i in range(2 * chips)])


def to_far(x):
    return lax.ppermute(x, "batch", [(0, 1), (1, 0)])


def after(x, *others):
    return lax.optimization_barrier((x, others))[0] if others else x


class RingGather:
    def __init__(self, x, chips, halves=True, cut=None):
        self.chips, self.halves = chips, halves
        self.cut = x.shape[0] // 2 if cut is None else cut
        self.pieces = [x]
        self.ahead = self.back = x
        self.left = chips // 2

    def hop(self, *gates):
        ahead, back = after((self.ahead, self.back), *gates)
        self.left -= 1
        if self.left == 0 and self.halves:
            ahead, back = ahead[: self.cut], back[self.cut :]
        self.ahead = ring_shift(ahead, self.chips, 1)
        got = [self.ahead]
        if self.left or self.halves:
            self.back = ring_shift(back, self.chips, -1)
            got.append(self.back)
        self.pieces += got
        return tuple(got)


def add_low(a, b):
    return (a.astype(F32) + b.astype(F32)).astype(BF16)


class RingSum:
    def __init__(self, parts, chips):
        self.parts, self.chips = parts, chips
        self.distance = chips // 2
        self.ahead = parts[chips - 1]
        self.back = parts[chips] if len(parts) > chips else None

    def hop(self, *gates):
        ahead, back = after((self.ahead, self.back), *gates)
        ahead = ring_shift(ahead, self.chips, 1)
        back = None if back is None else ring_shift(back, self.chips, -1)
        self.distance -= 1
        if self.distance:
            to_ahead, to_back = self.parts[2 * self.distance - 1], self.parts[2 * self.distance]
            if ahead.shape != to_ahead.shape:
                cut = ahead.shape[0]
                ahead = jnp.concatenate([add_low(ahead, to_ahead[:cut]), to_ahead[cut:]])
                back = jnp.concatenate([to_back[:cut], add_low(back, to_back[cut:])])
            else:
                ahead = add_low(ahead, to_ahead)
                back = to_back if back is None else add_low(back, to_back)
        self.ahead, self.back = ahead, back
        return ahead, back

    def terms(self):
        return self.parts[0], self.ahead, self.back


def sum_low(terms):
    return sum(term.astype(F32) for term in terms).astype(BF16)


def to_diag(x, chips):
    pairs = [(2 * i + b, 2 * (i ^ 1) + 1 - b) for i in range(2 * chips) for b in range(2)]
    return lax.ppermute(x, ("seq", "batch"), pairs)


PLAN = {
    "tables": (0, 1),
    "x_far": (0, 3),
    "pairs": (2, 4),
    "heads_far": (7, 9),
    "heads": (9, 11),
    "heads_mate": (9, 11),
    "out_grad_far": (8, 10),
    "out_grad": (9, 11),
    "ff_hop0": (4, 6),
    "ff_hop1": (11, 99),
    "ff_hop2": (12, 99),
    "ff_hop3": (13, 15),
    "six": (9, 10),
    "six_mate": (9, 8),
    "w_far0": (11, 13),
    "w_four0": (12, 13),
    "w_far1": (12, 99),
    "w_four1": (13, 15),
    "w_far2": (20, 99),
    "w_four2": (20, 99),
    "ff_parts": (19, 20),
    "ff_sum0": (19, 21),
    "ff_sum1": (21, 24),
    "ff_sum2": (27, 99),
    "ff_sum3": (27, 99),
    "small0": (20, 21),
    "small1": (30, 99),
    "small2": (30, 99),
    "small3": (32, 99),
    "small4": (33, 34),
    "att": (22, 23),
    "qkv_sum": (25, 23),
    "mixed_far": (22, 24),
    "mixed": (22, 24),
    "branch": (19, 21),
    "qkv_far": (27, 30),
    "inputs": (28, 31),
    "ff_total": (29, 31),
    "ff_far": (29, 34),
    "early": (29, 99),
}
ROOM = {'pick': {}, 'attend': {'room': 50}, 'residual': {}, 'back': {'room': 60}, 'attend_back': {}, 'ff': {'room': 60}, 'ff_weight': {'room': 60}, 'in_weight': {'room': 60}}


class Flow:
    def __init__(self, plan):
        self.plan = plan
        self.step, self.arrays = -1, ()
        self.ready, self.results = {}, {}

    def add(self, name, action):
        self.ready[name] = action
        if self.plan[name][0] <= self.step:
            self.run(name)

    def run(self, name):
        arrays = self.arrays if self.plan[name][0] == self.step else ()
        self.results[name] = self.ready.pop(name)(lambda x: after(x, *arrays))

    def get(self, name):
        if name in self.ready:
            self.run(name)
        return self.results[name]

    def cross(self, step, *arrays):
        self.step, self.arrays = step, arrays
        for name in [n for n in self.ready if self.plan[n][0] <= step]:
            self.run(name)
        waits = [self.get(n) for n, place in self.plan.items() if place[1] == step and (n in self.ready or n in self.results)]
        if waits:
            arrays = lax.optimization_barrier((arrays, waits))[0]
        return arrays if len(arrays) > 1 else arrays[0]


def fast_shards(
    frames, skip_frames, time_embed, cotangent, segments, owners, master, moment_one, moment_two,
    norm_gains, ff_biases, small_first, small_second,
):
    row_count, seg_len, width = frames.shape
    width_ff = ff_biases.shape[0] - width
    count = row_count * seg_len
    capacity = master.shape[0]
    seq_count = lax.axis_size("seq")
    chips = seq_count // 2
    half_width = width // 2
    group = lax.axis_index("batch")
    here = lax.axis_index("seq")
    chip, core = here // 2, here % 2
    order = jnp.array(ring_order(chips), jnp.int32)
    position = jnp.argmax(order == chip).astype(jnp.int32)
    rel = jnp.array([0, 1, -1, 2, -2, 3, -3, 4], jnp.int32)
    places = order[(position - rel) % chips]
    targets = order[(position + rel) % chips]
    sources = jnp.stack([2 * places + core, 2 * places + 1 - core], axis=1).reshape(-1)
    flow = Flow(PLAN)
    add, get, cross = flow.add, flow.get, flow.cross

    def by_core(own, mate):
        return jnp.where(core == 0, jnp.stack([own, mate]), jnp.stack([mate, own]))

    def pick(x, which):
        return lax.dynamic_index_in_dim(x, which, 0, False)

    def gather_four(parts):
        return [parts[0], to_far(parts[1]), to_mate(parts[2], chips), to_diag(parts[3], chips)]

    def same_four(x, far):
        return [x, far, to_mate(x, chips), to_mate(far, chips)]

    ids = jnp.arange(owners.shape[0], dtype=jnp.int32)
    slots = jnp.sum(
        ((owners[None, :] == owners[:, None]) & (ids[None, :] < ids[:, None])).astype(jnp.int32), axis=1
    )
    held = owners == group
    turned = jnp.swapaxes(master, 1, 2)
    block = turned.shape[1:]
    place = jnp.stack([group, core])
    stacks = lambda *counts: [((n,) + block, BF16) for n in counts]
    in_keep, in_send, in_give, head_own, pair_own, pair_far, pair_mate, pair_diag = kernel_call(
        pick_kernel, [((1024, block[1]), BF16)] * 2 + [((256, block[1]), BF16)] + stacks(24, 16, 16, 16, 16),
        turned, scalars=(slots, place), far_out=(3, 4, 5, 6, 7), **ROOM["pick"],
    )
    seg_own = jnp.zeros((16, 128), BF16).at[:row_count, :seg_len].set(segments.astype(BF16))
    (in_blocks,) = kernel_call(
        select_in_kernel, [((PIECE_ROWS, block[1]), BF16)],
        in_keep, to_far(in_send), to_mate(in_give, chips), to_diag(in_give, chips), seg_own, to_mate(seg_own, chips),
        scalars=(owners, place),
    )

    half_size = HEAD_DIM // 2
    spot = (sources[:, None] * seg_len + jnp.arange(seg_len, dtype=jnp.int32)[None, :]).reshape(-1).astype(F32)
    inverse = 10000.0 ** (-jnp.arange(half_size, dtype=jnp.int32).astype(F32) / half_size)
    phases = spot[:, None] * inverse[None, :]
    cosine, sine = jnp.cos(phases), jnp.sin(phases)
    cosine = jnp.concatenate([cosine, cosine], axis=1)
    sine = jnp.concatenate([-sine, sine], axis=1)
    add("tables", lambda tie: (cosine, sine))
    x_own = jnp.stack([frames.reshape(count, width), skip_frames.reshape(count, width), time_embed.reshape(count, width)])
    valid = (segments < UTTS).astype(F32).reshape(count, 1)
    grad_branch = (cotangent.reshape(count, width).astype(F32) * valid).astype(BF16)

    add("x_far", lambda tie: to_far(tie(x_own)))

    def exchange_pairs(tie):
        far, mate, diag = tie((pair_far, pair_mate, pair_diag))
        return kernel_call(
            select_pairs_kernel, [((2, 16) + block, BF16)],
            pair_own, to_far(far), to_mate(mate, chips), to_diag(diag, chips), scalars=(owners, place),
        )[0]

    add("pairs", exchange_pairs)
    add("heads_far", lambda tie: to_far(tie(head_own)))
    add("heads", lambda tie: kernel_call(
        select_heads_kernel, stacks(24), head_own, tie(get("heads_far")), scalars=(owners, place),
    )[0])
    add("heads_mate", lambda tie: to_mate(tie(get("heads")), chips))
    add("out_grad_far", lambda tie: to_far(tie(grad_branch)))
    add("out_grad", lambda tie: same_four(grad_branch, tie(get("out_grad_far"))))

    in_ring = RingGather(cross(0, in_blocks), chips, cut=PIECE_CUT)
    in_ring.hop()
    for hop in range(1, 4):
        in_ring.ahead, in_ring.back = cross(hop, in_ring.ahead, in_ring.back)
        in_ring.pieces[2 * hop - 1 : 2 * hop + 1] = [in_ring.ahead, in_ring.back]
        in_ring.hop()
    in_pieces = in_ring.pieces
    in_pieces[7:] = cross(4, *in_pieces[7:])

    ff_ring = RingGather(get("pairs"), chips, halves=False)

    def ff_hop(tie):
        ff_ring.ahead, ff_ring.back = tie((ff_ring.ahead, ff_ring.back))
        return ff_ring.hop()

    for hop in range(4):
        add("ff_hop%d" % hop, ff_hop)

    x_far = get("x_far")
    x_four = [x_own, x_far, to_mate(x_own, chips), to_mate(x_far, chips)]
    quarter_part = ((2, count, width // 4), F32)
    *trunk_parts, seg, w_zero, w_one, w_two = kernel_call(
        trunk_kernel, [quarter_part] * 4 + [((8, seq_count * seg_len), F32)] + [((width // 4, width), BF16)] * 3,
        *x_four, *in_pieces, scalars=(places,), flops=2 * 3 * 4 * count * width * width // 4, far_out=(5, 6, 7),
    )
    for t, w in enumerate((w_zero, w_one, w_two)):
        add("w_far%d" % t, lambda tie, w=w: to_far(tie(w)))
        add("w_four%d" % t, lambda tie, w=w, t=t: same_four(w, tie(get("w_far%d" % t))))
    add("six", lambda tie: kernel_call(
        assemble_out_kernel, [((width, half_width), BF16)], *tie(tuple(in_pieces)), scalars=(places, place),
    )[0])
    add("six_mate", lambda tie: to_mate(tie(get("six")), chips))
    trunk_parts = cross(5, *trunk_parts)
    trunk, gamma, normed = kernel_call(
        norm_kernel, [((count, width), F32), ((count, width), F32), ((count, width), BF16)],
        *cross(6, *gather_four(trunk_parts)), scalars=(place,), far_out=(0, 1),
    )

    normed_ring = RingGather(cross(7, normed), chips)
    normed_ring.hop()
    for hop in range(1, 4):
        normed_ring.ahead, normed_ring.back = cross(7 + hop, normed_ring.ahead, normed_ring.back)
        normed_ring.pieces[2 * hop - 1 : 2 * hop + 1] = [normed_ring.ahead, normed_ring.back]
        normed_ring.hop()
    normed_ring.pieces[7:] = cross(11, *normed_ring.pieces[7:])
    normed_pieces = normed_ring.pieces + [to_mate(piece, chips) for piece in normed_ring.pieces]

    row_len = seq_count * seg_len
    heads_out = ((3, row_count, row_len, HEAD_DIM), BF16)
    cosine, sine = get("tables")
    w_qkv = get("heads")
    qkv, mixed, normed_all = kernel_call(
        attend_kernel, [heads_out, ((seq_count, seg_len, 2 * HEAD_DIM), BF16), ((row_count * row_len, width), BF16)],
        w_qkv, cosine, sine, seg, *normed_pieces, scalars=(sources,), far_out=(0, 2), **ROOM["attend"],
        scratch=[pltpu.VMEM((row_count, row_len, HEAD_DIM), BF16)], flops=2 * 2 * row_len * (192 * width + 2 * row_len * 64),
    )
    heads = cross(13, lax.all_to_all(cross(12, mixed), "seq", 0, 0, tiled=True))
    residual, normed_two, mixed_rows = kernel_call(
        residual_kernel, [((count, width), F32), ((count, width), BF16), ((count, width), BF16)],
        heads, get("six"), get("six_mate"), trunk, norm_gains[None], scalars=(core[None],), flops=2 * count * width * width,
        far_in=(3,), far_out=(0, 2), **ROOM["residual"],
    )
    add("mixed_far", lambda tie: to_far(tie(mixed_rows)))
    add("mixed", lambda tie: same_four(mixed_rows, tie(get("mixed_far"))))

    normed_two = cross(14, normed_two)
    normed_far = to_far(normed_two)
    normed_four = cross(15, normed_two, normed_far, to_mate(normed_two, chips), to_mate(normed_far, chips))
    pair_index = 2 * group + core
    up_bias = lax.dynamic_slice_in_dim(ff_biases, pair_index * width, width, 0)[None]
    frame_part, frame_low, wide_low = ((count, width), F32), ((count, width), BF16), ((4 * count, width), BF16)
    for hop in range(4):
        get("ff_hop%d" % hop)
    grad_four = get("out_grad")
    *ff_outs, hidden, grad_pre, grad_up = kernel_call(
        forward_back_kernel, [frame_part] * 4 + [frame_low] * 4 + [wide_low, wide_low, ((1, width), F32)],
        *normed_four, *grad_four, up_bias, *ff_ring.pieces, scalars=(places,), far_in=tuple(range(17)), far_out=tuple(range(11)),
        lazy=True, **ROOM["ff"], scratch=[pltpu.VMEM((width, width), BF16)] * 2 + [pltpu.VMEM((4 * count, width), F32)],
        flops=4 * 2 * 4 * count * width * width,
    )
    add("branch", lambda tie: gather_four(tie(tuple(ff_outs[4:]))))

    def weight_parts(tie):
        return kernel_call(
            ff_weight_kernel, [((2, 16) + block, BF16)] * 8, *normed_four, *grad_four, *tie((hidden, grad_pre)),
            scalars=(targets,), flops=2 * 2 * 4 * count * width * width, far_in=tuple(range(10)), far_out=tuple(range(8)), **ROOM["ff_weight"],
        )

    add("ff_parts", weight_parts)
    grad_own, grad_far, grad_mate, grad_diag = cross(16, *ff_outs[:4])
    grad_sent = cross(17, (grad_far + to_mate(grad_diag, chips)).astype(BF16))
    grad_parts = cross(18, grad_own, to_mate(grad_mate, chips), to_far(grad_sent))
    quarter = ((count, width // 4), BF16)
    grad_res, grad_heads, grad_gains, *att_parts = kernel_call(
        back_out_kernel,
        [((count, width), F32), ((seq_count, seg_len, 2 * HEAD_DIM), BF16), ((1, width), F32)] + [quarter] * 4,
        *grad_parts, residual, norm_gains[None], grad_branch, get("six"), get("six_mate"), scalars=(place,),
        flops=2 * count * width * width, far_in=(3,), far_out=(0, 3, 4, 5, 6), **ROOM["back"],
    )
    add("att", lambda tie: gather_four(tie(tuple(att_parts))))

    grad_down = jnp.sum(grad_branch.astype(F32), axis=0)
    up_all = lax.dynamic_update_slice_in_dim(jnp.zeros((width_ff,), F32), grad_up[0], pair_index * width, 0)
    small = [jnp.concatenate([grad_gains[0], up_all, grad_down]).reshape(-1, 128)]

    def small_step(tie, bit):
        x = tie(small[-1])
        if bit == 0:
            got = to_far(x)
        else:
            got = lax.ppermute(x, "seq", [(j, j ^ bit) for j in range(seq_count)])
        small.append(x + got)
        return small[-1]

    for n, bit in enumerate((0, 1, 2, 4, 8)):
        add("small%d" % n, lambda tie, bit=bit: small_step(tie, bit))

    grad_heads = cross(19, grad_heads)
    ff_sums = []

    def ff_sum_hop(tie):
        if not ff_sums:
            ff_sums.append(RingSum(get("ff_parts"), chips))
        ring = ff_sums[0]
        if ring.back is None:
            ring.ahead = tie(ring.ahead)
        else:
            ring.ahead, ring.back = tie((ring.ahead, ring.back))
        return ring.hop()

    for hop in range(4):
        add("ff_sum%d" % hop, ff_sum_hop)
    rows_out = ((chips * count, 256), BF16)
    head_grads = cross(20, lax.all_to_all(grad_heads, "seq", 0, 0, tiled=True))
    qkv_grads, mate_grads, grad_qkv = kernel_call(
        attend_back_kernel, [rows_out, rows_out, heads_out], qkv, head_grads, cosine, sine, seg,
        scalars=(sources,), far_in=(0,), far_out=(2,), **ROOM["attend_back"],
        scratch=[pltpu.VMEM((row_count, row_len, HEAD_DIM), BF16)] + [pltpu.VMEM((row_count, row_len, HEAD_DIM), F32)] * 3,
        flops=2 * 2 * row_len * row_len * 64 * 5,
    )
    add("qkv_sum", lambda tie: kernel_call(
        qkv_weight_kernel, [((24,) + block, BF16)], *tie((grad_qkv, normed_all)), flops=2 * 2 * row_len * 192 * width,
        far_in=(0, 1), far_out=(0,),
    )[0])
    add("qkv_far", lambda tie: to_far(tie(get("qkv_sum"))))
    mate_grads = cross(21, mate_grads)
    norm_parts = kernel_call(
        back_qkv_kernel, [((row_count, seg_len, width), BF16)] * 7 + [((1, seg_len, width), BF16)] * 2,
        qkv_grads, to_mate(mate_grads, chips), w_qkv, get("heads_mate"),
        scratch=[pltpu.VMEM((512, width), BF16)], flops=2 * chips * count * 512 * width,
    )
    norm_ring = RingSum(norm_parts, chips)
    norm_ring.ahead, norm_ring.back = cross(22, norm_ring.ahead, norm_ring.back)
    norm_ring.hop()
    for hop in range(1, 4):
        norm_ring.ahead, norm_ring.back = cross(22 + hop, norm_ring.ahead, norm_ring.back)
        norm_ring.hop()
    trunk_parts = kernel_call(
        back_norm_kernel, [((2 * count, width // 4), BF16)] * 4,
        *cross(26, *norm_ring.terms()), trunk, gamma, grad_res, scalars=(place,), far_in=(3, 4, 5),
    )
    trunk_four = cross(28, *gather_four(cross(27, *trunk_parts)))

    in_parts = kernel_call(
        input_weight_kernel, [((32, 32, block[1]), BF16)] * 8,
        *x_four, *trunk_four, *get("mixed"), *get("att"), scalars=(targets,), far_in=tuple(range(16)), far_out=tuple(range(8)),
        lazy=True, **ROOM["in_weight"], scratch=[pltpu.VMEM((4, width // 4, width), BF16)], flops=2 * 4 * 4 * count * width * width // 4,
    )
    add("inputs", lambda tie: kernel_call(
        back_input_kernel, [frame_part] * 3, *tie(tuple(trunk_parts)), *[w for t in range(3) for w in get("w_four%d" % t)],
        flops=2 * 3 * count * width * width,
    ))

    def finish_ff(tie):
        for hop in range(4):
            get("ff_sum%d" % hop)
        total = sum_low(tie(ff_sums[0].terms()))
        return by_core(pick(total, core), to_mate(pick(total, 1 - core), chips)).reshape((32,) + block)

    add("ff_total", finish_ff)
    add("ff_far", lambda tie: to_far(tie(get("ff_total"))))
    in_sums = RingSum(in_parts, chips)
    in_sums.ahead, in_sums.back = cross(29, in_sums.ahead, in_sums.back)
    in_sums.hop()
    for hop in range(1, 4):
        in_sums.ahead, in_sums.back = cross(29 + hop, in_sums.ahead, in_sums.back)
        in_sums.hop()

    held_count = jnp.sum(held.astype(jnp.int32))
    match = held[None, :] & (slots[None, :] == jnp.arange(capacity, dtype=jnp.int32)[:, None])
    tile, row = ids // 8 - 7, ids % 8
    pair = tile % 4
    ff_place = 56 + 32 * (pair // 2 != group).astype(jnp.int32) + 16 * (pair % 2) + 8 * (tile // 4) + row
    source = jnp.sum(jnp.where(match, jnp.where(ids < 56, ids, ff_place)[None, :], 0), axis=1)
    stack = (capacity,) + block
    states = (turned, jnp.swapaxes(moment_one, 1, 2), jnp.swapaxes(moment_two, 1, 2))
    first_slots = 60
    per_step = math.gcd(math.gcd(first_slots, capacity - first_slots), 15)

    def update(grads, start, stop, done):
        state = pl.BlockSpec((per_step,) + block, lambda i, *_: (i + start // per_step, 0, 0))
        whole = [pl.BlockSpec(g.shape, lambda i, *_, n=g.ndim: (0,) * n) for g in grads]
        return pl.pallas_call(
            functools.partial(adam_kernel, start=start, early=not done),
            grid_spec=pltpu.PrefetchScalarGridSpec(
                num_scalar_prefetch=3, grid=((stop - start) // per_step,),
                in_specs=whole + [state] * 3 + [pl.BlockSpec(memory_space=pl.ANY)] * len(done), out_specs=[state] * 4,
            ),
            out_shape=[jax.ShapeDtypeStruct(stack, F32)] * 3 + [jax.ShapeDtypeStruct(stack, BF16)],
            input_output_aliases={9 + i: i for i in range(len(done))},
            compiler_params=pltpu.CompilerParams(vmem_limit_bytes=32 * MIB),
            cost_estimate=pl.CostEstimate(flops=0, bytes_accessed=(stop - start) * 8192 * 26, transcendentals=0),
        )(source, held_count[None], group[None], *grads, *states, *done)

    def early_update(tie):
        qkv_own, ff_total = tie((get("qkv_sum"), get("ff_total")))
        rest = jnp.concatenate([add_low(qkv_own, get("qkv_far")), ff_total, get("ff_far")])
        tiny = jnp.zeros((1, 32, block[1]), BF16)
        return rest, tuple(update((tiny, tiny, rest), first_slots, capacity, ()))

    add("early", early_update)
    in_sum = cross(33, sum_low(in_sums.terms()))
    in_far = cross(34, to_far(in_sum))
    rest_grads, done = get("early")
    new_first, new_second, new_master, new_low = update((in_sum, in_far, rest_grads), 0, first_slots, done)
    back = lambda a: jnp.swapaxes(a, 1, 2)

    for n in range(5):
        get("small%d" % n)
    small_values = jnp.concatenate([norm_gains, ff_biases])
    small_new, small_one, small_two = adam(small_values, small[-1].reshape(-1), small_first, small_second, SMALL_RATE)

    branch = sum(part.astype(F32) for part in get("branch"))
    output = (residual + branch + ff_biases[None, width_ff:]) * valid
    output = output.astype(BF16).reshape(row_count, seg_len, width)
    inputs = [part.reshape(row_count, seg_len, width) for part in get("inputs")]
    return (
        output, inputs[0], inputs[1], inputs[2],
        back(new_first), back(new_second), back(new_master), back(new_low),
        small_one, small_two, small_new,
    )


def slot_places(owners, group_count, capacity):
    one_hot = (owners[:, None] == jnp.arange(group_count, dtype=jnp.int32)[None, :]).astype(
        jnp.int32
    )
    before = jnp.cumsum(one_hot, axis=0) - one_hot
    slot_index = jnp.sum(before * one_hot, axis=1)
    return owners * capacity + slot_index


def rotate(tensor, offset):
    half_size = tensor.shape[-1] // 2
    position = (offset + jnp.arange(tensor.shape[1], dtype=jnp.int32)).astype(jnp.float32)
    inverse = 10000.0 ** (-jnp.arange(half_size, dtype=jnp.int32).astype(jnp.float32) / half_size)
    phases = position[:, None] * inverse[None, :]
    cosine = jnp.cos(phases)[None, :, None, :]
    sine_part = jnp.sin(phases)[None, :, None, :]
    front_half = tensor[..., :half_size]
    back_half = tensor[..., half_size:]
    return jnp.concatenate(
        [front_half * cosine - back_half * sine_part, front_half * sine_part + back_half * cosine],
        axis=-1,
    )


def adaptive_norm(trunk, gamma_map):
    return (
        trunk
        * lax.rsqrt(jnp.mean(trunk * trunk, axis=-1, keepdims=True) + NORM_EPS)
        * (1.0 + gamma_map)
    )


def root_norm(residual, norm_gains):
    return (
        residual
        * lax.rsqrt(jnp.mean(residual * residual, axis=-1, keepdims=True) + NORM_EPS)
        * norm_gains
    )


def gelu_exact(tensor):
    return jax.nn.gelu(tensor, approximate=False)


def adam_update(weight, gradient, first_moment, second_moment, step_rate):
    first_moment = BETA_ONE * first_moment + (1.0 - BETA_ONE) * gradient
    second_moment = BETA_TWO * second_moment + (1.0 - BETA_TWO) * gradient * gradient
    fix_one = 1.0 - BETA_ONE**STEP
    fix_two = 1.0 - BETA_TWO**STEP
    update = first_moment / fix_one / (jnp.sqrt(second_moment / fix_two) + ADAM_EPS)
    return (weight - step_rate * (update + WEIGHT_DECAY * weight), first_moment, second_moment)


def matmul(former, latter):
    return jnp.dot(former, latter, preferred_element_type=jnp.float32)


def contract_rows(former, latter):
    return lax.dot_general(
        former, latter, (((0,), (0,)), ((), ())), preferred_element_type=jnp.float32
    )


def contract_cols(former, latter):
    return lax.dot_general(
        former, latter, (((1,), (1,)), ((), ())), preferred_element_type=jnp.float32
    )


def score_block(queries, key_rows, same_utt):
    scores = jnp.einsum(
        "qhd,khd->hqk", queries, key_rows, preferred_element_type=jnp.float32
    ) * HEAD_DIM ** (-0.5)
    scores = jnp.where(same_utt[None], scores, MASKED_SCORE)
    row_max = jnp.max(scores, axis=-1, keepdims=True)
    exponent = jnp.exp(scores - row_max)
    total = jnp.sum(exponent, axis=-1, keepdims=True)
    return (exponent / total, row_max[..., 0], total[..., 0])


def attend(element):
    queries, key_rows, values, same_utt = element
    attn_probs, row_max, total = score_block(queries, key_rows, same_utt)
    mixed = jnp.einsum(
        "hqk,khd->qhd", attn_probs.astype(jnp.bfloat16), values, preferred_element_type=jnp.float32
    )
    return (mixed.astype(jnp.bfloat16), attn_probs, row_max, total)


def probs_only(element):
    return score_block(element[0], element[1], element[2])


def attend_query(element):
    queries, key_rows, values, attn_probs, grad_mixed = element
    prob_grad = jnp.einsum("qhd,khd->hqk", grad_mixed, values, preferred_element_type=jnp.float32)
    inner_sum = jnp.sum(attn_probs * prob_grad, axis=-1, keepdims=True)
    score_grad = (attn_probs * (prob_grad - inner_sum)).astype(jnp.bfloat16)
    query_grad = jnp.einsum(
        "hqk,khd->qhd", score_grad, key_rows, preferred_element_type=jnp.float32
    ) * HEAD_DIM ** (-0.5)
    return (query_grad, inner_sum[..., 0])


def attend_keys(element):
    query_all, grad_all, max_all, total_all, inner_all, seg_query, key_own, value_own, seg_own = (
        element
    )
    scores = jnp.einsum(
        "qhd,khd->hqk", query_all, key_own, preferred_element_type=jnp.float32
    ) * HEAD_DIM ** (-0.5)
    same_utt = seg_query[:, None] == seg_own[None, :]
    scores = jnp.where(same_utt[None], scores, MASKED_SCORE)
    attn_probs = jnp.exp(scores - max_all[..., None]) / total_all[..., None]
    prob_grad = jnp.einsum("qhd,khd->hqk", grad_all, value_own, preferred_element_type=jnp.float32)
    score_grad = (attn_probs * (prob_grad - inner_all[..., None])).astype(jnp.bfloat16)
    key_grad = jnp.einsum(
        "hqk,qhd->khd", score_grad, query_all, preferred_element_type=jnp.float32
    ) * HEAD_DIM ** (-0.5)
    value_grad = jnp.einsum(
        "hqk,qhd->khd",
        attn_probs.astype(jnp.bfloat16),
        grad_all,
        preferred_element_type=jnp.float32,
    )
    return (key_grad, value_grad)


def general_shards(
    frames,
    skip_frames,
    time_embed,
    cotangent,
    segments,
    owners,
    master,
    moment_one,
    moment_two,
    norm_gains,
    ff_biases,
    small_first,
    small_second,
):
    row_count, seg_len, model_width = frames.shape
    width_ff = ff_biases.shape[0] - model_width
    frame_count = row_count * seg_len
    group_count = lax.axis_size("batch")
    capacity = master.shape[0]
    block_rows = master.shape[1]
    scale_in = model_width ** (-0.5)
    scale_time = 0.5 * model_width ** (-0.5)
    scale_out = 4.0 * model_width ** (-0.5)
    scale_ff = width_ff ** (-0.5)
    places = slot_places(owners, group_count, capacity)
    low_master = master.astype(jnp.bfloat16)
    all_slots = lax.all_gather(low_master, "batch", axis=0, tiled=True)
    columns = jnp.take(all_slots, places, axis=0)
    tile_stack = lax.all_gather(columns, "seq", axis=2, tiled=True).reshape(15, model_width, model_width)
    up_weight = jnp.concatenate(
        [tile_stack[7], tile_stack[8], tile_stack[9], tile_stack[10]], axis=1
    )
    down_weight = tile_stack[11:15].reshape(width_ff, model_width)
    flat_frames = frames.reshape(frame_count, model_width)
    flat_skip = skip_frames.reshape(frame_count, model_width)
    flat_time = time_embed.reshape(frame_count, model_width)
    offset = lax.axis_index("seq") * seg_len

    def rotate_here(tensor):
        return rotate(tensor, offset)

    def split_heads(tensor):
        return tensor.reshape(row_count, seg_len, HEADS, HEAD_DIM)

    trunk = (matmul(flat_frames, tile_stack[0]) + matmul(flat_skip, tile_stack[1])) * scale_in
    gamma_map = matmul(flat_time, tile_stack[2]) * scale_time
    normed_f32, norm_pull = jax.vjp(adaptive_norm, trunk, gamma_map)
    normed = normed_f32.astype(jnp.bfloat16)
    query_rot, query_pull = jax.vjp(
        rotate_here, split_heads(matmul(normed, tile_stack[3]) * scale_in)
    )
    key_rot, key_pull = jax.vjp(rotate_here, split_heads(matmul(normed, tile_stack[4]) * scale_in))
    queries = query_rot.astype(jnp.bfloat16)
    key_local = key_rot.astype(jnp.bfloat16).reshape(row_count, seg_len, model_width)
    value_local = (
        (matmul(normed, tile_stack[5]) * scale_in)
        .astype(jnp.bfloat16)
        .reshape(row_count, seg_len, model_width)
    )
    seg_low = segments.astype(jnp.bfloat16)
    key_all, value_all, seg_all = (
        lax.all_gather(key_local, "seq", axis=1, tiled=True),
        lax.all_gather(value_local, "seq", axis=1, tiled=True),
        lax.all_gather(seg_low, "seq", axis=1, tiled=True),
    )
    key_total = key_all.shape[1]
    key_heads = key_all.reshape(row_count, key_total, HEADS, HEAD_DIM)
    value_heads = value_all.reshape(row_count, key_total, HEADS, HEAD_DIM)
    same_utt = seg_low[:, :, None] == seg_all[:, None, :]
    mixed_heads, probs_kept, max_kept, total_kept = lax.map(
        attend, (queries, key_heads, value_heads, same_utt)
    )
    mixed_rows = mixed_heads.reshape(frame_count, model_width)
    residual = trunk + matmul(mixed_rows, tile_stack[6]) * scale_out
    normed_two_f32, root_pull = jax.vjp(root_norm, residual, norm_gains)
    normed_two = normed_two_f32.astype(jnp.bfloat16)
    pre_act = matmul(normed_two, up_weight) * scale_in + ff_biases[:width_ff]
    activation, gelu_pull = jax.vjp(gelu_exact, pre_act)
    hidden = activation.astype(jnp.bfloat16)
    branch = matmul(hidden, down_weight) * scale_ff + ff_biases[width_ff:]
    valid_row = (segments < UTTS).astype(jnp.float32).reshape(frame_count, 1)
    output = (
        ((residual + branch) * valid_row)
        .astype(jnp.bfloat16)
        .reshape(row_count, seg_len, model_width)
    )
    grad_out = cotangent.reshape(frame_count, model_width).astype(jnp.float32) * valid_row
    grad_branch = grad_out.astype(jnp.bfloat16)
    grad_down_bias = jnp.sum(grad_branch.astype(jnp.float32), axis=0)
    down_grads = contract_rows(hidden, grad_branch) * scale_ff
    grad_hidden = contract_cols(grad_branch, down_weight) * scale_ff
    grad_pre = gelu_pull(grad_hidden)[0].astype(jnp.bfloat16)
    grad_up_bias = jnp.sum(grad_pre.astype(jnp.float32), axis=0)
    up_grads = contract_rows(normed_two, grad_pre) * scale_in
    grad_normed_two = contract_cols(grad_pre, up_weight) * scale_in
    grad_residual_norm, grad_gains = root_pull(grad_normed_two)
    grad_residual = grad_out + grad_residual_norm
    grad_attention = grad_residual.astype(jnp.bfloat16)
    out_grads = contract_rows(mixed_rows, grad_attention) * scale_out
    grad_mixed = (contract_cols(grad_attention, tile_stack[6]) * scale_out).astype(jnp.bfloat16)
    grad_mixed = grad_mixed.reshape(row_count, seg_len, HEADS, HEAD_DIM)
    key_again, value_again, seg_again = (
        lax.all_gather(key_local, "seq", axis=1, tiled=True),
        lax.all_gather(value_local, "seq", axis=1, tiled=True),
        lax.all_gather(seg_low, "seq", axis=1, tiled=True),
    )
    back_keys = key_again.reshape(row_count, key_total, HEADS, HEAD_DIM)
    back_values = value_again.reshape(row_count, key_total, HEADS, HEAD_DIM)
    same_again = seg_low[:, :, None] == seg_again[:, None, :]
    back_probs, back_max, back_total = lax.map(probs_only, (queries, back_keys, same_again))
    query_raw, inner_sum = lax.map(
        attend_query, (queries, back_keys, back_values, back_probs, grad_mixed)
    )
    query_all, grad_all = (
        lax.all_gather(queries, "seq", axis=1, tiled=True),
        lax.all_gather(grad_mixed, "seq", axis=1, tiled=True),
    )
    max_all, total_all, inner_all = (
        lax.all_gather(back_max, "seq", axis=2, tiled=True),
        lax.all_gather(back_total, "seq", axis=2, tiled=True),
        lax.all_gather(inner_sum, "seq", axis=2, tiled=True),
    )
    key_own = key_local.reshape(row_count, seg_len, HEADS, HEAD_DIM)
    value_own = value_local.reshape(row_count, seg_len, HEADS, HEAD_DIM)
    key_sum, value_sum = lax.map(
        attend_keys,
        (
            query_all,
            grad_all,
            max_all,
            total_all,
            inner_all,
            seg_again,
            key_own,
            value_own,
            seg_low,
        ),
    )
    grad_q = query_pull(query_raw)[0].reshape(frame_count, model_width).astype(jnp.bfloat16)
    grad_k = key_pull(key_sum)[0].reshape(frame_count, model_width).astype(jnp.bfloat16)
    grad_v = value_sum.reshape(frame_count, model_width).astype(jnp.bfloat16)
    query_grads = contract_rows(normed, grad_q) * scale_in
    key_grads = contract_rows(normed, grad_k) * scale_in
    value_grads = contract_rows(normed, grad_v) * scale_in
    grad_normed = (
        contract_cols(grad_q, tile_stack[3])
        + contract_cols(grad_k, tile_stack[4])
        + contract_cols(grad_v, tile_stack[5])
    ) * scale_in
    grad_trunk_norm, grad_gamma_f32 = norm_pull(grad_normed)
    grad_trunk = (grad_residual + grad_trunk_norm).astype(jnp.bfloat16)
    grad_gamma = grad_gamma_f32.astype(jnp.bfloat16)
    frame_grads = contract_rows(flat_frames, grad_trunk) * scale_in
    skip_grads = contract_rows(flat_skip, grad_trunk) * scale_in
    time_grads = contract_rows(flat_time, grad_gamma) * scale_time
    grad_frames = (contract_cols(grad_trunk, tile_stack[0]) * scale_in).reshape(
        row_count, seg_len, model_width
    )
    grad_skip = (contract_cols(grad_trunk, tile_stack[1]) * scale_in).reshape(
        row_count, seg_len, model_width
    )
    grad_time = (contract_cols(grad_gamma, tile_stack[2]) * scale_time).reshape(
        row_count, seg_len, model_width
    )
    first_tiles = jnp.stack(
        [frame_grads, skip_grads, time_grads, query_grads, key_grads, value_grads, out_grads]
    )
    up_tiles = up_grads.reshape(model_width, 4, model_width).transpose(1, 0, 2)
    down_tiles = down_grads.reshape(4, model_width, model_width)
    blocks = jnp.concatenate([first_tiles, up_tiles, down_tiles], axis=0).reshape(
        -1, block_rows, model_width
    )
    block_count = blocks.shape[0]
    partial_cols = lax.psum_scatter(
        blocks.astype(jnp.bfloat16), "seq", scatter_dimension=2, tiled=True
    )
    matches = places[None, :] == jnp.arange(group_count * capacity, dtype=jnp.int32)[:, None]
    source = jnp.sum(
        jnp.where(matches, jnp.arange(block_count, dtype=jnp.int32)[None, :], 0), axis=1
    )
    filled = jnp.any(matches, axis=1)
    placed = jnp.where(filled[:, None, None], jnp.take(partial_cols, source, axis=0), 0)
    reduced = lax.psum_scatter(placed, "batch", scatter_dimension=0, tiled=True).astype(
        jnp.float32
    )
    small_grad = jnp.concatenate([grad_gains, grad_up_bias, grad_down_bias])
    small_grad = lax.psum(small_grad, ("seq", "batch"))
    owner_index = lax.axis_index("batch")
    held_count = jnp.sum((owners == owner_index).astype(jnp.int32))
    live_slot = (jnp.arange(capacity, dtype=jnp.int32) < held_count).astype(jnp.float32)[
        :, None, None
    ]
    new_master, new_first, new_second = adam_update(
        master, reduced, moment_one, moment_two, LEARN_RATE
    )
    new_master = new_master * live_slot
    new_first = new_first * live_slot
    new_second = new_second * live_slot
    small_values = jnp.concatenate([norm_gains, ff_biases])
    small_new, small_first_new, small_second_new = adam_update(
        small_values, small_grad, small_first, small_second, SMALL_RATE
    )
    return (
        output,
        grad_frames,
        grad_skip,
        grad_time,
        new_first,
        new_second,
        new_master,
        new_master.astype(jnp.bfloat16),
        small_first_new,
        small_second_new,
        small_new,
    )


def solution(mesh):
    fast = mesh.shape["seq"] == HEADS and mesh.shape["batch"] == 2
    rows, slots, whole = P("batch", "seq", None), P("batch", None, "seq"), P()
    return jax.shard_map(
        fast_shards if fast else general_shards,
        mesh=mesh,
        in_specs=(rows, rows, rows, rows, P("batch", "seq"), whole, slots, slots, slots, whole, whole, whole, whole),
        out_specs=(rows, rows, rows, rows, slots, slots, slots, slots, whole, whole, whole),
        check_vma=False,
    )
```
